32 devices in a mesh: wide: 8 (over y, x, core), narrow: 4 (over z).
Axes of the slice: x: 2, y: 2, z: 4, core: 2. Of those that a mesh axis runs over, the one named last changes fastest.
Arguments:
- x_in: bfloat16 [4096, 2560], P('wide', 'narrow'), may hold values from -6 to 6
- grad_out: bfloat16 [4096, 2560], P('wide', 'narrow'), may hold values from -6 to 6
- w_qa: bfloat16 [2560, 768], P('wide', 'narrow'), may hold values from -0.125 to 0.125
- w_kv: bfloat16 [2560, 256], P('wide', 'narrow'), may hold values from -0.125 to 0.125
- w_kr: bfloat16 [2560, 32], P('wide'), may hold values from -0.125 to 0.125
- w_qb: bfloat16 [768, 3840], P('wide', 'narrow'), may hold values from -0.21875 to 0.21875
- w_kvb: bfloat16 [256, 5120], P('wide', 'narrow'), may hold values from -0.375 to 0.375
- w_o: bfloat16 [2560, 2560], P('wide', 'narrow'), may hold values from -6 to 6
- w_gate: bfloat16 [2560, 6400], P('wide', 'narrow'), may hold values from -0.125 to 0.125
- w_up: bfloat16 [2560, 6400], P('wide', 'narrow'), may hold values from -0.125 to 0.125
- w_down: bfloat16 [2560, 6400], P('wide', 'narrow'), may hold values from -0.75 to 0.75
- norm_gains: float32 [2, 2560], P(None, 'narrow'), may hold values from 0.5 to 1.5
- q_gain: float32 [768], P('narrow'), may hold values from 0.5 to 1.5
- kv_gain: float32 [256], P('narrow'), may hold values from 0.5 to 1.5
- deal: int32 [8, 8], replicated, may hold values from 0 to 7, each once within a row
- lengths: int32 [8, 4], P('wide'), may hold values from 1 to 384, 512 in all within a row
- step_count: int32 [1], replicated, may hold values from 1 to 20
- owner_a: int32 [4, 89], P('narrow'), may hold values from 0 to 135, as said below
- owner_b: int32 [4, 15], P('narrow'), may hold values from 0 to 23, as said below
- owner_c: int32 [4, 20], P('narrow'), may hold values from 0 to 31, as said below
- basis_la: float32 [136, 2560, 512], P('wide', None, 'narrow'), as said below
- basis_ra: float32 [136, 64, 256], P('wide', None, 'narrow'), as said below
- basis_lb: float32 [24, 768, 512], P('wide', None, 'narrow'), as said below
- basis_rb: float32 [24, 64, 256], P('wide', None, 'narrow'), as said below
- basis_lc: float32 [32, 256, 512], P('wide', None, 'narrow'), as said below
- basis_rc: float32 [32, 64, 256], P('wide', None, 'narrow'), as said below
- mom_a: float32 [136, 2560, 256], P('wide', None, 'narrow')
- sq_a: float32 [136, 2560, 256], P('wide', None, 'narrow'), as said below
- mom_b: float32 [24, 768, 256], P('wide', None, 'narrow')
- sq_b: float32 [24, 768, 256], P('wide', None, 'narrow'), as said below
- mom_c: float32 [32, 256, 256], P('wide', None, 'narrow')
- sq_c: float32 [32, 256, 256], P('wide', None, 'narrow'), as said below
- kr_mom: float32 [2560, 32], P('wide')
- kr_sq: float32 [2560, 32], P('wide'), as said below
- gain_mom: float32 [2, 2560], P(None, 'narrow')
- gain_sq: float32 [2, 2560], P(None, 'narrow'), as said below
- qgain_mom: float32 [768], P('narrow')
- qgain_sq: float32 [768], P('narrow'), as said below
- kvgain_mom: float32 [256], P('narrow')
- kvgain_sq: float32 [256], P('narrow'), as said below
Outputs:
- layer_out: float32 [4096, 2560], P('wide', 'narrow')
- grad_in: float32 [4096, 2560], P('wide', 'narrow')
- grad_qa: float32 [2560, 768], P('wide', 'narrow')
- grad_kv: float32 [2560, 256], P('wide', 'narrow')
- grad_qb: float32 [768, 3840], P('wide', 'narrow')
- grad_kvb: float32 [256, 5120], P('wide', 'narrow')
- grad_o: float32 [2560, 2560], P('wide', 'narrow')
- grad_gate: float32 [2560, 6400], P('wide', 'narrow')
- grad_up: float32 [2560, 6400], P('wide', 'narrow')
- grad_down: float32 [2560, 6400], P('wide', 'narrow')
- new_qa: float32 [2560, 768], P('wide', 'narrow')
- new_kv: float32 [2560, 256], P('wide', 'narrow')
- new_qb: float32 [768, 3840], P('wide', 'narrow')
- new_kvb: float32 [256, 5120], P('wide', 'narrow')
- new_o: float32 [2560, 2560], P('wide', 'narrow')
- new_gate: float32 [2560, 6400], P('wide', 'narrow')
- new_up: float32 [2560, 6400], P('wide', 'narrow')
- new_down: float32 [2560, 6400], P('wide', 'narrow')
- grad_kr: float32 [2560, 32], P('wide')
- new_kr: float32 [2560, 32], P('wide')
- new_kr_mom: float32 [2560, 32], P('wide')
- new_kr_sq: float32 [2560, 32], P('wide')
- grad_gains: float32 [2, 2560], P(None, 'narrow')
- new_gains: float32 [2, 2560], P(None, 'narrow')
- new_gain_mom: float32 [2, 2560], P(None, 'narrow')
- new_gain_sq: float32 [2, 2560], P(None, 'narrow')
- grad_qgain: float32 [768], P('narrow')
- new_qgain: float32 [768], P('narrow')
- new_qgain_mom: float32 [768], P('narrow')
- new_qgain_sq: float32 [768], P('narrow')
- grad_kvgain: float32 [256], P('narrow')
- new_kvgain: float32 [256], P('narrow')
- new_kvgain_mom: float32 [256], P('narrow')
- new_kvgain_sq: float32 [256], P('narrow')
- new_mom_a: float32 [136, 2560, 256], P('wide', None, 'narrow')
- new_sq_a: float32 [136, 2560, 256], P('wide', None, 'narrow')
- new_mom_b: float32 [24, 768, 256], P('wide', None, 'narrow')
- new_sq_b: float32 [24, 768, 256], P('wide', None, 'narrow')
- new_mom_c: float32 [32, 256, 256], P('wide', None, 'narrow')
- new_sq_c: float32 [32, 256, 256], P('wide', None, 'narrow')
The draws below stay inside these ranges and needn't reach their ends.
Inputs may be any that keep to these rules, and one draw needn't show every extreme that they name: Each row of deal is a permutation. `lengths`: each row sums to 512; its largest entry is 384; the last entry counts padding rows. `owner_a`: entries of a row are distinct; slot k belongs to owner k // 17 of wide; in every row some owner holds exactly 17 units. `owner_b`: entries of a row are distinct; slot k belongs to owner k // 3 of wide; in every row some owner holds exactly 3 units. `owner_c`: entries of a row are distinct; slot k belongs to owner k // 4 of wide; in every row some owner holds exactly 4 units. `basis_la`: every block of 128 by 128 is orthogonal. `basis_ra`: every block of 64 by 64 is orthogonal. `basis_lb`: every block of 128 by 128 is orthogonal. `basis_rb`: every block of 64 by 64 is orthogonal. `basis_lc`: every block of 128 by 128 is orthogonal. `basis_rc`: every block of 64 by 64 is orthogonal. `sq_a`: Positive. `sq_b`: Positive. `sq_c`: Positive. `kr_sq`: Positive. `gain_sq`: Positive. `qgain_sq`: Positive. `kvgain_sq`: Positive.
All inputs are finite; a program needn't handle non-finite values.
Results may differ from the reference program's by a relative error of at most 0.015.
Values may be sent and summed in bfloat16 or wider, within the bound.
No kernel may reach another device: no remote copies, remote signals or barrier semaphores. Data moves between devices by JAX's collectives and lax.ppermute only.
A program may use at most 200 MiB of HBM per device.

```python
import math
import jax
import jax.numpy as jnp
import numpy as np
from jax import lax

D = 2560
HEADS = 40
NOPE = 64
ROPE = 32
VH = 64
QR = 768
KVR = 256
FF = 6400
TOK_DEV = 512
SEQS = 4
SLAB = 64
BASIS = 128
TOKENS = 4096
PIECE = 64
UA = 89
UB = 15
UC = 20
CAPA = 17
CAPB = 3
CAPC = 4
N_WIDE = 8
N_NARROW = 4


def owner_slots(key, unit_count, capacity):

    def per_column(column_key):
        full_key, spread_key, order_key = jax.random.split(column_key, 3)
        full_owner = jax.random.randint(full_key, (), 0, N_WIDE).astype(jnp.int32)
        others = jax.random.permutation(spread_key, (N_WIDE - 1) * capacity)[:unit_count - capacity].astype(jnp.int32)
        owner_ids = others // capacity
        owner_ids = owner_ids + (owner_ids >= full_owner).astype(jnp.int32)
        picked = owner_ids * capacity + others % capacity
        chosen = jnp.concatenate([full_owner * capacity + jnp.arange(capacity, dtype=jnp.int32), picked])
        return jax.random.permutation(order_key, chosen)
    column_keys = jax.random.split(key, N_NARROW)
    return jax.vmap(per_column)(column_keys).astype(jnp.int32)


def draw_owner_a(key, part):
    return owner_slots(jax.random.fold_in(key, 11), UA, CAPA)


def draw_owner_b(key, part):
    return owner_slots(jax.random.fold_in(key, 12), UB, CAPB)


def draw_owner_c(key, part):
    return owner_slots(jax.random.fold_in(key, 13), UC, CAPC)


def orthogonal_blocks(key, count, order):
    sign_key, angle_key = jax.random.split(key)
    index_row = jnp.arange(order, dtype=jnp.int32)
    shared_bits = index_row[:, None] & index_row[None, :]
    parity = jnp.zeros((order, order), jnp.int32)
    for level in range(int(math.log2(order))):
        parity = parity + shared_bits // 2 ** level % 2
    hadamard = (1 - 2 * (parity % 2)).astype(jnp.float32)
    angles = jax.random.uniform(angle_key, (count, 1, order // 2), jnp.float32, -math.pi, math.pi)
    cosine_table = jnp.cos(angles)
    sine_table = jnp.sin(angles)
    even_cols = hadamard[:, 0::2][None]
    odd_cols = hadamard[:, 1::2][None]
    first_cols = even_cols * cosine_table - odd_cols * sine_table
    second_cols = even_cols * sine_table + odd_cols * cosine_table
    mixed = jnp.stack([first_cols, second_cols], axis=-1).reshape(count, order, order)
    signs = (1 - 2 * jax.random.randint(sign_key, (count, order, 1), 0, 2)).astype(jnp.float32)
    return mixed * signs / math.sqrt(order)


def left_bases(key, slots, row_count):
    blocks = orthogonal_blocks(key, slots * (row_count // BASIS) * N_NARROW, BASIS)
    blocks = blocks.reshape(slots, row_count // BASIS, N_NARROW, BASIS, BASIS).transpose(0, 1, 3, 2, 4)
    return blocks.reshape(slots, row_count, N_NARROW * BASIS)


def right_bases(key, slots):
    blocks = orthogonal_blocks(key, slots * N_NARROW, SLAB)
    blocks = blocks.reshape(slots, N_NARROW, SLAB, SLAB).transpose(0, 2, 1, 3)
    return blocks.reshape(slots, SLAB, N_NARROW * SLAB)


def draw_basis_la(key, part):
    return left_bases(jax.random.fold_in(key, 21), N_WIDE * CAPA, D)


def draw_basis_ra(key, part):
    return right_bases(jax.random.fold_in(key, 22), N_WIDE * CAPA)


def draw_basis_lb(key, part):
    return left_bases(jax.random.fold_in(key, 23), N_WIDE * CAPB, QR)


def draw_basis_rb(key, part):
    return right_bases(jax.random.fold_in(key, 24), N_WIDE * CAPB)


def draw_basis_lc(key, part):
    return left_bases(jax.random.fold_in(key, 25), N_WIDE * CAPC, KVR)


def draw_basis_rc(key, part):
    return right_bases(jax.random.fold_in(key, 26), N_WIDE * CAPC)


def grad_scales():
    token_root = (0.85 * TOKENS) ** 0.5
    keys_seen = max(TOK_DEV // 5, 4)
    heads_grad = 0.3 * D ** 0.5
    query_side = heads_grad * VH ** 0.5 / (keys_seen * (NOPE + ROPE)) ** 0.5
    active_grad = 0.178 * D ** 0.5 / 8.0
    q_side = query_side * (HEADS * (NOPE + ROPE) / QR) ** 0.5
    kv_side = query_side * (HEADS * (NOPE + VH) / KVR) ** 0.5
    table = {'qa': q_side, 'kv': kv_side, 'o': 0.3 / keys_seen ** 0.5, 'gate': 0.5 * active_grad, 'up': 0.6 * active_grad, 'down': 0.107, 'qb': query_side, 'kvb': query_side, 'kr': query_side * HEADS ** 0.5, 'first': 2.0 * query_side, 'second': 1.4, 'qgain': q_side, 'kvgain': kv_side}
    return {entry: amount * token_root for entry, amount in table.items()}


def unit_scales(entries, col_widths):
    scales = grad_scales()
    return jnp.concatenate([jnp.full((col_width // (N_NARROW * SLAB),), scales[entry], jnp.float32) for entry, col_width in zip(entries, col_widths)])


def slot_scales(owner_key, unit_count, capacity, per_unit, row_count):
    owners = owner_slots(owner_key, unit_count, capacity)
    fill_value = jnp.mean(per_unit)
    table = jnp.full((N_NARROW, N_WIDE * capacity), 1.0, jnp.float32) * fill_value
    column_ids = jnp.broadcast_to(jnp.arange(N_NARROW, dtype=jnp.int32)[:, None], owners.shape)
    table = table.at[column_ids, owners].set(jnp.broadcast_to(per_unit[None, :], owners.shape))
    spread = jnp.broadcast_to(table.T[:, None, :, None], (N_WIDE * capacity, row_count, N_NARROW, SLAB))
    return spread.reshape(N_WIDE * capacity, row_count, N_NARROW * SLAB)


def scale_a(key):
    per_unit = unit_scales(['qa', 'kv', 'o', 'gate', 'up', 'down'], [QR, KVR, HEADS * VH, FF, FF, FF])
    return slot_scales(jax.random.fold_in(key, 11), UA, CAPA, per_unit, D)


def scale_b(key):
    per_unit = unit_scales(['qb'], [HEADS * (NOPE + ROPE)])
    return slot_scales(jax.random.fold_in(key, 12), UB, CAPB, per_unit, QR)


def scale_c(key):
    per_unit = unit_scales(['kvb'], [HEADS * (NOPE + VH)])
    return slot_scales(jax.random.fold_in(key, 13), UC, CAPC, per_unit, KVR)


def moment_draw(key, scale):
    noise = jnp.clip(jax.random.normal(key, scale.shape, jnp.float32), -6.0, 6.0)
    return 0.1 / 0.9 * scale * noise


def square_draw(key, scale):
    factor = jnp.exp(jax.random.uniform(key, scale.shape, jnp.float32, 0.0, math.log(4.0)))
    return 0.05 / 0.95 * scale * scale * factor


def draw_mom_a(key, part):
    return moment_draw(jax.random.fold_in(key, 41), scale_a(key))


def draw_sq_a(key, part):
    scale = scale_a(key)
    return square_draw(jax.random.fold_in(key, 42), scale)


def draw_mom_b(key, part):
    return moment_draw(jax.random.fold_in(key, 43), scale_b(key))


def draw_sq_b(key, part):
    return square_draw(jax.random.fold_in(key, 44), scale_b(key))


def draw_mom_c(key, part):
    return moment_draw(jax.random.fold_in(key, 45), scale_c(key))


def draw_sq_c(key, part):
    return square_draw(jax.random.fold_in(key, 46), scale_c(key))


def scale_kr():
    return jnp.full((D, ROPE), grad_scales()['kr'], jnp.float32)


def scale_gains():
    scales = grad_scales()
    return jnp.stack([jnp.full((D,), scales['first'], jnp.float32), jnp.full((D,), scales['second'], jnp.float32)])


def draw_kr_mom(key, part):
    return moment_draw(jax.random.fold_in(key, 51), scale_kr())


def draw_kr_sq(key, part):
    return square_draw(jax.random.fold_in(key, 52), scale_kr())


def draw_gain_mom(key, part):
    return moment_draw(jax.random.fold_in(key, 53), scale_gains())


def draw_gain_sq(key, part):
    return square_draw(jax.random.fold_in(key, 54), scale_gains())


def draw_qgain_mom(key, part):
    return moment_draw(jax.random.fold_in(key, 55), jnp.full((QR,), grad_scales()['qgain'], jnp.float32))


def draw_qgain_sq(key, part):
    return square_draw(jax.random.fold_in(key, 56), jnp.full((QR,), grad_scales()['qgain'], jnp.float32))


def draw_kvgain_mom(key, part):
    return moment_draw(jax.random.fold_in(key, 57), jnp.full((KVR,), grad_scales()['kvgain'], jnp.float32))


def draw_kvgain_sq(key, part):
    return square_draw(jax.random.fold_in(key, 58), jnp.full((KVR,), grad_scales()['kvgain'], jnp.float32))


def level_of(rng, shape, shards, smallest, high):
    factor_of, own = 1.0, jax.random.fold_in(rng, 6)
    for axis_at, shards_of in shards:
        steps = jnp.exp(jax.random.uniform(jax.random.fold_in(own, axis_at), (shards_of,), jnp.float32, smallest / len(shards), high / len(shards)))
        factor_of = factor_of * jnp.repeat(steps, shape[axis_at] // shards_of).reshape([-1 if axis == axis_at else 1 for axis in range(len(shape))])
    return factor_of


def profile(count, total, limit, lean):
    loads = [(1 << 20) // math.isqrt(grade ** lean) + 1 for grade in range(2, count + 1)]
    surplus, given = total - limit - (count - 1), [1] * (count - 1)
    while surplus > 0:
        candidates = [i for i in range(count - 1) if given[i] < limit]
        pool, remaining = sum([loads[i] for i in candidates]), surplus
        for i in candidates:
            more = min(limit - given[i], max(1, remaining * loads[i] // pool), surplus)
            given[i] = given[i] + more
            surplus = surplus - more
    return np.array([limit] + given)


def ragged_sizes(own_key, number_of, total, most, slope):
    if number_of == 2:
        one = jax.random.randint(own_key, (), max(1, total - most), min(most, total - 1) + 1)
        return jnp.stack([one, total - one])
    sizes = jnp.asarray(profile(number_of, total, most, slope), jnp.int32)
    twos = (number_of - 1) // 2
    giver, sink = sizes[1:1 + 2 * twos:2], sizes[2:2 + 2 * twos:2]
    room = jnp.minimum(giver - 1, most - sink)
    moved = jax.random.randint(jax.random.fold_in(own_key, 1), (twos,), 0, 1 << 20) % (room + 1)
    sizes = sizes.at[1:1 + 2 * twos:2].set(giver - moved).at[2:2 + 2 * twos:2].set(sink + moved)
    return sizes[jax.random.permutation(jax.random.fold_in(own_key, 2), number_of)]


def gaussian(rng, extent, scale, bound, cuts=(), kind=jnp.bfloat16):
    values = scale * jax.random.normal(rng, extent, jnp.float32)
    if cuts:
        values = values * level_of(rng, extent, cuts, -0.22, 0.18)
    return jnp.clip(values, -bound, bound).astype(kind)


def setup_inputs(seed: int = 0) -> dict:
    key_list = jax.random.split(jax.random.key(seed), 41)
    return {
        "x_in": gaussian(key_list[0], (TOKENS, D), 1.0, 6.0, ((0, 8), (1, 4))),
        "grad_out": gaussian(key_list[1], (TOKENS, D), 1.0, 6.0, ((0, 8), (1, 4))),
        "w_qa": gaussian(key_list[2], (D, QR), D ** -0.5, 0.125, ((0, 8), (1, 4))),
        "w_kv": gaussian(key_list[3], (D, KVR), D ** -0.5, 0.125, ((0, 8), (1, 4))),
        "w_kr": gaussian(key_list[4], (D, ROPE), D ** -0.5, 0.125, ((0, 8),)),
        "w_qb": gaussian(key_list[5], (QR, HEADS * (NOPE + ROPE)), QR ** -0.5, 0.21875, ((0, 8), (1, 4))),
        "w_kvb": gaussian(key_list[6], (KVR, HEADS * (NOPE + VH)), KVR ** -0.5, 0.375, ((0, 8), (1, 4))),
        "w_o": gaussian(key_list[7], (D, HEADS * VH), 1 ** -0.5, 6.0, ((0, 8), (1, 4))),
        "w_gate": gaussian(key_list[8], (D, FF), D ** -0.5, 0.125, ((0, 8), (1, 4))),
        "w_up": gaussian(key_list[9], (D, FF), D ** -0.5, 0.125, ((0, 8), (1, 4))),
        "w_down": gaussian(key_list[10], (D, FF), 64 ** -0.5, 0.75, ((0, 8), (1, 4))),
        "norm_gains": jnp.clip(1.0 + 0.1 * jax.random.normal(key_list[11], (2, D), jnp.float32), 0.5, 1.5),
        "q_gain": jnp.clip(1.0 + 0.1 * jax.random.normal(key_list[12], (QR,), jnp.float32), 0.5, 1.5),
        "kv_gain": jnp.clip(1.0 + 0.1 * jax.random.normal(key_list[13], (KVR,), jnp.float32), 0.5, 1.5),
        "deal": jax.vmap(lambda own: jax.random.permutation(own, N_WIDE))(jax.random.split(key_list[14], N_WIDE)).reshape((N_WIDE, N_WIDE)).astype(jnp.int32),
        "lengths": jax.vmap(lambda own: ragged_sizes(own, SEQS, TOK_DEV, 3 * TOK_DEV // 4, 2))(jax.random.split(key_list[15], N_WIDE)).reshape((N_WIDE, SEQS)).astype(jnp.int32),
        "step_count": jax.random.randint(key_list[16], (1,), 1, 21).astype(jnp.int32),
        "owner_a": draw_owner_a(jax.random.fold_in(key_list[40], 71), 0),
        "owner_b": draw_owner_b(jax.random.fold_in(key_list[40], 71), 0),
        "owner_c": draw_owner_c(jax.random.fold_in(key_list[40], 71), 0),
        "basis_la": draw_basis_la(jax.random.fold_in(key_list[40], 71), 0),
        "basis_ra": draw_basis_ra(jax.random.fold_in(key_list[40], 71), 0),
        "basis_lb": draw_basis_lb(jax.random.fold_in(key_list[40], 71), 0),
        "basis_rb": draw_basis_rb(jax.random.fold_in(key_list[40], 71), 0),
        "basis_lc": draw_basis_lc(jax.random.fold_in(key_list[40], 71), 0),
        "basis_rc": draw_basis_rc(jax.random.fold_in(key_list[40], 71), 0),
        "mom_a": draw_mom_a(jax.random.fold_in(key_list[40], 71), 0),
        "sq_a": draw_sq_a(jax.random.fold_in(key_list[40], 71), 0),
        "mom_b": draw_mom_b(jax.random.fold_in(key_list[40], 71), 0),
        "sq_b": draw_sq_b(jax.random.fold_in(key_list[40], 71), 0),
        "mom_c": draw_mom_c(jax.random.fold_in(key_list[40], 71), 0),
        "sq_c": draw_sq_c(jax.random.fold_in(key_list[40], 71), 0),
        "kr_mom": draw_kr_mom(jax.random.fold_in(key_list[40], 71), 0),
        "kr_sq": draw_kr_sq(jax.random.fold_in(key_list[40], 71), 0),
        "gain_mom": draw_gain_mom(jax.random.fold_in(key_list[40], 71), 0),
        "gain_sq": draw_gain_sq(jax.random.fold_in(key_list[40], 71), 0),
        "qgain_mom": draw_qgain_mom(jax.random.fold_in(key_list[40], 71), 0),
        "qgain_sq": draw_qgain_sq(jax.random.fold_in(key_list[40], 71), 0),
        "kvgain_mom": draw_kvgain_mom(jax.random.fold_in(key_list[40], 71), 0),
        "kvgain_sq": draw_kvgain_sq(jax.random.fold_in(key_list[40], 71), 0),
    }


@jax.custom_vjp
def low(v):
    return lax.optimization_barrier(v.astype(jnp.bfloat16)).astype(jnp.float32)

@jax.custom_vjp
def low_back(v):
    return v

def low_keep(v):
    return (low(v), None)

def low_pass(kept, grad):
    return (grad,)

def back_keep(v):
    return (v, None)

def back_low(kept, grad):
    return (low(grad),)
low.defvjp(low_keep, low_pass)
low_back.defvjp(back_keep, back_low)
norm_eps = 1e-05
residual_scale = 1.4 / 62 ** 0.5
beta_one = 0.9
beta_two = 0.95
adam_eps = 1e-08
gain_rate = 0.5
masked_value = -1e+30
highest = lax.Precision.HIGHEST

def matmul(left_side, right_side):
    return jnp.dot(left_side, right_side, precision=highest)

def rms_scale(block_in, gain):
    return block_in * lax.rsqrt(lax.optimization_barrier(jnp.mean(block_in * block_in, axis=-1, keepdims=True)) + norm_eps) * gain

def rope_tables(positions):
    half_width = ROPE // 2
    frequency = 10000.0 ** (-2.0 * jnp.arange(half_width, dtype=jnp.float32) / ROPE)
    angles = positions.astype(jnp.float32)[:, None] * frequency[None, :]
    return (jnp.cos(angles), jnp.sin(angles))

def rotate(block_in, cosine_table, sine_table):
    half_width = block_in.shape[-1] // 2
    lower_half = block_in[..., :half_width]
    upper_half = block_in[..., half_width:]
    return jnp.concatenate([lower_half * cosine_table - upper_half * sine_table, upper_half * cosine_table + lower_half * sine_table], axis=-1)

def layout(seq_lengths):
    seq_ends = jnp.cumsum(seq_lengths).astype(jnp.int32)
    row_ids = jnp.arange(TOK_DEV, dtype=jnp.int32)
    segment = lax.optimization_barrier(jnp.sum((row_ids[:, None] >= seq_ends[None, :SEQS - 1]).astype(jnp.int32), axis=1)).astype(jnp.int32)
    seq_starts = (seq_ends - seq_lengths).astype(jnp.int32)
    pick = jnp.arange(SEQS, dtype=jnp.int32)[None, :] == segment[:, None]
    seq_start = lax.optimization_barrier(jnp.sum(jnp.where(pick, seq_starts[None, :], 0), axis=1)).astype(jnp.int32)
    return (row_ids, segment, row_ids - seq_start)

def layer_block(params, block_in, seq_lengths):
    row_ids, segment, positions = layout(seq_lengths)
    live_rows = (segment < SEQS - 1).astype(jnp.float32)[:, None]
    cosine_table, sine_table = rope_tables(positions)
    normed = low(rms_scale(block_in, params['norm_gains'][0]))
    q_latent = low_back(matmul(normed, params['w_qa']))
    kv_latent = low_back(matmul(normed, params['w_kv']))
    key_rot = low_back(matmul(normed, params['w_kr']))
    q_normed = low(rms_scale(q_latent, params['q_gain']))
    kv_normed = low(rms_scale(kv_latent, params['kv_gain']))
    q_pre = low_back(matmul(q_normed, params['w_qb'])).reshape(TOK_DEV, HEADS, NOPE + ROPE)
    kv_pre = low_back(matmul(kv_normed, params['w_kvb'])).reshape(TOK_DEV, HEADS, NOPE + VH)
    q_turned = rotate(q_pre[..., NOPE:], cosine_table[:, None, :], sine_table[:, None, :])
    queries = low(jnp.concatenate([q_pre[..., :NOPE], q_turned], axis=-1))
    key_turned = rotate(key_rot, cosine_table, sine_table)
    key_heads = low(jnp.concatenate([kv_pre[..., :NOPE], jnp.broadcast_to(key_turned[:, None, :], (TOK_DEV, HEADS, ROPE))], axis=-1))
    values = low(kv_pre[..., NOPE:])
    allowed = (segment[:, None] == segment[None, :]) & (row_ids[None, :] <= row_ids[:, None])
    scores = low_back(jnp.einsum('qhd,khd->hqk', queries, key_heads, precision=highest) * (NOPE + ROPE) ** (-0.5))
    scores = jnp.where(allowed[None], scores, masked_value)
    prob_rows = low(jax.nn.softmax(scores, axis=-1))
    heads_out = jnp.einsum('hqk,khd->qhd', prob_rows, values, precision=highest)
    heads_out = low_back(low(heads_out)).reshape(TOK_DEV, HEADS * VH)
    attn_out = low_back(matmul(heads_out, params['w_o'].T))
    middle = block_in + residual_scale * live_rows * attn_out
    normed_two = low(rms_scale(middle, params['norm_gains'][1]))
    gate_act = low_back(matmul(normed_two, params['w_gate']))
    upward = low_back(matmul(normed_two, params['w_up']))
    active = low(jax.nn.silu(gate_act) * upward)
    mlp_out = low_back(matmul(active, params['w_down'].T))
    return middle + residual_scale * live_rows * mlp_out

def to_units(matrix):
    row_count, col_count = matrix.shape
    count = col_count // (N_NARROW * SLAB)
    return matrix.reshape(row_count, N_NARROW, count, SLAB).transpose(1, 2, 0, 3)

def from_units(unit_rows, row_count):
    return unit_rows.transpose(2, 0, 1, 3).reshape(row_count, -1)

def soap_class(matrices, rates, owner, basis_l, basis_r, moment, square, tcount):
    row_count = matrices[0].shape[0]
    counts = [matrix.shape[1] // (N_NARROW * SLAB) for matrix in matrices]
    unit_rows = jnp.concatenate([to_units(matrix) for matrix in matrices], axis=1)
    unit_rate = jnp.concatenate([jnp.full((count,), step_rate, jnp.float32) for count, step_rate in zip(counts, rates)])
    slots = moment.shape[0]

    def by_narrow(array_in, col_width):
        return array_in.reshape(slots, array_in.shape[1], N_NARROW, col_width).transpose(2, 0, 1, 3)

    def per_column(unit_block, owner_ids, left_basis, right_basis, moment_col, square_col):
        left_pick = left_basis[owner_ids].reshape(-1, row_count // BASIS, BASIS, BASIS)
        right_pick = right_basis[owner_ids]
        blocks = unit_block.reshape(-1, row_count // BASIS, BASIS, SLAB)
        turned = jnp.einsum('ubik,ubin->ubkn', left_pick, blocks, precision=highest)
        turned = jnp.einsum('ubkn,unm->ubkm', turned, right_pick, precision=highest).reshape(unit_block.shape)
        new_moment = beta_one * moment_col[owner_ids] + (1.0 - beta_one) * turned
        new_square = beta_two * square_col[owner_ids] + (1.0 - beta_two) * turned * turned
        direction = new_moment / (1.0 - beta_one ** tcount) / (jnp.sqrt(new_square / (1.0 - beta_two ** tcount)) + adam_eps)
        rotated_back = jnp.einsum('ubkm,unm->ubkn', direction.reshape(blocks.shape), right_pick, precision=highest)
        rotated_back = jnp.einsum('ubik,ubkn->ubin', left_pick, rotated_back, precision=highest).reshape(unit_block.shape)
        return (-unit_rate[:, None, None] * rotated_back, moment_col.at[owner_ids].set(new_moment), square_col.at[owner_ids].set(new_square))
    updates, moments, squares = jax.vmap(per_column)(unit_rows, owner, by_narrow(basis_l, BASIS), by_narrow(basis_r, SLAB), by_narrow(moment, SLAB), by_narrow(square, SLAB))
    pieces, begin_unit = ([], 0)
    for count in counts:
        pieces.append(from_units(updates[:, begin_unit:begin_unit + count], row_count))
        begin_unit += count

    def restore(array_in):
        return array_in.transpose(1, 2, 0, 3).reshape(slots, row_count, N_NARROW * SLAB)
    return (pieces, restore(moments), restore(squares))

def plain_adam(gradient, moment, square, step_rate, tcount):
    new_moment = beta_one * moment + (1.0 - beta_one) * gradient
    new_square = beta_two * square + (1.0 - beta_two) * gradient * gradient
    direction = new_moment / (1.0 - beta_one ** tcount) / (jnp.sqrt(new_square / (1.0 - beta_two ** tcount)) + adam_eps)
    return (-step_rate * direction, new_moment, new_square)

def reference(x_in, grad_out, w_qa, w_kv, w_kr, w_qb, w_kvb, w_o, w_gate, w_up, w_down, norm_gains, q_gain, kv_gain, deal, lengths, step_count, owner_a, owner_b, owner_c, basis_la, basis_ra, basis_lb, basis_rb, basis_lc, basis_rc, mom_a, sq_a, mom_b, sq_b, mom_c, sq_c, kr_mom, kr_sq, gain_mom, gain_sq, qgain_mom, qgain_sq, kvgain_mom, kvgain_sq):
    inverse = jnp.argsort(deal, axis=1).astype(jnp.int32)
    sources = jnp.arange(N_WIDE, dtype=jnp.int32)

    def to_work(array_in):
        pieces = array_in.astype(jnp.float32).reshape(N_WIDE, N_WIDE, PIECE, D)
        return pieces[sources[None, :], inverse.T].reshape(N_WIDE, TOK_DEV, D)

    def to_input(array_in):
        pieces = array_in.reshape(N_WIDE, N_WIDE, PIECE, D)
        return pieces[deal, sources[:, None]].reshape(TOKENS, D)
    params = {'w_qa': w_qa.astype(jnp.float32), 'w_kv': w_kv.astype(jnp.float32), 'w_kr': w_kr.astype(jnp.float32), 'w_qb': w_qb.astype(jnp.float32), 'w_kvb': w_kvb.astype(jnp.float32), 'w_o': w_o.astype(jnp.float32), 'w_gate': w_gate.astype(jnp.float32), 'w_up': w_up.astype(jnp.float32), 'w_down': w_down.astype(jnp.float32), 'norm_gains': norm_gains, 'q_gain': q_gain, 'kv_gain': kv_gain}

    def forward(prm, blocks):

        def scan_step(carried, inputs):
            return (carried, jax.checkpoint(layer_block)(prm, inputs[0], inputs[1]))
        return lax.scan(scan_step, None, (blocks, lengths))[1]
    outputs, pullback = jax.vjp(forward, params, to_work(x_in))
    gradients, grad_work = pullback(to_work(grad_out))
    tcount = step_count[0].astype(jnp.float32)
    wide_rate = D ** (-0.5)
    updates_a, new_mom_a, new_sq_a = soap_class([gradients['w_qa'], gradients['w_kv'], gradients['w_o'], gradients['w_gate'], gradients['w_up'], gradients['w_down']], [wide_rate, wide_rate, 1.0, wide_rate, wide_rate, 0.125], owner_a, basis_la, basis_ra, mom_a, sq_a, tcount)
    updates_b, new_mom_b, new_sq_b = soap_class([gradients['w_qb']], [QR ** (-0.5)], owner_b, basis_lb, basis_rb, mom_b, sq_b, tcount)
    updates_c, new_mom_c, new_sq_c = soap_class([gradients['w_kvb']], [KVR ** (-0.5)], owner_c, basis_lc, basis_rc, mom_c, sq_c, tcount)
    update_kr, new_kr_mom, new_kr_sq = plain_adam(gradients['w_kr'], kr_mom, kr_sq, wide_rate, tcount)
    update_gains, new_gain_mom, new_gain_sq = plain_adam(gradients['norm_gains'], gain_mom, gain_sq, gain_rate, tcount)
    update_qgain, new_qgain_mom, new_qgain_sq = plain_adam(gradients['q_gain'], qgain_mom, qgain_sq, gain_rate, tcount)
    update_kvgain, new_kvgain_mom, new_kvgain_sq = plain_adam(gradients['kv_gain'], kvgain_mom, kvgain_sq, gain_rate, tcount)
    return (to_input(outputs), to_input(grad_work), gradients['w_qa'], gradients['w_kv'], gradients['w_qb'], gradients['w_kvb'], gradients['w_o'], gradients['w_gate'], gradients['w_up'], gradients['w_down'], params['w_qa'] + updates_a[0], params['w_kv'] + updates_a[1], params['w_qb'] + updates_b[0], params['w_kvb'] + updates_c[0], params['w_o'] + updates_a[2], params['w_gate'] + updates_a[3], params['w_up'] + updates_a[4], params['w_down'] + updates_a[5], gradients['w_kr'], params['w_kr'] + update_kr, new_kr_mom, new_kr_sq, gradients['norm_gains'], norm_gains + update_gains, new_gain_mom, new_gain_sq, gradients['q_gain'], q_gain + update_qgain, new_qgain_mom, new_qgain_sq, gradients['kv_gain'], kv_gain + update_kvgain, new_kvgain_mom, new_kvgain_sq, new_mom_a, new_sq_a, new_mom_b, new_sq_b, new_mom_c, new_sq_c)
```

```python
import jax
import jax.numpy as jnp
from jax import lax
from jax.experimental import pallas as pl
from jax.experimental.pallas import tpu as pltpu
from jax.sharding import PartitionSpec as P

D = 2560
NOPE = 64
ROPE = 32
VH = 64
QR = 768
KVR = 256
SLAB = 64
BASIS = 128


norm_eps = 1e-05
residual_scale = 1.4 / 62**0.5
beta_one = 0.9
beta_two = 0.95
adam_eps = 1e-08
gain_rate = 0.5
masked_value = -1e30
bf16 = jnp.bfloat16
f32 = jnp.float32


def product(left_side, right_side):
    return jnp.dot(left_side, right_side, preferred_element_type=jnp.float32)


def inner_rows(left_side, right_side):
    return lax.dot_general(
        left_side, right_side, (((0,), (0,)), ((), ())), preferred_element_type=jnp.float32
    )


def against_rows(left_side, right_side):
    return lax.dot_general(
        left_side, right_side, (((1,), (1,)), ((), ())), preferred_element_type=jnp.float32
    )


def rope_tables(positions):
    half_width = ROPE // 2
    frequency = 10000.0 ** (-2.0 * jnp.arange(half_width, dtype=jnp.float32) / ROPE)
    angles = positions.astype(jnp.float32)[:, None] * frequency[None, :]
    return (jnp.cos(angles), jnp.sin(angles))


def rotate(block_in, cosine_table, sine_table, direction_sign):
    half_width = block_in.shape[-1] // 2
    lower_half = block_in[..., :half_width]
    upper_half = block_in[..., half_width:]
    signed_sine = direction_sign * sine_table
    return jnp.concatenate(
        [
            lower_half * cosine_table - upper_half * signed_sine,
            upper_half * cosine_table + lower_half * signed_sine,
        ],
        axis=-1,
    )


def plain_adam(gradient, moment, square, step_rate, tcount):
    new_moment = beta_one * moment + (1.0 - beta_one) * gradient
    new_square = beta_two * square + (1.0 - beta_two) * gradient * gradient
    direction = (
        new_moment
        / (1.0 - beta_one**tcount)
        / (jnp.sqrt(new_square / (1.0 - beta_two**tcount)) + adam_eps)
    )
    return (-step_rate * direction, new_moment, new_square)


def shifted(value, step):
    count = lax.axis_size("narrow")
    return lax.ppermute(value, "narrow", [(i, (i + step) % count) for i in range(count)])


def flipped(value, bit):
    count = lax.axis_size("wide")
    return lax.ppermute(value, "wide", [(i, i ^ bit) for i in range(count)])


def gather_features(features):
    count = lax.axis_size("narrow")
    index = lax.axis_index("narrow")
    width = features.shape[1]
    parts = [features] + [shifted(features, step) for step in range(1, count)]
    joined = jnp.zeros((features.shape[0], count * width), features.dtype)
    for step, part in enumerate(parts):
        joined = lax.dynamic_update_slice(joined, part, (0, ((index - step) % count) * width))
    return joined


def reduce_features(features):
    count = lax.axis_size("narrow")
    index = lax.axis_index("narrow")
    width = features.shape[1] // count

    def piece(step):
        return lax.dynamic_slice_in_dim(features, ((index + step) % count) * width, width, 1)

    arrived = [shifted(piece(step), step) for step in range(1, count)]
    total = piece(0).astype(f32)
    for part in arrived:
        total = total + part.astype(f32)
    return total


def row_totals(values):
    count = lax.axis_size("narrow")
    return values + sum(shifted(values, step) for step in range(1, count))


def relative_chunks(features):
    count = lax.axis_size("wide")
    order = lax.axis_index("wide") ^ jnp.arange(count, dtype=jnp.int32)
    turned = features.T.reshape(count, features.shape[1] // count, features.shape[0])
    return jnp.take(turned, order, axis=0)


def scatter_rows(left_chunks, right_side):
    count, rows, tokens = left_chunks.shape
    bits = count.bit_length() - 1
    columns = right_side.shape[1]
    near = left_chunks[0::2].reshape(-1, tokens)
    away = left_chunks[1::2].reshape(-1, tokens)
    sent = flipped(product(away, right_side).astype(bf16), 1)
    kept = product(near, right_side).astype(bf16)
    shape = (2,) * (bits - 1) + (rows, columns)
    sent = sent.reshape(shape)
    kept = kept.reshape(shape)
    first_bits = list(range(1, bits))
    middle = (bits - 1) // 2
    half = rows // 2
    results = []
    for begin, order in (
        (0, first_bits),
        (half, first_bits[middle:] + first_bits[:middle]),
    ):
        total = kept[..., begin : begin + half, :].astype(f32) + sent[
            ..., begin : begin + half, :
        ].astype(f32)
        dims = list(range(bits - 1, 0, -1))
        for bit in order:
            at = dims.index(bit)
            dims.pop(at)
            away_part = lax.index_in_dim(total, 1, at, keepdims=False)
            near_part = lax.index_in_dim(total, 0, at, keepdims=False)
            arrived = flipped(away_part.astype(bf16), 1 << bit)
            total = near_part + arrived.astype(f32)
        results.append(total)
    return jnp.concatenate(results, axis=0)


def unit_rates(col_widths, rates):
    return jnp.concatenate(
        [
            jnp.full((col_width // SLAB,), step_rate, jnp.float32)
            for col_width, step_rate in zip(col_widths, rates)
        ]
    )


def slot_kernel(scale_ref, gradient_ref, left_ref, right_ref, moment_ref, square_ref,
                change_ref, new_moment_ref, new_square_ref, whole_ref, turned_ref):
    slot = pl.program_id(0)
    sources, rows = gradient_ref.shape[0], gradient_ref.shape[3]
    blocks = left_ref.shape[1] // BASIS
    right_basis = right_ref[0].astype(bf16)
    for source in range(sources):
        whole_ref[:, source * rows : (source + 1) * rows] = gradient_ref[source, 0].astype(f32)
    rate = scale_ref[slot]
    occupied = scale_ref[pl.num_programs(0) + slot]
    first_scale = scale_ref[2 * pl.num_programs(0)]
    second_scale = scale_ref[2 * pl.num_programs(0) + 1]
    turned_ref[...] = lax.dot_general(
        right_basis, whole_ref[...].astype(bf16), (((0,), (0,)), ((), ())),
        preferred_element_type=f32,
    )

    for block in range(blocks):
        at = slice(block * BASIS, (block + 1) * BASIS)
        left_basis = left_ref[0, at, :].astype(bf16)
        turned = jnp.dot(turned_ref[:, at].astype(bf16), left_basis, preferred_element_type=f32)
        moment = moment_ref[0, :, at]
        square = square_ref[0, :, at]
        new_moment = beta_one * moment + (1.0 - beta_one) * turned
        new_square = beta_two * square + (1.0 - beta_two) * turned * turned
        new_moment_ref[0, :, at] = jnp.where(occupied > 0.5, new_moment, moment)
        new_square_ref[0, :, at] = jnp.where(occupied > 0.5, new_square, square)
        direction = new_moment * first_scale / (jnp.sqrt(new_square * second_scale) + adam_eps)
        turned_ref[:, at] = lax.dot_general(
            direction.astype(bf16), left_basis, (((1,), (1,)), ((), ())),
            preferred_element_type=f32,
        )
    whole_ref[...] = rate * jnp.dot(
        right_basis, turned_ref[...].astype(bf16), preferred_element_type=f32
    )
    for source in range(sources):
        change_ref[source, 0] = whole_ref[:, source * rows : (source + 1) * rows].astype(bf16)


def slot_steps(gradient, left_basis, right_basis, moment, square, scales):
    sources, capacity, _, rows = gradient.shape
    row_count = sources * rows
    moment = moment.transpose(0, 2, 1)
    square = square.transpose(0, 2, 1)
    state = pl.BlockSpec((1, SLAB, row_count), lambda slot: (slot, 0, 0))
    traded = pl.BlockSpec((sources, 1, SLAB, rows), lambda slot: (0, slot, 0, 0))
    change, new_moment, new_square = pl.pallas_call(
        slot_kernel,
        grid=(capacity,),
        in_specs=[
            pl.BlockSpec(memory_space=pltpu.SMEM),
            traded,
            pl.BlockSpec((1, row_count, BASIS), lambda slot: (slot, 0, 0)),
            pl.BlockSpec((1, SLAB, SLAB), lambda slot: (slot, 0, 0)),
            state,
            state,
        ],
        out_specs=[traded, state, state],
        out_shape=[
            jax.ShapeDtypeStruct(gradient.shape, bf16),
            jax.ShapeDtypeStruct(moment.shape, f32),
            jax.ShapeDtypeStruct(square.shape, f32),
        ],
        scratch_shapes=[
            pltpu.VMEM((SLAB, row_count), f32),
            pltpu.VMEM((SLAB, row_count), f32),
        ],
        compiler_params=pltpu.CompilerParams(vmem_limit_bytes=48 * 1024 * 1024),
    )(scales, gradient, left_basis, right_basis, moment, square)
    return change, new_moment.transpose(0, 2, 1), new_square.transpose(0, 2, 1)


def owner_step(
    blocks, owner_ids, left_basis, right_basis, moment, square, rate_table, wide_index, tcount
):
    wide_count = lax.axis_size("wide")
    capacity = moment.shape[0]
    rows = blocks[0].shape[0]
    unit_rows = jnp.concatenate([block.T for block in blocks], axis=0).astype(bf16)
    unit_rows = unit_rows.reshape(-1, SLAB, rows)
    units = unit_rows.shape[0]
    slots = jnp.arange(wide_count * capacity, dtype=jnp.int32)
    matches = slots[:, None] == owner_ids[None, :]
    unit_of = jnp.sum(
        jnp.where(matches, jnp.arange(units, dtype=jnp.int32)[None, :], 0), axis=1
    )
    sending = jnp.take(unit_rows, unit_of, axis=0, mode="clip")
    owned = lax.all_to_all(
        sending.reshape(wide_count, capacity, SLAB, rows), "wide", split_axis=0, concat_axis=0,
        tiled=True,
    )
    slot_ids = wide_index * capacity + jnp.arange(capacity, dtype=jnp.int32)
    own = (owner_ids[None, :] == slot_ids[:, None]).astype(f32)
    slot_rate = -jnp.sum(own * rate_table[None, :], axis=1)
    scales = jnp.concatenate(
        [
            slot_rate,
            jnp.sum(own, axis=1),
            (1.0 / (1.0 - beta_one**tcount))[None],
            (1.0 / (1.0 - beta_two**tcount))[None],
        ]
    )
    change, new_moment, new_square = slot_steps(
        owned, left_basis, right_basis, moment, square, scales
    )
    back = lax.all_to_all(change, "wide", split_axis=0, concat_axis=0, tiled=True)
    back = back.reshape(wide_count * capacity, SLAB, rows)
    steps = jnp.take(back, owner_ids, axis=0, mode="clip").reshape(units * SLAB, rows)
    pieces, begin = ([], 0)
    for block in blocks:
        pieces.append(steps[begin : begin + block.shape[1]].T.astype(f32))
        begin += block.shape[1]
    return pieces, new_moment, new_square


def body(
    x_in,
    grad_out,
    w_qa,
    w_kv,
    w_kr,
    w_qb,
    w_kvb,
    w_o,
    w_gate,
    w_up,
    w_down,
    norm_gains,
    q_gain,
    kv_gain,
    deal,
    lengths,
    step_count,
    owner_a,
    owner_b,
    owner_c,
    basis_la,
    basis_ra,
    basis_lb,
    basis_rb,
    basis_lc,
    basis_rc,
    mom_a,
    sq_a,
    mom_b,
    sq_b,
    mom_c,
    sq_c,
    kr_mom,
    kr_sq,
    gain_mom,
    gain_sq,
    qgain_mom,
    qgain_sq,
    kvgain_mom,
    kvgain_sq,
):
    wide_count = lax.axis_size("wide")
    wide_index = lax.axis_index("wide")
    narrow_index = lax.axis_index("narrow")
    row_count, local_width = x_in.shape
    piece_rows = row_count // wide_count
    deal_row = lax.dynamic_index_in_dim(deal, wide_index, 0, keepdims=False)
    wide_ids = jnp.arange(wide_count, dtype=jnp.int32)
    inverse = jnp.sum(
        jnp.where(deal_row[None, :] == wide_ids[:, None], wide_ids[None, :], 0), axis=1
    )

    def to_working(features):
        outgoing = jnp.take(
            features.reshape((wide_count, piece_rows) + features.shape[1:]), inverse, axis=0,
            mode="clip",
        )
        dealt = lax.all_to_all(outgoing, "wide", split_axis=0, concat_axis=0, tiled=True)
        return dealt.reshape(row_count, -1)

    token_in = to_working(x_in)
    token_grad = to_working(grad_out)
    residual = token_in.astype(f32)
    grad_top = token_grad.astype(f32)
    seq_lengths = lengths[0]
    seq_ends = jnp.cumsum(seq_lengths)
    row_ids = jnp.arange(row_count, dtype=jnp.int32)
    segment = jnp.sum((row_ids[:, None] >= seq_ends[None, :-1]).astype(jnp.int32), axis=1)
    pick = jnp.arange(seq_lengths.shape[0], dtype=jnp.int32)[None, :] == segment[:, None]
    seq_start = jnp.sum(jnp.where(pick, (seq_ends - seq_lengths)[None, :], 0), axis=1)
    live_rows = (segment < seq_lengths.shape[0] - 1).astype(f32)[:, None]
    cosine_table, sine_table = rope_tables(row_ids - seq_start)
    cos_heads = cosine_table[:, None, :]
    sin_heads = sine_table[:, None, :]

    latent_own = jnp.concatenate([w_qa, w_kv, w_kr], axis=1)
    head_rows = jnp.concatenate(
        [jnp.pad(w_qb, ((0, 0), (0, w_kvb.shape[1] - w_qb.shape[1]))), w_kvb], axis=0
    )
    full_latent = lax.all_gather(latent_own, "wide", axis=0, tiled=True)
    full_heads = lax.all_gather(head_rows, "wide", axis=0)
    full_qb = full_heads[:, : w_qb.shape[0], : w_qb.shape[1]].reshape(-1, w_qb.shape[1])
    full_kvb = full_heads[:, w_qb.shape[0] :, :].reshape(-1, w_kvb.shape[1])
    full_o = lax.all_gather(w_o, "wide", axis=0, tiled=True)
    full_gate = lax.all_gather(w_gate, "wide", axis=0, tiled=True)
    full_up = lax.all_gather(w_up, "wide", axis=0, tiled=True)
    full_down = lax.all_gather(w_down, "wide", axis=0, tiled=True)
    gains_all = lax.all_gather(
        jnp.concatenate([norm_gains[0], norm_gains[1], q_gain, kv_gain]), "narrow"
    )
    first_gain = gains_all[:, :local_width].reshape(1, -1)
    second_gain = gains_all[:, local_width : 2 * local_width].reshape(1, -1)
    q_width = q_gain.shape[0]
    kv_width = kv_gain.shape[0]
    q_gain_all = gains_all[:, 2 * local_width : 2 * local_width + q_width].reshape(1, -1)
    kv_gain_all = gains_all[:, 2 * local_width + q_width :].reshape(1, -1)

    def inverse_rms(features, width):
        wide = features.astype(f32)
        return lax.rsqrt(jnp.sum(wide * wide, axis=1, keepdims=True) / width + norm_eps)

    token_all = gather_features(token_in)
    inv_first = inverse_rms(token_all, D)
    normed = (token_all.astype(f32) * inv_first * first_gain).astype(bf16)
    latents = product(normed, full_latent)
    q_latent = latents[:, :q_width]
    kv_latent = latents[:, q_width : q_width + kv_width]
    key_rot = latents[:, q_width + kv_width :]
    narrow_count = lax.axis_size("narrow")
    latents_all = gather_features(latents[:, : q_width + kv_width].astype(bf16))
    latents_all = latents_all.reshape(row_count, narrow_count, q_width + kv_width)
    q_latent_all = latents_all[:, :, :q_width].reshape(row_count, QR).astype(f32)
    kv_latent_all = latents_all[:, :, q_width:].reshape(row_count, KVR).astype(f32)
    inv_q = inverse_rms(q_latent_all, QR)
    inv_kv = inverse_rms(kv_latent_all, KVR)
    q_normed = (q_latent_all * inv_q * q_gain_all).astype(bf16)
    kv_normed = (kv_latent_all * inv_kv * kv_gain_all).astype(bf16)
    heads_here = w_o.shape[1] // VH
    q_pre = product(q_normed, full_qb)
    kv_pre = product(kv_normed, full_kvb)
    q_pre_heads = q_pre.reshape(row_count, heads_here, NOPE + ROPE)
    kv_pre_heads = kv_pre.reshape(row_count, heads_here, NOPE + VH)
    queries = jnp.concatenate(
        [
            q_pre_heads[..., :NOPE],
            rotate(q_pre_heads[..., NOPE:], cos_heads, sin_heads, 1.0),
        ],
        axis=-1,
    ).astype(bf16)
    key_turned = rotate(key_rot, cosine_table, sine_table, 1.0)
    key_heads = jnp.concatenate(
        [
            kv_pre_heads[..., :NOPE],
            jnp.broadcast_to(key_turned[:, None, :], (row_count, heads_here, ROPE)),
        ],
        axis=-1,
    ).astype(bf16)
    values = kv_pre_heads[..., NOPE:].astype(bf16)
    score_scale = (NOPE + ROPE) ** (-0.5)
    allowed = (segment[:, None] == segment[None, :]) & (row_ids[None, :] <= row_ids[:, None])

    def all_scores():
        scores = (
            jnp.einsum("qhd,khd->hqk", queries, key_heads, preferred_element_type=f32)
            * score_scale
        )
        return jnp.where(allowed[None], scores, masked_value)

    scores = all_scores()
    row_max = jnp.max(scores, axis=-1, keepdims=True)
    exp_scores = jnp.exp(scores - row_max)
    row_total = jnp.sum(exp_scores, axis=-1, keepdims=True)
    prob_rows = (exp_scores / row_total).astype(bf16)
    heads_out = jnp.einsum("hqk,khd->qhd", prob_rows, values, preferred_element_type=f32)
    heads_out = heads_out.astype(bf16).reshape(row_count, heads_here * VH)
    log_totals = row_max + jnp.log(row_total)
    attn_out = reduce_features(against_rows(heads_out, full_o).astype(bf16))
    middle = residual + residual_scale * live_rows * attn_out
    middle_all = gather_features(middle.astype(bf16)).astype(f32)
    inv_second = inverse_rms(middle_all, D)
    normed_two = (middle_all * inv_second * second_gain).astype(bf16)
    gate_act = product(normed_two, full_gate)
    upward = product(normed_two, full_up)
    sigmoid_gate = jax.nn.sigmoid(gate_act)
    silu_gate = gate_act * sigmoid_gate
    active = (silu_gate * upward).astype(bf16)
    mlp_out = reduce_features(against_rows(active, full_down).astype(bf16))
    layer_out = middle + residual_scale * live_rows * mlp_out

    mlp_grad = gather_features((residual_scale * live_rows * grad_top).astype(bf16))
    active_grad = product(mlp_grad, full_down)
    gate_grad = (
        active_grad * upward * (sigmoid_gate + silu_gate * (1.0 - sigmoid_gate))
    ).astype(bf16)
    up_grad = (active_grad * silu_gate).astype(bf16)
    normed_two_part = (
        against_rows(gate_grad, full_gate) + against_rows(up_grad, full_up)
    ).astype(bf16)
    second_dot = row_totals(
        jnp.sum(gate_grad.astype(f32) * gate_act + up_grad.astype(f32) * upward, axis=1)
    )[:, None]
    normed_two_grad = reduce_features(normed_two_part)
    block_down = scatter_rows(relative_chunks(mlp_grad), active)
    chunks_two = relative_chunks(normed_two)
    block_gate = scatter_rows(chunks_two, gate_grad)
    block_up = scatter_rows(chunks_two, up_grad)
    post_gain_grad = jnp.sum(normed_two_grad * middle * inv_second, axis=0)
    middle_grad = (
        grad_top
        + inv_second * norm_gains[1] * normed_two_grad
        - middle * inv_second**2 * second_dot / D
    )
    attn_grad = gather_features((residual_scale * live_rows * middle_grad).astype(bf16))
    block_o = scatter_rows(relative_chunks(attn_grad), heads_out)
    heads_grad = product(attn_grad, full_o).astype(bf16).reshape(row_count, heads_here, VH)

    prob_rows = jnp.exp(all_scores() - log_totals)
    value_grad = jnp.einsum(
        "hqk,qhd->khd", prob_rows.astype(bf16), heads_grad, preferred_element_type=f32
    )
    prob_grad = jnp.einsum("qhd,khd->hqk", heads_grad, values, preferred_element_type=f32)
    delta_rows = jnp.sum(prob_rows * prob_grad, axis=-1, keepdims=True)
    score_grad = (prob_rows * (prob_grad - delta_rows)).astype(bf16)
    query_grad = score_scale * jnp.einsum(
        "hqk,khd->qhd", score_grad, key_heads, preferred_element_type=f32
    )
    key_grad = score_scale * jnp.einsum(
        "hqk,qhd->khd", score_grad, queries, preferred_element_type=f32
    )
    q_pre_grad = jnp.concatenate(
        [query_grad[..., :NOPE], rotate(query_grad[..., NOPE:], cos_heads, sin_heads, -1.0)],
        axis=-1,
    )
    q_pre_grad = q_pre_grad.reshape(row_count, -1).astype(bf16)
    kv_pre_grad = jnp.concatenate([key_grad[..., :NOPE], value_grad], axis=-1)
    kv_pre_grad = kv_pre_grad.reshape(row_count, -1).astype(bf16)
    rot_partial = rotate(jnp.sum(key_grad[..., NOPE:], axis=1), cosine_table, sine_table, -1.0)
    rot_grad = row_totals(rot_partial).astype(bf16)
    q_dot = jnp.sum(q_pre_grad.astype(f32) * q_pre, axis=1)
    kv_dot = jnp.sum(kv_pre_grad.astype(f32) * kv_pre, axis=1)
    dots = row_totals(jnp.stack([q_dot, kv_dot]))
    q_dot = dots[0][:, None]
    kv_dot = dots[1][:, None]
    q_part = against_rows(q_pre_grad, full_qb).astype(bf16)
    kv_part = against_rows(kv_pre_grad, full_kvb).astype(bf16)
    both_part = jnp.concatenate(
        [
            q_part.reshape(row_count, narrow_count, q_width),
            kv_part.reshape(row_count, narrow_count, kv_width),
        ],
        axis=-1,
    ).reshape(row_count, -1)
    both_grad = reduce_features(both_part)
    q_normed_grad = both_grad[:, :q_width]
    kv_normed_grad = both_grad[:, q_width:]
    block_qb = scatter_rows(relative_chunks(q_normed), q_pre_grad)
    block_kvb = scatter_rows(relative_chunks(kv_normed), kv_pre_grad)
    q_gain_grad = jnp.sum(q_normed_grad * q_latent * inv_q, axis=0)
    kv_gain_grad = jnp.sum(kv_normed_grad * kv_latent * inv_kv, axis=0)
    q_latent_grad = (
        inv_q * q_gain * q_normed_grad - q_latent * inv_q**2 * q_dot / QR
    ).astype(bf16)
    kv_latent_grad = (
        inv_kv * kv_gain * kv_normed_grad - kv_latent * inv_kv**2 * kv_dot / KVR
    ).astype(bf16)
    share = (narrow_index == 0).astype(f32)
    first_dot = row_totals(
        jnp.sum(q_latent_grad.astype(f32) * q_latent, axis=1)
        + jnp.sum(kv_latent_grad.astype(f32) * kv_latent, axis=1)
        + share * jnp.sum(rot_grad.astype(f32) * key_rot, axis=1)
    )[:, None]
    latent_grad = jnp.concatenate([q_latent_grad, kv_latent_grad, rot_grad], axis=1)
    block_latent = scatter_rows(relative_chunks(normed), latent_grad)
    block_qa = block_latent[:, :q_width]
    block_kv = block_latent[:, q_width : q_width + kv_width]
    block_kr = block_latent[:, q_width + kv_width :]
    full_kr = full_latent[:, q_width + kv_width :]
    own_kr = lax.dynamic_slice_in_dim(full_kr, narrow_index * local_width, local_width, 0)
    normed_part = against_rows(
        latent_grad[:, : q_width + kv_width], full_latent[:, : q_width + kv_width]
    ).astype(bf16)
    normed_grad = reduce_features(normed_part) + against_rows(rot_grad, own_kr)
    in_gain_grad = jnp.sum(normed_grad * residual * inv_first, axis=0)
    input_grad = (
        middle_grad
        + inv_first * norm_gains[0] * normed_grad
        - residual * inv_first**2 * first_dot / D
    )

    def to_input(features):
        returned = lax.all_to_all(
            features.astype(bf16).reshape(wide_count, piece_rows, -1), "wide", split_axis=0,
            concat_axis=0, tiled=True,
        )
        return jnp.take(returned, deal_row, axis=0, mode="clip").astype(f32).reshape(row_count, -1)

    final_out = to_input(layer_out)
    final_grad = to_input(input_grad)
    gain_grads = lax.psum(
        jnp.concatenate([in_gain_grad, post_gain_grad, q_gain_grad, kv_gain_grad]), "wide"
    )
    gains_total = gain_grads[: 2 * local_width].reshape(2, local_width)
    qgain_total = gain_grads[2 * local_width : 2 * local_width + q_width]
    kvgain_total = gain_grads[2 * local_width + q_width :]
    tcount = step_count[0].astype(f32)
    wide_rate = D ** (-0.5)
    class_a = [block_qa, block_kv, block_o, block_gate, block_up, block_down]
    widths_a = [block.shape[1] for block in class_a]
    rates_a = unit_rates(widths_a, [wide_rate, wide_rate, 1.0, wide_rate, wide_rate, 0.125])
    rates_b = unit_rates([block_qb.shape[1]], [QR ** (-0.5)])
    rates_c = unit_rates([block_kvb.shape[1]], [KVR ** (-0.5)])
    updates_a, new_mom_a, new_sq_a = owner_step(
        class_a, owner_a[0], basis_la, basis_ra, mom_a, sq_a, rates_a, wide_index, tcount
    )
    updates_b, new_mom_b, new_sq_b = owner_step(
        [block_qb], owner_b[0], basis_lb, basis_rb, mom_b, sq_b, rates_b, wide_index, tcount
    )
    updates_c, new_mom_c, new_sq_c = owner_step(
        [block_kvb], owner_c[0], basis_lc, basis_rc, mom_c, sq_c, rates_c, wide_index, tcount
    )
    update_qb = updates_b[0]
    update_kvb = updates_c[0]
    update_kr, new_kr_mom, new_kr_sq = plain_adam(block_kr, kr_mom, kr_sq, wide_rate, tcount)
    update_gains, new_gain_mom, new_gain_sq = plain_adam(
        gains_total, gain_mom, gain_sq, gain_rate, tcount
    )
    update_qgain, new_qgain_mom, new_qgain_sq = plain_adam(
        qgain_total, qgain_mom, qgain_sq, gain_rate, tcount
    )
    update_kvgain, new_kvgain_mom, new_kvgain_sq = plain_adam(
        kvgain_total, kvgain_mom, kvgain_sq, gain_rate, tcount
    )
    return (
        final_out,
        final_grad,
        block_qa,
        block_kv,
        block_qb,
        block_kvb,
        block_o,
        block_gate,
        block_up,
        block_down,
        w_qa.astype(f32) + updates_a[0],
        w_kv.astype(f32) + updates_a[1],
        w_qb.astype(f32) + update_qb,
        w_kvb.astype(f32) + update_kvb,
        w_o.astype(f32) + updates_a[2],
        w_gate.astype(f32) + updates_a[3],
        w_up.astype(f32) + updates_a[4],
        w_down.astype(f32) + updates_a[5],
        block_kr,
        w_kr.astype(f32) + update_kr,
        new_kr_mom,
        new_kr_sq,
        gains_total,
        norm_gains + update_gains,
        new_gain_mom,
        new_gain_sq,
        qgain_total,
        q_gain + update_qgain,
        new_qgain_mom,
        new_qgain_sq,
        kvgain_total,
        kv_gain + update_kvgain,
        new_kvgain_mom,
        new_kvgain_sq,
        new_mom_a,
        new_sq_a,
        new_mom_b,
        new_sq_b,
        new_mom_c,
        new_sq_c,
    )


def solution(mesh):
    return jax.shard_map(
        body,
        mesh=mesh,
        in_specs=(
            P("wide", "narrow"),
            P("wide", "narrow"),
            P("wide", "narrow"),
            P("wide", "narrow"),
            P("wide", None),
            P("wide", "narrow"),
            P("wide", "narrow"),
            P("wide", "narrow"),
            P("wide", "narrow"),
            P("wide", "narrow"),
            P("wide", "narrow"),
            P(None, "narrow"),
            P("narrow"),
            P("narrow"),
            P(),
            P("wide", None),
            P(),
            P("narrow", None),
            P("narrow", None),
            P("narrow", None),
            P("wide", None, "narrow"),
            P("wide", None, "narrow"),
            P("wide", None, "narrow"),
            P("wide", None, "narrow"),
            P("wide", None, "narrow"),
            P("wide", None, "narrow"),
            P("wide", None, "narrow"),
            P("wide", None, "narrow"),
            P("wide", None, "narrow"),
            P("wide", None, "narrow"),
            P("wide", None, "narrow"),
            P("wide", None, "narrow"),
            P("wide", None),
            P("wide", None),
            P(None, "narrow"),
            P(None, "narrow"),
            P("narrow"),
            P("narrow"),
            P("narrow"),
            P("narrow"),
        ),
        out_specs=(
            P("wide", "narrow"),
            P("wide", "narrow"),
            P("wide", "narrow"),
            P("wide", "narrow"),
            P("wide", "narrow"),
            P("wide", "narrow"),
            P("wide", "narrow"),
            P("wide", "narrow"),
            P("wide", "narrow"),
            P("wide", "narrow"),
            P("wide", "narrow"),
            P("wide", "narrow"),
            P("wide", "narrow"),
            P("wide", "narrow"),
            P("wide", "narrow"),
            P("wide", "narrow"),
            P("wide", "narrow"),
            P("wide", "narrow"),
            P("wide", None),
            P("wide", None),
            P("wide", None),
            P("wide", None),
            P(None, "narrow"),
            P(None, "narrow"),
            P(None, "narrow"),
            P(None, "narrow"),
            P("narrow"),
            P("narrow"),
            P("narrow"),
            P("narrow"),
            P("narrow"),
            P("narrow"),
            P("narrow"),
            P("narrow"),
            P("wide", None, "narrow"),
            P("wide", None, "narrow"),
            P("wide", None, "narrow"),
            P("wide", None, "narrow"),
            P("wide", None, "narrow"),
            P("wide", None, "narrow"),
        ),
        check_vma=False,
    )
```

```python
import functools

import jax
import jax.numpy as jnp
from jax import lax
from jax.experimental import pallas as pl
from jax.experimental.pallas import tpu as pltpu
from jax.sharding import PartitionSpec as P

D = 2560
NOPE = 64
ROPE = 32
VH = 64
QR = 768
KVR = 256
SLAB = 64
BASIS = 128


norm_eps = 1e-05
residual_scale = 1.4 / 62**0.5
beta_one = 0.9
beta_two = 0.95
adam_eps = 1e-08
gain_rate = 0.5
masked_value = -1e30
bf16 = jnp.bfloat16
f32 = jnp.float32


def product(left_side, right_side):
    return jnp.dot(left_side, right_side, preferred_element_type=jnp.float32)


def inner_rows(left_side, right_side):
    return lax.dot_general(
        left_side, right_side, (((0,), (0,)), ((), ())), preferred_element_type=jnp.float32
    )


def against_rows(left_side, right_side):
    return lax.dot_general(
        left_side, right_side, (((1,), (1,)), ((), ())), preferred_element_type=jnp.float32
    )


def rope_tables(positions):
    half_width = ROPE // 2
    frequency = 10000.0 ** (-2.0 * jnp.arange(half_width, dtype=jnp.float32) / ROPE)
    angles = positions.astype(jnp.float32)[:, None] * frequency[None, :]
    return (jnp.cos(angles), jnp.sin(angles))


def rotate(block_in, cosine_table, sine_table, direction_sign):
    half_width = block_in.shape[-1] // 2
    lower_half = block_in[..., :half_width]
    upper_half = block_in[..., half_width:]
    signed_sine = direction_sign * sine_table
    return jnp.concatenate(
        [
            lower_half * cosine_table - upper_half * signed_sine,
            upper_half * cosine_table + lower_half * signed_sine,
        ],
        axis=-1,
    )


def plain_adam(gradient, moment, square, step_rate, tcount):
    new_moment = beta_one * moment + (1.0 - beta_one) * gradient
    new_square = beta_two * square + (1.0 - beta_two) * gradient * gradient
    direction = (
        new_moment
        / (1.0 - beta_one**tcount)
        / (jnp.sqrt(new_square / (1.0 - beta_two**tcount)) + adam_eps)
    )
    return (-step_rate * direction, new_moment, new_square)


def shifted(value, step):
    count = lax.axis_size("narrow")
    return lax.ppermute(value, "narrow", [(i, (i + step) % count) for i in range(count)])


def flipped(value, bit):
    count = lax.axis_size("wide")
    return lax.ppermute(value, "wide", [(i, i ^ bit) for i in range(count)])


def along_line(value, pairs):
    return lax.ppermute(value, "narrow", pairs)


pairs_next = [(0, 1), (1, 0), (2, 3), (3, 2)]
pairs_second = [(0, 2), (2, 0), (1, 3), (3, 1)]
pairs_inner = [(1, 2), (2, 1)]
pairs_outward = [(1, 0), (2, 3)]
pairs_inward = [(0, 1), (3, 2)]


def gather_features(features, hold=None):
    count = lax.axis_size("narrow")
    index = lax.axis_index("narrow")
    width = features.shape[1]
    second = along_line(features, pairs_second)
    near = along_line(features, pairs_next)
    inner = along_line(features, pairs_inner)
    if hold is not None:
        second, hold = tie(second, hold)
    outer = along_line(second, pairs_outward)
    third = jnp.where((index == 1) | (index == 2), inner, outer)
    parts = [features, near, second, third]
    places = [index ^ step for step in range(count)]
    joined = jnp.zeros((features.shape[0], count * width), features.dtype)
    for place, part in zip(places, parts):
        joined = lax.dynamic_update_slice(joined, part, (0, place * width))
    return joined if hold is None else (joined, hold)


def line_piece(features, place):
    width = features.shape[1] // lax.axis_size("narrow")
    return lax.dynamic_slice_in_dim(features, place * width, width, 1)


def reduce_start(features):
    index = lax.axis_index("narrow")
    far = line_piece(features, index ^ 3)
    passed = along_line(far, pairs_inward)
    inner = along_line(far, pairs_inner)
    near = along_line(line_piece(features, index ^ 1), pairs_next)
    return passed, inner, near


def reduce_relay(features, passed):
    index = lax.axis_index("narrow")
    return (line_piece(features, index ^ 2).astype(f32) + passed.astype(f32)).astype(bf16)


def reduce_end(features, arrived):
    index = lax.axis_index("narrow")
    total = line_piece(features, index).astype(f32)
    for part in arrived:
        total = total + part.astype(f32)
    return total


def reduce_features(features):
    passed, inner, near = reduce_start(features)
    second = along_line(reduce_relay(features, passed), pairs_second)
    return reduce_end(features, (inner, near, second))


def gather_small(values):
    count = lax.axis_size("narrow")
    index = lax.axis_index("narrow")
    joined = jnp.zeros((count, values.shape[0]), values.dtype)
    for step in range(count):
        part = shifted(values, step) if step else values
        joined = lax.dynamic_update_slice(joined, part[None], ((index - step) % count, 0))
    return joined


def tie(*values):
    return lax.optimization_barrier(values)


def wide_totals(values):
    bit = 1
    while bit < lax.axis_size("wide"):
        values = values + flipped(values, bit)
        bit *= 2
    return values


def row_parts(values):
    return [values] + [shifted(values, step) for step in range(1, lax.axis_size("narrow"))]


def row_totals(values):
    count = lax.axis_size("narrow")
    return values + sum(shifted(values, step) for step in range(1, count))


def halving_orders(count):
    bits = list(range(1, count.bit_length() - 1))
    middle = len(bits) // 2
    return [bits, bits[middle:] + bits[:middle]]


def chunk_rows(features):
    count = lax.axis_size("wide")
    tokens, width = features.shape
    places = []
    for core in (1, 0):
        for half, order in enumerate(halving_orders(count)):
            chunks = [core]
            for bit in reversed(order):
                chunks = chunks + [chunk | (1 << bit) for chunk in chunks]
            places.append([(chunk, half) for chunk in chunks])
    chunks = jnp.array([chunk for group in places for chunk, _ in group], jnp.int32)
    halves = jnp.array([half for group in places for _, half in group], jnp.int32)
    pieces = features.T.reshape(2 * count, width // (2 * count), tokens)
    order = 2 * (lax.axis_index("wide") ^ chunks) + halves
    rows = jnp.take(pieces, order, axis=0, mode="clip").reshape(width, tokens)
    return rows[: width // 2], rows[width // 2 :]


def halves_of(rows):
    half = rows.shape[0] // 2
    return rows[:half], rows[half:]


def summed(values):
    total = values[0].astype(f32)
    for value in values[1:]:
        total = total + value.astype(f32)
    return total


def add_kernel(sizes, rows, *refs):
    outs = refs[sum(sizes) :]
    begin = 0
    for group, size in enumerate(sizes):
        columns = outs[0].shape[1]
        total = summed([ref[:, :columns] for ref in refs[begin : begin + size]])
        begin += size
        if len(outs) == 1:
            outs[0][group * rows : (group + 1) * rows, :] = total.astype(outs[0].dtype)
        else:
            outs[group][...] = total.astype(outs[group].dtype)


def add_rows(groups, place, rows, joined, kept):
    columns = groups[0][0].shape[1]
    start = place * rows
    if rows % 16:
        totals = [summed([part[start : start + rows] for part in parts]) for parts in groups]
        if joined:
            return jnp.concatenate(totals, axis=0)[:, :kept]
        return [total.astype(bf16) for total in totals]
    steps = 1 if joined or rows % 32 else 2
    block = rows // steps
    source = pl.BlockSpec((block, columns), lambda step: (place * steps + step, 0))
    if joined:
        out_specs = [pl.BlockSpec((len(groups) * rows, kept), lambda step: (0, 0))]
        out_shape = [jax.ShapeDtypeStruct((len(groups) * rows, kept), f32)]
    else:
        out_specs = [pl.BlockSpec((block, columns), lambda step: (step, 0))] * len(groups)
        out_shape = [jax.ShapeDtypeStruct((rows, columns), bf16)] * len(groups)
    outs = pl.pallas_call(
        functools.partial(add_kernel, [len(parts) for parts in groups], block),
        grid=(steps,),
        in_specs=[source] * sum(len(parts) for parts in groups),
        out_specs=out_specs,
        out_shape=out_shape,
        compiler_params=pltpu.CompilerParams(vmem_limit_bytes=48 * 1024 * 1024),
    )(*[part for parts in groups for part in parts])
    return outs[0] if joined else list(outs)


class Scatter:
    def __init__(self, products):
        near, away = products[:2], products[2:]
        self.orders = halving_orders(lax.axis_size("wide"))
        self.parts = [[own, flipped(sent, 1)] for own, sent in zip(near, away)]
        self.rows = near[0].shape[0]
        self.stage = 0

    def outgoing(self):
        return add_rows(self.parts, 1, self.rows // 2, False, None)

    def send(self, sending):
        for at, value in enumerate(sending):
            bit = 1 << self.orders[at][self.stage]
            self.parts[at] = self.parts[at] + [flipped(value, bit)]
        self.rows //= 2
        self.stage += 1

    def step(self):
        self.send(self.outgoing())

    def finish(self, kept):
        while self.stage < len(self.orders[0]):
            self.step()
        return add_rows(self.parts, 0, self.rows, True, kept)


def chunk_kernel(order_ref, left_ref, right_ref, near_a, near_b, away_a, away_b, whole_ref):
    core = order_ref[2 * pl.num_programs(0)]
    rows = near_a.shape[0]
    whole_ref[...] = inner_rows(left_ref[...], right_ref[...])
    near = pl.multiple_of(core * 2 * rows, 2 * rows)
    away = pl.multiple_of((1 - core) * 2 * rows, 2 * rows)
    columns = whole_ref.shape[1]
    for out, start in ((near_a, near), (near_b, near + rows), (away_a, away), (away_b, away + rows)):
        out[:, :columns] = whole_ref[pl.ds(start, rows), :].astype(bf16)
        if out.shape[1] > columns:
            out[:, columns:] = jnp.zeros((rows, out.shape[1] - columns), bf16)


def chunk_places(count):
    table = []
    for order in halving_orders(count):
        chips = [0]
        for bit in reversed(order):
            chips = chips + [chip | (1 << (bit - 1)) for chip in chips]
        table.append([chips.index(chip) for chip in range(count // 2)])
    return table


def chunk_products(left, right):
    count = lax.axis_size("wide")
    tokens, width = left.shape
    columns = right.shape[1]
    chips = count // 2
    group = width // chips
    rows = group // 4
    if group % 128 or rows % 16:
        away, near = [product(part, right).astype(bf16) for part in chunk_rows(left)]
        return [*halves_of(near), *halves_of(away)]
    index = lax.axis_index("wide")
    relative = (index // 2) ^ jnp.arange(chips, dtype=jnp.int32)
    order = jnp.concatenate(
        [jnp.array(table, jnp.int32)[relative] for table in chunk_places(count)]
        + [(index % 2)[None]]
    ).astype(jnp.int32)
    padded = -(-columns // 128) * 128
    first = pl.BlockSpec((rows, padded), lambda step, at: (at[step], 0))
    last = pl.BlockSpec((rows, padded), lambda step, at: (at[pl.num_programs(0) + step], 0))
    return list(
        pl.pallas_call(
            chunk_kernel,
            grid_spec=pltpu.PrefetchScalarGridSpec(
                num_scalar_prefetch=1,
                grid=(chips,),
                in_specs=[
                    pl.BlockSpec((tokens, group), lambda step, at: (0, step)),
                    pl.BlockSpec((tokens, columns), lambda step, at: (0, 0)),
                ],
                out_specs=[first, last, first, last],
                scratch_shapes=[pltpu.VMEM((group, columns), f32)],
            ),
            out_shape=[jax.ShapeDtypeStruct((chips * rows, padded), bf16)] * 4,
            compiler_params=pltpu.CompilerParams(vmem_limit_bytes=48 * 1024 * 1024),
        )(order, left, right)
    )


def pack_kernel(send_ref, *refs):
    count = len(refs) - 3
    blocks, outs, turned = refs[:count], refs[count : count + 2], refs[-1]
    begin = 0
    for block in blocks:
        width = block.shape[1]
        turned[begin : begin + width, :] = block[...].T.astype(bf16)
        begin += width
    capacity = outs[0].shape[1] + outs[1].shape[1]
    for out, offset in zip(outs, (0, outs[0].shape[1])):
        slots = out.shape[1]

        def place(step, carry, out=out, offset=offset, slots=slots):
            owner = step // slots
            slot = step % slots
            unit = send_ref[owner * capacity + offset + slot]
            out[owner, slot] = turned[pl.ds(pl.multiple_of(unit * SLAB, SLAB), SLAB), :]
            return carry

        lax.fori_loop(0, out.shape[0] * slots, place, 0)


def pack_units(send, blocks, count, sizes):
    rows = blocks[0].shape[0]
    total = sum(block.shape[1] for block in blocks)
    vmem = pl.BlockSpec(memory_space=pltpu.VMEM)
    return pl.pallas_call(
        pack_kernel,
        in_specs=[pl.BlockSpec(memory_space=pltpu.SMEM)] + [vmem] * len(blocks),
        out_specs=[vmem] * 2,
        out_shape=[jax.ShapeDtypeStruct((count, size, SLAB, rows), bf16) for size in sizes],
        scratch_shapes=[pltpu.VMEM((total, rows), bf16)],
        compiler_params=pltpu.CompilerParams(vmem_limit_bytes=56 * 1024 * 1024),
    )(send, *blocks)


def unpack_kernel(back_ref, first_ref, last_ref, *refs):
    count = (len(refs) - 1) // 2
    weights, outs, turned = refs[:count], refs[count : 2 * count], refs[-1]
    first = first_ref.shape[1]
    capacity = first + last_ref.shape[1]

    def place(unit, carry):
        slot = back_ref[unit]
        owner = slot // capacity
        at = slot % capacity
        rows = pl.ds(pl.multiple_of(unit * SLAB, SLAB), SLAB)

        @pl.when(at < first)
        def _():
            turned[rows, :] = first_ref[owner, at]

        @pl.when(at >= first)
        def _():
            turned[rows, :] = last_ref[owner, at - first]

        return carry

    lax.fori_loop(0, turned.shape[0] // SLAB, place, 0)
    begin = 0
    for weight, out in zip(weights, outs):
        width = out.shape[1]
        steps = turned[begin : begin + width, :].astype(f32).T
        out[...] = weight[...].astype(f32) + steps
        begin += width


def unpack_units(back, first, last, weights):
    rows = first.shape[3]
    total = sum(weight.shape[1] for weight in weights)
    vmem = pl.BlockSpec(memory_space=pltpu.VMEM)
    return pl.pallas_call(
        unpack_kernel,
        in_specs=[pl.BlockSpec(memory_space=pltpu.SMEM)] + [vmem] * (2 + len(weights)),
        out_specs=[vmem] * len(weights),
        out_shape=[jax.ShapeDtypeStruct(weight.shape, f32) for weight in weights],
        scratch_shapes=[pltpu.VMEM((total, rows), bf16)],
        compiler_params=pltpu.CompilerParams(vmem_limit_bytes=56 * 1024 * 1024),
    )(back, first, last, *weights)


def unit_rates(col_widths, rates):
    return jnp.concatenate(
        [
            jnp.full((col_width // SLAB,), step_rate, jnp.float32)
            for col_width, step_rate in zip(col_widths, rates)
        ]
    )


def rotated_step(gradient, left_ref, right_ref, moment_ref, square_ref, new_moment_ref,
                 new_square_ref, turned_ref, occupied, first_scale, second_scale):
    blocks = left_ref.shape[1] // BASIS
    right_basis = right_ref[0].astype(bf16)
    turned_ref[...] = lax.dot_general(
        right_basis, gradient, (((0,), (0,)), ((), ())), preferred_element_type=f32
    )
    for block in range(blocks):
        at = slice(block * BASIS, (block + 1) * BASIS)
        left_basis = left_ref[0, at, :].astype(bf16)
        turned = jnp.dot(turned_ref[:, at].astype(bf16), left_basis, preferred_element_type=f32)
        moment = moment_ref[0, :, at]
        square = square_ref[0, :, at]
        new_moment = beta_one * moment + (1.0 - beta_one) * turned
        new_square = beta_two * square + (1.0 - beta_two) * turned * turned
        new_moment_ref[0, :, at] = jnp.where(occupied > 0.5, new_moment, moment)
        new_square_ref[0, :, at] = jnp.where(occupied > 0.5, new_square, square)
        direction = new_moment * first_scale / (jnp.sqrt(new_square * second_scale) + adam_eps)
        turned_ref[:, at] = lax.dot_general(
            direction.astype(bf16), left_basis, (((1,), (1,)), ((), ())),
            preferred_element_type=f32,
        )
    return jnp.dot(right_basis, turned_ref[...].astype(bf16), preferred_element_type=f32)


def slot_kernel(place_ref, scale_ref, gradient_ref, left_ref, right_ref, moment_ref, square_ref,
                change_ref, new_moment_ref, new_square_ref, whole_ref, turned_ref):
    step = pl.program_id(0)
    steps = pl.num_programs(0)
    sources, rows = gradient_ref.shape[0], gradient_ref.shape[3]
    rate = scale_ref[step]
    occupied = scale_ref[steps + step]

    @pl.when(occupied > 0.5)
    def _():
        for source in range(sources):
            whole_ref[:, source * rows : (source + 1) * rows] = gradient_ref[source, 0].astype(f32)
        whole_ref[...] = rate * rotated_step(
            whole_ref[...].astype(bf16), left_ref, right_ref, moment_ref, square_ref,
            new_moment_ref, new_square_ref, turned_ref, occupied,
            scale_ref[2 * steps], scale_ref[2 * steps + 1],
        )
        for source in range(sources):
            change_ref[source, 0] = whole_ref[:, source * rows : (source + 1) * rows].astype(bf16)

    @pl.when(occupied <= 0.5)
    def _():
        change_ref[...] = jnp.zeros_like(change_ref)

    @pl.when(jnp.logical_and(occupied <= 0.5, place_ref[steps + step] > 0))
    def _():
        new_moment_ref[...] = moment_ref[...]
        new_square_ref[...] = square_ref[...]


def slot_call(places, scales, gradient, left_basis, right_basis, moment, square, written):
    sources, steps, _, rows = gradient.shape
    row_count = sources * rows
    moment = moment.transpose(0, 2, 1)
    square = square.transpose(0, 2, 1)
    state = pl.BlockSpec((1, SLAB, row_count), lambda step, place: (place[step], 0, 0))
    traded = pl.BlockSpec((sources, 1, SLAB, rows), lambda step, place: (0, step, 0, 0))
    operands = [places, scales, gradient, left_basis, right_basis, moment, square]
    in_specs = [
        pl.BlockSpec(memory_space=pltpu.SMEM),
        traded,
        pl.BlockSpec((1, row_count, BASIS), lambda step, place: (place[step], 0, 0)),
        pl.BlockSpec((1, SLAB, SLAB), lambda step, place: (place[step], 0, 0)),
        state,
        state,
    ]
    aliases = {}
    kernel = slot_kernel
    if written == "same":
        aliases = {5: 1, 6: 2}
    elif written is not None:
        operands += [value.transpose(0, 2, 1) for value in written]
        in_specs += [pl.BlockSpec(memory_space=pl.ANY)] * 2
        aliases = {7: 1, 8: 2}

        def kernel(*refs):
            slot_kernel(*refs[:7], *refs[9:])

    change, new_moment, new_square = pl.pallas_call(
        kernel,
        grid_spec=pltpu.PrefetchScalarGridSpec(
            num_scalar_prefetch=1,
            grid=(steps,),
            in_specs=in_specs,
            out_specs=[traded, state, state],
            scratch_shapes=[
                pltpu.VMEM((SLAB, row_count), f32),
                pltpu.VMEM((SLAB, row_count), f32),
            ],
        ),
        out_shape=[
            jax.ShapeDtypeStruct(gradient.shape, bf16),
            jax.ShapeDtypeStruct(moment.shape, f32),
            jax.ShapeDtypeStruct(square.shape, f32),
        ],
        input_output_aliases=aliases,
        compiler_params=pltpu.CompilerParams(vmem_limit_bytes=48 * 1024 * 1024),
    )(*operands)
    return change, new_moment.transpose(0, 2, 1), new_square.transpose(0, 2, 1)


def slot_group(scales, gradient, left_basis, right_basis, moment, square, group, written):
    capacity = moment.shape[0]
    count = group.stop - group.start
    places = jnp.concatenate(
        [
            jnp.arange(group.start, group.stop, dtype=jnp.int32),
            jnp.ones((count,), jnp.int32),
        ]
    )
    scales = jnp.concatenate(
        [
            scales[group],
            scales[capacity + group.start : capacity + group.stop],
            scales[2 * capacity :],
        ]
    )
    return slot_call(places, scales, gradient, left_basis, right_basis, moment, square, written)


def all_slots(scales, gradient, left_basis, right_basis, moment, square):
    group = slice(0, moment.shape[0])
    return slot_group(
        scales, gradient, left_basis, right_basis, moment, square, group, None
    )


def late_steps(places, scales, gradient, left_basis, right_basis, moment, square):
    return slot_call(places, scales, gradient, left_basis, right_basis, moment, square, "same")


def correction_scales(tcount):
    return jnp.stack([1.0 / (1.0 - beta_one**tcount), 1.0 / (1.0 - beta_two**tcount)])


def slot_scales(owners, rates, capacity, wide_index, tcount):
    slot_ids = wide_index * capacity + jnp.arange(capacity, dtype=jnp.int32)
    own = (owners[None, :] == slot_ids[:, None]).astype(f32)
    return jnp.concatenate(
        [
            -jnp.sum(own * rates[None, :], axis=1),
            jnp.sum(own, axis=1),
            correction_scales(tcount),
        ]
    )


def ranks_within(owners, capacity):
    device = owners // capacity
    units = owners.shape[0]
    earlier = jnp.arange(units)[None, :] < jnp.arange(units)[:, None]
    return jnp.sum(
        jnp.where(earlier & (device[None, :] == device[:, None]), 1, 0).astype(jnp.int32), axis=1
    )


def routes(owners, capacity, room, wide_count):
    units = owners.shape[0]
    if room == capacity:
        places = owners
    else:
        places = owners // capacity * room + ranks_within(owners, capacity)
    slots = jnp.arange(wide_count * room, dtype=jnp.int32)
    matches = slots[:, None] == places[None, :]
    unit_of = jnp.sum(
        jnp.where(matches, jnp.arange(units, dtype=jnp.int32)[None, :], 0), axis=1
    )
    return jnp.minimum(unit_of, units - 1), places


def late_places(owners, rates, capacity, room, wide_index, tcount):
    ranks = ranks_within(owners, capacity)
    mine = owners // capacity == wide_index
    own = mine[None, :] & (ranks[None, :] == jnp.arange(room, dtype=jnp.int32)[:, None])
    slot = jnp.sum(jnp.where(own, (owners % capacity)[None, :], 0), axis=1)
    filled = jnp.sum(own.astype(jnp.int32), axis=1)
    last = jnp.maximum(jnp.sum(filled) - 1, 0)
    last_slot = jnp.sum(jnp.where(jnp.arange(room) == last, slot, 0))
    places = jnp.where(filled > 0, slot, last_slot)
    untouched = jnp.where((jnp.arange(room) == 0) & (filled == 0), 1, 0)
    scales = jnp.concatenate(
        [
            -jnp.sum(own.astype(f32) * rates[None, :], axis=1),
            filled.astype(f32),
            correction_scales(tcount),
        ]
    )
    return jnp.concatenate([places, untouched]).astype(jnp.int32), scales


def unit_rows(blocks):
    joined = jnp.concatenate([block.T for block in blocks], axis=0).astype(bf16)
    return joined.reshape(-1, SLAB, joined.shape[1])


def unit_columns(units, blocks):
    joined = units.reshape(-1, units.shape[2])
    pieces, begin = ([], 0)
    for block in blocks:
        pieces.append(joined[begin : begin + block.shape[1]].T.astype(f32))
        begin += block.shape[1]
    return pieces


def trade_joined(parts, count):
    steps = [part.shape[0] // count for part in parts]
    widths = [part.shape[2] for part in parts]
    room = max(steps)
    joined = jnp.concatenate(
        [
            jnp.pad(
                part.reshape(count, own, SLAB, width), ((0, 0), (0, room - own), (0, 0), (0, 0))
            )
            for part, own, width in zip(parts, steps, widths)
        ],
        axis=3,
    )
    traded = lax.all_to_all(joined, "wide", split_axis=0, concat_axis=0, tiled=True)
    pieces, begin = ([], 0)
    for own, width in zip(steps, widths):
        pieces.append(traded[:, :own, :, begin : begin + width])
        begin += width
    return pieces


def body(
    x_in,
    grad_out,
    w_qa,
    w_kv,
    w_kr,
    w_qb,
    w_kvb,
    w_o,
    w_gate,
    w_up,
    w_down,
    norm_gains,
    q_gain,
    kv_gain,
    deal,
    lengths,
    step_count,
    owner_a,
    owner_b,
    owner_c,
    basis_la,
    basis_ra,
    basis_lb,
    basis_rb,
    basis_lc,
    basis_rc,
    mom_a,
    sq_a,
    mom_b,
    sq_b,
    mom_c,
    sq_c,
    kr_mom,
    kr_sq,
    gain_mom,
    gain_sq,
    qgain_mom,
    qgain_sq,
    kvgain_mom,
    kvgain_sq,
):
    wide_count = lax.axis_size("wide")
    wide_index = lax.axis_index("wide")
    narrow_index = lax.axis_index("narrow")
    row_count, local_width = x_in.shape
    piece_rows = row_count // wide_count
    deal_row = lax.dynamic_index_in_dim(deal, wide_index, 0, keepdims=False)
    wide_ids = jnp.arange(wide_count, dtype=jnp.int32)
    inverse = jnp.sum(
        jnp.where(deal_row[None, :] == wide_ids[:, None], wide_ids[None, :], 0), axis=1
    )

    def to_working(features):
        outgoing = jnp.take(
            features.reshape((wide_count, piece_rows) + features.shape[1:]), inverse, axis=0,
            mode="clip",
        )
        dealt = lax.all_to_all(outgoing, "wide", split_axis=0, concat_axis=0, tiled=True)
        return dealt.reshape(row_count, -1)

    token_in = to_working(x_in)
    residual = token_in.astype(f32)
    seq_lengths = lengths[0]
    seq_ends = jnp.cumsum(seq_lengths)
    row_ids = jnp.arange(row_count, dtype=jnp.int32)
    segment = jnp.sum((row_ids[:, None] >= seq_ends[None, :-1]).astype(jnp.int32), axis=1)
    pick = jnp.arange(seq_lengths.shape[0], dtype=jnp.int32)[None, :] == segment[:, None]
    seq_start = jnp.sum(jnp.where(pick, (seq_ends - seq_lengths)[None, :], 0), axis=1)
    live_rows = (segment < seq_lengths.shape[0] - 1).astype(f32)[:, None]
    cosine_table, sine_table = rope_tables(row_ids - seq_start)
    cos_heads = cosine_table[:, None, :]
    sin_heads = sine_table[:, None, :]

    latent_own = jnp.concatenate([w_qa, w_kv, w_kr], axis=1)
    head_rows = jnp.concatenate(
        [jnp.pad(w_qb, ((0, 0), (0, w_kvb.shape[1] - w_qb.shape[1]))), w_kvb], axis=0
    )
    full_latent = lax.all_gather(latent_own, "wide", axis=0, tiled=True)
    full_heads = lax.all_gather(head_rows, "wide", axis=0)
    full_qb = full_heads[:, : w_qb.shape[0], : w_qb.shape[1]].reshape(-1, w_qb.shape[1])
    full_kvb = full_heads[:, w_qb.shape[0] :, :].reshape(-1, w_kvb.shape[1])
    full_o = lax.all_gather(w_o, "wide", axis=0, tiled=True)
    full_gate = lax.all_gather(w_gate, "wide", axis=0, tiled=True)
    full_up = lax.all_gather(w_up, "wide", axis=0, tiled=True)
    full_down = lax.all_gather(w_down, "wide", axis=0, tiled=True)
    gains_all = gather_small(jnp.concatenate([norm_gains[0], norm_gains[1], q_gain, kv_gain]))
    first_gain = gains_all[:, :local_width].reshape(1, -1)
    second_gain = gains_all[:, local_width : 2 * local_width].reshape(1, -1)
    q_width = q_gain.shape[0]
    kv_width = kv_gain.shape[0]
    q_gain_all = gains_all[:, 2 * local_width : 2 * local_width + q_width].reshape(1, -1)
    kv_gain_all = gains_all[:, 2 * local_width + q_width :].reshape(1, -1)

    def inverse_rms(features, width):
        wide = features.astype(f32)
        return lax.rsqrt(jnp.sum(wide * wide, axis=1, keepdims=True) / width + norm_eps)

    token_all = gather_features(token_in)
    inv_first = inverse_rms(token_all, D)
    normed = (token_all.astype(f32) * inv_first * first_gain).astype(bf16)
    latents = product(normed, full_latent)
    q_latent = latents[:, :q_width]
    kv_latent = latents[:, q_width : q_width + kv_width]
    key_rot = latents[:, q_width + kv_width :]
    narrow_count = lax.axis_size("narrow")
    latents_all = gather_features(latents[:, : q_width + kv_width].astype(bf16))
    latents_all, grad_out = tie(latents_all, grad_out)
    latents_all = latents_all.reshape(row_count, narrow_count, q_width + kv_width)
    q_latent_all = latents_all[:, :, :q_width].reshape(row_count, QR).astype(f32)
    kv_latent_all = latents_all[:, :, q_width:].reshape(row_count, KVR).astype(f32)
    inv_q = inverse_rms(q_latent_all, QR)
    inv_kv = inverse_rms(kv_latent_all, KVR)
    q_normed = (q_latent_all * inv_q * q_gain_all).astype(bf16)
    kv_normed = (kv_latent_all * inv_kv * kv_gain_all).astype(bf16)
    heads_here = w_o.shape[1] // VH
    q_pre = product(q_normed, full_qb)
    kv_pre = product(kv_normed, full_kvb)
    q_pre_heads = q_pre.reshape(row_count, heads_here, NOPE + ROPE)
    kv_pre_heads = kv_pre.reshape(row_count, heads_here, NOPE + VH)
    queries = jnp.concatenate(
        [
            q_pre_heads[..., :NOPE],
            rotate(q_pre_heads[..., NOPE:], cos_heads, sin_heads, 1.0),
        ],
        axis=-1,
    ).astype(bf16)
    key_turned = rotate(key_rot, cosine_table, sine_table, 1.0)
    key_heads = jnp.concatenate(
        [
            kv_pre_heads[..., :NOPE],
            jnp.broadcast_to(key_turned[:, None, :], (row_count, heads_here, ROPE)),
        ],
        axis=-1,
    ).astype(bf16)
    values = kv_pre_heads[..., NOPE:].astype(bf16)
    score_scale = (NOPE + ROPE) ** (-0.5)
    allowed = (segment[:, None] == segment[None, :]) & (row_ids[None, :] <= row_ids[:, None])

    def all_scores():
        scores = (
            jnp.einsum("qhd,khd->hqk", queries, key_heads, preferred_element_type=f32)
            * score_scale
        )
        return jnp.where(allowed[None], scores, masked_value)

    scores = all_scores()
    row_max = jnp.max(scores, axis=-1, keepdims=True)
    grad_all, row_max = gather_features(grad_out, row_max)
    token_grad_all = to_working(grad_all)
    grad_top = lax.dynamic_slice_in_dim(
        token_grad_all, narrow_index * local_width, local_width, 1
    ).astype(f32)
    exp_scores = jnp.exp(scores - row_max)
    row_total = jnp.sum(exp_scores, axis=-1, keepdims=True)
    prob_rows = (exp_scores / row_total).astype(bf16)
    heads_out = jnp.einsum("hqk,khd->qhd", prob_rows, values, preferred_element_type=f32)
    mlp_grad = (residual_scale * live_rows * token_grad_all.astype(f32)).astype(bf16)
    heads_out = heads_out.astype(bf16).reshape(row_count, heads_here * VH)
    log_totals = row_max + jnp.log(row_total)
    attn_out = reduce_features(against_rows(heads_out, full_o).astype(bf16))
    middle = residual + residual_scale * live_rows * attn_out
    middle_all = gather_features(middle.astype(bf16)).astype(f32)
    inv_second = inverse_rms(middle_all, D)
    normed_two = (middle_all * inv_second * second_gain).astype(bf16)
    gate_act = product(normed_two, full_gate)
    upward = product(normed_two, full_up)
    sigmoid_gate = jax.nn.sigmoid(gate_act)
    silu_gate = gate_act * sigmoid_gate
    active = (silu_gate * upward).astype(bf16)
    mlp_part = against_rows(active, full_down).astype(bf16)
    mlp_passed, mlp_inner, mlp_near = reduce_start(mlp_part)
    down_products = chunk_products(mlp_grad, active)
    active_grad = product(mlp_grad, full_down)
    gate_grad = (
        active_grad * upward * (sigmoid_gate + silu_gate * (1.0 - sigmoid_gate))
    ).astype(bf16)
    up_grad = (active_grad * silu_gate).astype(bf16)
    gate_grad, up_grad, down_products = tie(gate_grad, up_grad, down_products)
    down_sum = Scatter(down_products)
    normed_two_part = (
        against_rows(gate_grad, full_gate) + against_rows(up_grad, full_up)
    ).astype(bf16)
    second_dot = jnp.sum(gate_grad.astype(f32) * gate_act + up_grad.astype(f32) * upward, axis=1)
    passed, inner, near = reduce_start(normed_two_part)
    gate_products = chunk_products(normed_two, gate_grad)
    passed, gate_products, up_grad = tie(passed, gate_products, up_grad)
    gate_sum = Scatter(gate_products)
    relayed = reduce_relay(normed_two_part, passed)
    relayed, up_grad = tie(relayed, up_grad)
    second = along_line(relayed, pairs_second)
    up_sum = Scatter(chunk_products(normed_two, up_grad))
    second_dot, up_sum.parts = tie(second_dot, up_sum.parts)
    second_dot = row_parts(second_dot)
    second, down_sending, gate_sending, up_sum.parts = tie(
        second, down_sum.outgoing(), gate_sum.outgoing(), up_sum.parts
    )
    second_dot = sum(second_dot)[:, None]
    down_sum.send(down_sending)
    gate_sum.send(gate_sending)
    normed_two_grad = reduce_end(normed_two_part, (inner, near, second))
    post_gain_grad = jnp.sum(normed_two_grad * middle * inv_second, axis=0)
    middle_grad = (
        grad_top
        + inv_second * norm_gains[1] * normed_two_grad
        - middle * inv_second**2 * second_dot / D
    )
    attn_grad = gather_features((residual_scale * live_rows * middle_grad).astype(bf16))
    up_sum.step()
    attn_grad, down_sending, gate_sending = tie(
        attn_grad, down_sum.outgoing(), gate_sum.outgoing()
    )
    down_sum.send(down_sending)
    gate_sum.send(gate_sending)
    o_products = chunk_products(attn_grad, heads_out)
    attn_grad, o_products, up_sending = tie(attn_grad, o_products, up_sum.outgoing())
    up_sum.send(up_sending)
    mlp_passed, attn_grad = tie(mlp_passed, attn_grad)
    mlp_second = along_line(reduce_relay(mlp_part, mlp_passed), pairs_second)
    o_sum = Scatter(o_products)
    heads_grad = product(attn_grad, full_o).astype(bf16).reshape(row_count, heads_here, VH)

    prob_rows = jnp.exp(all_scores() - log_totals)
    value_grad = jnp.einsum(
        "hqk,qhd->khd", prob_rows.astype(bf16), heads_grad, preferred_element_type=f32
    )
    prob_grad = jnp.einsum("qhd,khd->hqk", heads_grad, values, preferred_element_type=f32)
    delta_rows = jnp.sum(prob_rows * prob_grad, axis=-1, keepdims=True)
    delta_rows, o_sending = tie(delta_rows, o_sum.outgoing())
    o_sum.send(o_sending)
    score_grad = (prob_rows * (prob_grad - delta_rows)).astype(bf16)
    query_grad = score_scale * jnp.einsum(
        "hqk,khd->qhd", score_grad, key_heads, preferred_element_type=f32
    )
    key_grad = score_scale * jnp.einsum(
        "hqk,qhd->khd", score_grad, queries, preferred_element_type=f32
    )
    mlp_arrived = (mlp_inner, mlp_near, mlp_second)
    query_grad, o_sending = tie(query_grad, o_sum.outgoing())
    o_sum.send(o_sending)
    query_grad, key_grad, value_grad, mlp_arrived = tie(
        query_grad, key_grad, value_grad, mlp_arrived
    )
    mlp_out = reduce_end(mlp_part, mlp_arrived)
    layer_out = middle + residual_scale * live_rows * mlp_out
    q_pre_grad = jnp.concatenate(
        [query_grad[..., :NOPE], rotate(query_grad[..., NOPE:], cos_heads, sin_heads, -1.0)],
        axis=-1,
    )
    q_pre_grad = q_pre_grad.reshape(row_count, -1).astype(bf16)
    kv_pre_grad = jnp.concatenate([key_grad[..., :NOPE], value_grad], axis=-1)
    kv_pre_grad = kv_pre_grad.reshape(row_count, -1).astype(bf16)
    rot_partial = rotate(jnp.sum(key_grad[..., NOPE:], axis=1), cosine_table, sine_table, -1.0)
    q_dot = jnp.sum(q_pre_grad.astype(f32) * q_pre, axis=1)
    kv_dot = jnp.sum(kv_pre_grad.astype(f32) * kv_pre, axis=1)
    dots = row_parts(jnp.concatenate([jnp.stack([q_dot, kv_dot]), rot_partial.T], axis=0))
    q_part = against_rows(q_pre_grad, full_qb).astype(bf16)
    kv_part = against_rows(kv_pre_grad, full_kvb).astype(bf16)
    both_part = jnp.concatenate(
        [
            q_part.reshape(row_count, narrow_count, q_width),
            kv_part.reshape(row_count, narrow_count, kv_width),
        ],
        axis=-1,
    ).reshape(row_count, -1)
    passed, inner, near = reduce_start(both_part)
    extra = kv_pre_grad.shape[1] - q_pre_grad.shape[1]
    tcount = step_count[0].astype(f32)
    wide_rate = D ** (-0.5)
    block_down = down_sum.finish(w_down.shape[1])
    block_gate = gate_sum.finish(w_gate.shape[1])
    block_up = up_sum.finish(w_up.shape[1])
    block_o = o_sum.finish(w_o.shape[1])
    passed, q_pre_late, kv_pre_late, block_down, block_gate, block_up = tie(
        passed, q_pre_grad, kv_pre_grad, block_down, block_gate, block_up
    )
    main_blocks = [block_o, block_gate, block_up, block_down]
    late_blocks_widths = [q_width, kv_width]
    late_units = sum(late_blocks_widths) // SLAB
    main_rates = unit_rates(
        [block.shape[1] for block in main_blocks], [1.0, wide_rate, wide_rate, 0.125]
    )
    late_rates = unit_rates(late_blocks_widths, [wide_rate, wide_rate])
    late_owners, main_owners = owner_a[0, :late_units], owner_a[0, late_units:]
    capacity_a = mom_a.shape[0]
    main_send, main_back = routes(main_owners, capacity_a, capacity_a, wide_count)
    main_scales = slot_scales(main_owners, main_rates, capacity_a, wide_index, tcount)
    first_slots = (capacity_a + 1) // 2
    groups = [slice(0, first_slots), slice(first_slots, capacity_a)]
    main_sent = pack_units(
        main_send, main_blocks, wide_count, [group.stop - group.start for group in groups]
    )
    second = along_line(reduce_relay(both_part, passed), pairs_second)
    head_columns = w_kvb.shape[1]
    chips = wide_count // 2
    head_products = [
        jnp.concatenate(
            [
                jnp.pad(first, ((0, 0), (0, extra))).reshape(chips, -1, head_columns),
                last.reshape(chips, -1, head_columns),
            ],
            axis=1,
        ).reshape(-1, head_columns)
        for first, last in zip(
            chunk_products(q_normed, q_pre_late), chunk_products(kv_normed, kv_pre_late)
        )
    ]
    second, dots, main_sent, head_products = tie(second, dots, main_sent, head_products)
    main_owned = [
        lax.all_to_all(part, "wide", split_axis=0, concat_axis=0, tiled=True)
        for part in main_sent
    ]
    dots = sum(dots).T
    q_dot, kv_dot = dots[:, :1], dots[:, 1:2]
    rot_grad = dots[:, 2:].astype(bf16)
    heads_sum = Scatter(head_products)
    both_grad = reduce_end(both_part, (inner, near, second))
    q_normed_grad = both_grad[:, :q_width]
    kv_normed_grad = both_grad[:, q_width:]
    q_gain_grad = jnp.sum(q_normed_grad * q_latent * inv_q, axis=0)
    kv_gain_grad = jnp.sum(kv_normed_grad * kv_latent * inv_kv, axis=0)
    q_latent_grad = (
        inv_q * q_gain * q_normed_grad - q_latent * inv_q**2 * q_dot / QR
    ).astype(bf16)
    kv_latent_grad = (
        inv_kv * kv_gain * kv_normed_grad - kv_latent * inv_kv**2 * kv_dot / KVR
    ).astype(bf16)
    share = (narrow_index == 0).astype(f32)
    first_dot = row_totals(
        jnp.sum(q_latent_grad.astype(f32) * q_latent, axis=1)
        + jnp.sum(kv_latent_grad.astype(f32) * kv_latent, axis=1)
        + share * jnp.sum(rot_grad.astype(f32) * key_rot, axis=1)
    )[:, None]
    latent_grad = jnp.concatenate([q_latent_grad, kv_latent_grad, rot_grad], axis=1)
    full_kr = full_latent[:, q_width + kv_width :]
    own_kr = lax.dynamic_slice_in_dim(full_kr, narrow_index * local_width, local_width, 0)
    normed_part = against_rows(
        latent_grad[:, : q_width + kv_width], full_latent[:, : q_width + kv_width]
    ).astype(bf16)
    normed_passed, normed_inner, normed_near = reduce_start(normed_part)
    latent_sum = Scatter(chunk_products(normed, latent_grad))
    head_sending = heads_sum.outgoing()
    latent_sum.parts, head_sending = tie(latent_sum.parts, head_sending)
    heads_sum.send(head_sending)
    normed_passed, latent_sending = tie(normed_passed, latent_sum.outgoing())
    latent_sum.send(latent_sending)
    normed_second = along_line(reduce_relay(normed_part, normed_passed), pairs_second)
    head_sending, latent_sending = heads_sum.outgoing(), latent_sum.outgoing()
    normed_second, head_sending, latent_sending = tie(
        normed_second, head_sending, latent_sending
    )
    heads_sum.send(head_sending)
    latent_sum.send(latent_sending)
    normed_second, first_owned = tie(normed_second, main_owned[0])
    normed_grad = reduce_end(normed_part, (normed_inner, normed_near, normed_second)) + (
        against_rows(rot_grad, own_kr)
    )
    in_gain_grad = jnp.sum(normed_grad * residual * inv_first, axis=0)
    input_grad = (
        middle_grad
        + inv_first * norm_gains[0] * normed_grad
        - residual * inv_first**2 * first_dot / D
    )

    gain_grads = wide_totals(
        jnp.concatenate([in_gain_grad, post_gain_grad, q_gain_grad, kv_gain_grad])
    )
    gains_total = gain_grads[: 2 * local_width].reshape(2, local_width)
    qgain_total = gain_grads[2 * local_width : 2 * local_width + q_width]
    kvgain_total = gain_grads[2 * local_width + q_width :]
    change_one, mid_mom_a, mid_sq_a = slot_group(
        main_scales, first_owned, basis_la, basis_ra, mom_a, sq_a, groups[0], None
    )
    last_owned, input_grad = tie(main_owned[1], input_grad)
    change_one, latent_sum.parts, heads_sum.parts = tie(
        change_one, latent_sum.parts, heads_sum.parts
    )
    back_one = lax.all_to_all(change_one, "wide", split_axis=0, concat_axis=0, tiled=True)
    block_heads = heads_sum.finish(w_kvb.shape[1]).reshape(2, -1, w_kvb.shape[1])
    half_qb = w_qb.shape[0] // 2
    block_qb = block_heads[:, :half_qb, : w_qb.shape[1]].reshape(w_qb.shape)
    block_kvb = block_heads[:, half_qb:].reshape(w_kvb.shape)
    block_latent = latent_sum.finish(latent_grad.shape[1])
    block_qa = block_latent[:, :q_width]
    block_kv = block_latent[:, q_width : q_width + kv_width]
    block_kr = block_latent[:, q_width + kv_width :]
    late_blocks = [block_qa, block_kv]
    change_two, mid_mom_a, mid_sq_a = slot_group(
        main_scales, last_owned, basis_la, basis_ra, mom_a, sq_a, groups[1],
        (mid_mom_a, mid_sq_a),
    )
    back_two = lax.all_to_all(change_two, "wide", split_axis=0, concat_axis=0, tiled=True)
    late_capacity = min(late_units, capacity_a)
    late_send, late_back = routes(late_owners, capacity_a, late_capacity, wide_count)
    late_slots, late_scales = late_places(
        late_owners, late_rates, capacity_a, late_capacity, wide_index, tcount
    )
    owners_b, owners_c = owner_b[0], owner_c[0]
    capacity_b, capacity_c = mom_b.shape[0], mom_c.shape[0]
    b_send, b_back = routes(owners_b, capacity_b, capacity_b, wide_count)
    c_send, c_back = routes(owners_c, capacity_c, capacity_c, wide_count)
    sent_parts = [
        jnp.take(unit_rows(blocks), send, axis=0, mode="clip")
        for blocks, send in (
            (late_blocks, late_send),
            ([block_qb], b_send),
            ([block_kvb], c_send),
        )
    ]
    late_owned, owned_b, owned_c = trade_joined(sent_parts, wide_count)
    late_owned, back_one = tie(late_owned, back_one)

    def to_input(*features):
        joined = jnp.stack([value.astype(bf16) for value in features], axis=0)
        joined = joined.reshape(len(features), wide_count, piece_rows, -1).transpose(1, 0, 2, 3)
        returned = lax.all_to_all(joined, "wide", split_axis=0, concat_axis=0, tiled=True)
        placed = jnp.take(returned, deal_row, axis=0, mode="clip").astype(f32)
        return [placed[:, at].reshape(row_count, -1) for at in range(len(features))]

    final_out, final_grad = to_input(layer_out, input_grad)
    late_change, new_mom_a, new_sq_a = late_steps(
        late_slots, late_scales, late_owned, basis_la, basis_ra, mid_mom_a, mid_sq_a
    )
    change_b, new_mom_b, new_sq_b = all_slots(
        slot_scales(owners_b, unit_rates([block_qb.shape[1]], [QR ** (-0.5)]), capacity_b,
                    wide_index, tcount),
        owned_b, basis_lb, basis_rb, mom_b, sq_b,
    )
    change_c, new_mom_c, new_sq_c = all_slots(
        slot_scales(owners_c, unit_rates([block_kvb.shape[1]], [KVR ** (-0.5)]), capacity_c,
                    wide_index, tcount),
        owned_c, basis_lc, basis_rc, mom_c, sq_c,
    )
    returned = trade_joined(
        [change.reshape((-1,) + change.shape[2:]) for change in (late_change, change_b, change_c)],
        wide_count,
    )
    late_result, result_b, result_c = [
        jnp.take(part.reshape((-1,) + part.shape[2:]), back, axis=0, mode="clip")
        for part, back in zip(returned, (late_back, b_back, c_back))
    ]
    new_o, new_gate, new_up, new_down = unpack_units(
        main_back, back_one, back_two, [w_o, w_gate, w_up, w_down]
    )
    update_qa, update_kv = unit_columns(late_result, late_blocks)
    update_qb = unit_columns(result_b, [block_qb])[0]
    update_kvb = unit_columns(result_c, [block_kvb])[0]
    update_kr, new_kr_mom, new_kr_sq = plain_adam(block_kr, kr_mom, kr_sq, wide_rate, tcount)
    update_gains, new_gain_mom, new_gain_sq = plain_adam(
        gains_total, gain_mom, gain_sq, gain_rate, tcount
    )
    update_qgain, new_qgain_mom, new_qgain_sq = plain_adam(
        qgain_total, qgain_mom, qgain_sq, gain_rate, tcount
    )
    update_kvgain, new_kvgain_mom, new_kvgain_sq = plain_adam(
        kvgain_total, kvgain_mom, kvgain_sq, gain_rate, tcount
    )
    return (
        final_out,
        final_grad,
        block_qa,
        block_kv,
        block_qb,
        block_kvb,
        block_o,
        block_gate,
        block_up,
        block_down,
        w_qa.astype(f32) + update_qa,
        w_kv.astype(f32) + update_kv,
        w_qb.astype(f32) + update_qb,
        w_kvb.astype(f32) + update_kvb,
        new_o,
        new_gate,
        new_up,
        new_down,
        block_kr,
        w_kr.astype(f32) + update_kr,
        new_kr_mom,
        new_kr_sq,
        gains_total,
        norm_gains + update_gains,
        new_gain_mom,
        new_gain_sq,
        qgain_total,
        q_gain + update_qgain,
        new_qgain_mom,
        new_qgain_sq,
        kvgain_total,
        kv_gain + update_kvgain,
        new_kvgain_mom,
        new_kvgain_sq,
        new_mom_a,
        new_sq_a,
        new_mom_b,
        new_sq_b,
        new_mom_c,
        new_sq_c,
    )


def solution(mesh):
    return jax.shard_map(
        body,
        mesh=mesh,
        in_specs=(
            P("wide", "narrow"),
            P("wide", "narrow"),
            P("wide", "narrow"),
            P("wide", "narrow"),
            P("wide", None),
            P("wide", "narrow"),
            P("wide", "narrow"),
            P("wide", "narrow"),
            P("wide", "narrow"),
            P("wide", "narrow"),
            P("wide", "narrow"),
            P(None, "narrow"),
            P("narrow"),
            P("narrow"),
            P(),
            P("wide", None),
            P(),
            P("narrow", None),
            P("narrow", None),
            P("narrow", None),
            P("wide", None, "narrow"),
            P("wide", None, "narrow"),
            P("wide", None, "narrow"),
            P("wide", None, "narrow"),
            P("wide", None, "narrow"),
            P("wide", None, "narrow"),
            P("wide", None, "narrow"),
            P("wide", None, "narrow"),
            P("wide", None, "narrow"),
            P("wide", None, "narrow"),
            P("wide", None, "narrow"),
            P("wide", None, "narrow"),
            P("wide", None),
            P("wide", None),
            P(None, "narrow"),
            P(None, "narrow"),
            P("narrow"),
            P("narrow"),
            P("narrow"),
            P("narrow"),
        ),
        out_specs=(
            P("wide", "narrow"),
            P("wide", "narrow"),
            P("wide", "narrow"),
            P("wide", "narrow"),
            P("wide", "narrow"),
            P("wide", "narrow"),
            P("wide", "narrow"),
            P("wide", "narrow"),
            P("wide", "narrow"),
            P("wide", "narrow"),
            P("wide", "narrow"),
            P("wide", "narrow"),
            P("wide", "narrow"),
            P("wide", "narrow"),
            P("wide", "narrow"),
            P("wide", "narrow"),
            P("wide", "narrow"),
            P("wide", "narrow"),
            P("wide", None),
            P("wide", None),
            P("wide", None),
            P("wide", None),
            P(None, "narrow"),
            P(None, "narrow"),
            P(None, "narrow"),
            P(None, "narrow"),
            P("narrow"),
            P("narrow"),
            P("narrow"),
            P("narrow"),
            P("narrow"),
            P("narrow"),
            P("narrow"),
            P("narrow"),
            P("wide", None, "narrow"),
            P("wide", None, "narrow"),
            P("wide", None, "narrow"),
            P("wide", None, "narrow"),
            P("wide", None, "narrow"),
            P("wide", None, "narrow"),
        ),
        check_vma=False,
    )
```

```python
import functools

import jax
import jax.numpy as jnp
from jax import lax
from jax.experimental import pallas as pl
from jax.experimental.pallas import tpu as pltpu
from jax.sharding import PartitionSpec as P

D = 2560
NOPE = 64
ROPE = 32
VH = 64
QR = 768
KVR = 256
SLAB = 64
BASIS = 128


norm_eps = 1e-05
residual_scale = 1.4 / 62**0.5
beta_one = 0.9
beta_two = 0.95
adam_eps = 1e-08
gain_rate = 0.5
masked_value = -1e30
bf16 = jnp.bfloat16
f32 = jnp.float32


def product(left_side, right_side):
    return jnp.dot(left_side, right_side, preferred_element_type=jnp.float32)


def inner_rows(left_side, right_side):
    return lax.dot_general(
        left_side, right_side, (((0,), (0,)), ((), ())), preferred_element_type=jnp.float32
    )


def against_rows(left_side, right_side):
    return lax.dot_general(
        left_side, right_side, (((1,), (1,)), ((), ())), preferred_element_type=jnp.float32
    )


def rope_tables(positions):
    half_width = ROPE // 2
    frequency = 10000.0 ** (-2.0 * jnp.arange(half_width, dtype=jnp.float32) / ROPE)
    angles = positions.astype(jnp.float32)[:, None] * frequency[None, :]
    return (jnp.cos(angles), jnp.sin(angles))


def rotate(block_in, cosine_table, sine_table, direction_sign):
    half_width = block_in.shape[-1] // 2
    lower_half = block_in[..., :half_width]
    upper_half = block_in[..., half_width:]
    signed_sine = direction_sign * sine_table
    return jnp.concatenate(
        [
            lower_half * cosine_table - upper_half * signed_sine,
            upper_half * cosine_table + lower_half * signed_sine,
        ],
        axis=-1,
    )


def plain_adam(gradient, moment, square, step_rate, tcount):
    new_moment = beta_one * moment + (1.0 - beta_one) * gradient
    new_square = beta_two * square + (1.0 - beta_two) * gradient * gradient
    direction = (
        new_moment
        / (1.0 - beta_one**tcount)
        / (jnp.sqrt(new_square / (1.0 - beta_two**tcount)) + adam_eps)
    )
    return (-step_rate * direction, new_moment, new_square)


def shifted(value, step):
    count = lax.axis_size("narrow")
    return lax.ppermute(value, "narrow", [(i, (i + step) % count) for i in range(count)])


def flipped(value, bit):
    count = lax.axis_size("wide")
    return lax.ppermute(value, "wide", [(i, i ^ bit) for i in range(count)])


def along_line(value, pairs):
    return lax.ppermute(value, "narrow", pairs)


pairs_next = [(0, 1), (1, 0), (2, 3), (3, 2)]
pairs_second = [(0, 2), (2, 0), (1, 3), (3, 1)]
pairs_inner = [(1, 2), (2, 1)]
pairs_outward = [(1, 0), (2, 3)]
pairs_inward = [(0, 1), (3, 2)]


def gather_features(features, hold=None):
    count = lax.axis_size("narrow")
    index = lax.axis_index("narrow")
    width = features.shape[1]
    second = along_line(features, pairs_second)
    near = along_line(features, pairs_next)
    inner = along_line(features, pairs_inner)
    if hold is not None:
        second, hold = tie(second, hold)
    outer = along_line(second, pairs_outward)
    third = jnp.where((index == 1) | (index == 2), inner, outer)
    parts = [features, near, second, third]
    places = [index ^ step for step in range(count)]
    joined = jnp.zeros((features.shape[0], count * width), features.dtype)
    for place, part in zip(places, parts):
        joined = lax.dynamic_update_slice(joined, part, (0, place * width))
    return joined if hold is None else (joined, hold)


def line_piece(features, place):
    width = features.shape[1] // lax.axis_size("narrow")
    return lax.dynamic_slice_in_dim(features, place * width, width, 1)


def reduce_start(features):
    index = lax.axis_index("narrow")
    far = line_piece(features, index ^ 3)
    passed = along_line(far, pairs_inward)
    inner = along_line(far, pairs_inner)
    near = along_line(line_piece(features, index ^ 1), pairs_next)
    return passed, inner, near


def reduce_relay(features, passed):
    index = lax.axis_index("narrow")
    return (line_piece(features, index ^ 2).astype(f32) + passed.astype(f32)).astype(bf16)


def reduce_end(features, arrived):
    index = lax.axis_index("narrow")
    total = line_piece(features, index).astype(f32)
    for part in arrived:
        total = total + part.astype(f32)
    return total


def reduce_features(features):
    passed, inner, near = reduce_start(features)
    second = along_line(reduce_relay(features, passed), pairs_second)
    return reduce_end(features, (inner, near, second))


def gather_small(values):
    count = lax.axis_size("narrow")
    index = lax.axis_index("narrow")
    joined = jnp.zeros((count, values.shape[0]), values.dtype)
    for step in range(count):
        part = shifted(values, step) if step else values
        joined = lax.dynamic_update_slice(joined, part[None], ((index - step) % count, 0))
    return joined


def tie(*values):
    return lax.optimization_barrier(values)


def wide_totals(values):
    bit = 1
    while bit < lax.axis_size("wide"):
        values = values + flipped(values, bit)
        bit *= 2
    return values


def row_parts(values):
    return [values] + [shifted(values, step) for step in range(1, lax.axis_size("narrow"))]


def row_totals(values):
    count = lax.axis_size("narrow")
    return values + sum(shifted(values, step) for step in range(1, count))


def halving_orders(count):
    bits = list(range(1, count.bit_length() - 1))
    middle = len(bits) // 2
    return [bits, bits[middle:] + bits[:middle]]


def chunk_rows(features):
    count = lax.axis_size("wide")
    tokens, width = features.shape
    places = []
    for core in (1, 0):
        for half, order in enumerate(halving_orders(count)):
            chunks = [core]
            for bit in reversed(order):
                chunks = chunks + [chunk | (1 << bit) for chunk in chunks]
            places.append([(chunk, half) for chunk in chunks])
    chunks = jnp.array([chunk for group in places for chunk, _ in group], jnp.int32)
    halves = jnp.array([half for group in places for _, half in group], jnp.int32)
    pieces = features.T.reshape(2 * count, width // (2 * count), tokens)
    order = 2 * (lax.axis_index("wide") ^ chunks) + halves
    rows = jnp.take(pieces, order, axis=0, mode="clip").reshape(width, tokens)
    return rows[: width // 2], rows[width // 2 :]


def halves_of(rows):
    half = rows.shape[0] // 2
    return rows[:half], rows[half:]


def summed(values):
    total = values[0].astype(f32)
    for value in values[1:]:
        total = total + value.astype(f32)
    return total


def add_kernel(sizes, rows, *refs):
    outs = refs[sum(sizes) :]
    begin = 0
    for group, size in enumerate(sizes):
        columns = outs[0].shape[1]
        total = summed([ref[:, :columns] for ref in refs[begin : begin + size]])
        begin += size
        if len(outs) == 1:
            outs[0][group * rows : (group + 1) * rows, :] = total.astype(outs[0].dtype)
        else:
            outs[group][...] = total.astype(outs[group].dtype)


def add_rows(groups, place, rows, joined, kept):
    columns = groups[0][0].shape[1]
    start = place * rows
    if rows % 16:
        totals = [summed([part[start : start + rows] for part in parts]) for parts in groups]
        if joined:
            return jnp.concatenate(totals, axis=0)[:, :kept]
        return [total.astype(bf16) for total in totals]
    steps = 1 if joined or rows % 32 else 2
    block = rows // steps
    source = pl.BlockSpec((block, columns), lambda step: (place * steps + step, 0))
    if joined:
        out_specs = [pl.BlockSpec((len(groups) * rows, kept), lambda step: (0, 0))]
        out_shape = [jax.ShapeDtypeStruct((len(groups) * rows, kept), f32)]
    else:
        out_specs = [pl.BlockSpec((block, columns), lambda step: (step, 0))] * len(groups)
        out_shape = [jax.ShapeDtypeStruct((rows, columns), bf16)] * len(groups)
    outs = pl.pallas_call(
        functools.partial(add_kernel, [len(parts) for parts in groups], block),
        grid=(steps,),
        in_specs=[source] * sum(len(parts) for parts in groups),
        out_specs=out_specs,
        out_shape=out_shape,
        compiler_params=pltpu.CompilerParams(vmem_limit_bytes=48 * 1024 * 1024),
    )(*[part for parts in groups for part in parts])
    return outs[0] if joined else list(outs)


class Scatter:
    def __init__(self, products):
        near, away = products[:2], products[2:]
        self.orders = halving_orders(lax.axis_size("wide"))
        self.parts = [[own, flipped(sent, 1)] for own, sent in zip(near, away)]
        self.rows = near[0].shape[0]
        self.stage = 0

    def outgoing(self):
        return add_rows(self.parts, 1, self.rows // 2, False, None)

    def send(self, sending):
        for at, value in enumerate(sending):
            bit = 1 << self.orders[at][self.stage]
            self.parts[at] = self.parts[at] + [flipped(value, bit)]
        self.rows //= 2
        self.stage += 1

    def step(self):
        self.send(self.outgoing())

    def finish(self, kept):
        while self.stage < len(self.orders[0]):
            self.step()
        return add_rows(self.parts, 0, self.rows, True, kept)


def chunk_kernel(order_ref, left_ref, right_ref, near_a, near_b, away_a, away_b, whole_ref):
    core = order_ref[2 * pl.num_programs(0)]
    rows = near_a.shape[0]
    whole_ref[...] = inner_rows(left_ref[...], right_ref[...])
    near = pl.multiple_of(core * 2 * rows, 2 * rows)
    away = pl.multiple_of((1 - core) * 2 * rows, 2 * rows)
    columns = whole_ref.shape[1]
    for out, start in ((near_a, near), (near_b, near + rows), (away_a, away), (away_b, away + rows)):
        out[:, :columns] = whole_ref[pl.ds(start, rows), :].astype(bf16)
        if out.shape[1] > columns:
            out[:, columns:] = jnp.zeros((rows, out.shape[1] - columns), bf16)


def chunk_places(count):
    table = []
    for order in halving_orders(count):
        chips = [0]
        for bit in reversed(order):
            chips = chips + [chip | (1 << (bit - 1)) for chip in chips]
        table.append([chips.index(chip) for chip in range(count // 2)])
    return table


def chunk_products(left, right):
    count = lax.axis_size("wide")
    tokens, width = left.shape
    columns = right.shape[1]
    chips = count // 2
    group = width // chips
    rows = group // 4
    if group % 128 or rows % 16:
        away, near = [product(part, right).astype(bf16) for part in chunk_rows(left)]
        return [*halves_of(near), *halves_of(away)]
    index = lax.axis_index("wide")
    relative = (index // 2) ^ jnp.arange(chips, dtype=jnp.int32)
    order = jnp.concatenate(
        [jnp.array(table, jnp.int32)[relative] for table in chunk_places(count)]
        + [(index % 2)[None]]
    ).astype(jnp.int32)
    padded = -(-columns // 128) * 128
    first = pl.BlockSpec((rows, padded), lambda step, at: (at[step], 0))
    last = pl.BlockSpec((rows, padded), lambda step, at: (at[pl.num_programs(0) + step], 0))
    return list(
        pl.pallas_call(
            chunk_kernel,
            grid_spec=pltpu.PrefetchScalarGridSpec(
                num_scalar_prefetch=1,
                grid=(chips,),
                in_specs=[
                    pl.BlockSpec((tokens, group), lambda step, at: (0, step)),
                    pl.BlockSpec((tokens, columns), lambda step, at: (0, 0)),
                ],
                out_specs=[first, last, first, last],
                scratch_shapes=[pltpu.VMEM((group, columns), f32)],
            ),
            out_shape=[jax.ShapeDtypeStruct((chips * rows, padded), bf16)] * 4,
            compiler_params=pltpu.CompilerParams(vmem_limit_bytes=48 * 1024 * 1024),
        )(order, left, right)
    )


def weight_kernel(left_ref, right_ref, out_ref):
    out_ref[...] = inner_rows(left_ref[...], right_ref[...]).astype(bf16)


def weight_product(left, right):
    tokens, width = left.shape
    columns = right.shape[1]
    group = width // 4
    if group % 128:
        return inner_rows(left, right).astype(bf16)
    return pl.pallas_call(
        weight_kernel,
        grid=(4,),
        in_specs=[
            pl.BlockSpec((tokens, group), lambda step: (0, step)),
            pl.BlockSpec((tokens, columns), lambda step: (0, 0)),
        ],
        out_specs=pl.BlockSpec((group, columns), lambda step: (step, 0)),
        out_shape=jax.ShapeDtypeStruct((width, columns), bf16),
        compiler_params=pltpu.CompilerParams(vmem_limit_bytes=48 * 1024 * 1024),
    )(left, right)


def scatter_rows(partial):
    return lax.psum_scatter(partial, "wide", scatter_dimension=0, tiled=True)


def pack_kernel(send_ref, *refs):
    count = len(refs) - 3
    blocks, outs, turned = refs[:count], refs[count : count + 2], refs[-1]
    begin = 0
    for block in blocks:
        width = block.shape[1]
        turned[begin : begin + width, :] = block[...].astype(f32).T.astype(bf16)
        begin += width
    capacity = outs[0].shape[1] + outs[1].shape[1]
    for out, offset in zip(outs, (0, outs[0].shape[1])):
        slots = out.shape[1]

        def place(step, carry, out=out, offset=offset, slots=slots):
            owner = step // slots
            slot = step % slots
            unit = send_ref[owner * capacity + offset + slot]
            out[owner, slot] = turned[pl.ds(pl.multiple_of(unit * SLAB, SLAB), SLAB), :]
            return carry

        lax.fori_loop(0, out.shape[0] * slots, place, 0)


def pack_units(send, blocks, count, sizes):
    rows = blocks[0].shape[0]
    total = sum(block.shape[1] for block in blocks)
    vmem = pl.BlockSpec(memory_space=pltpu.VMEM)
    return pl.pallas_call(
        pack_kernel,
        in_specs=[pl.BlockSpec(memory_space=pltpu.SMEM)] + [vmem] * len(blocks),
        out_specs=[vmem] * 2,
        out_shape=[jax.ShapeDtypeStruct((count, size, SLAB, rows), bf16) for size in sizes],
        scratch_shapes=[pltpu.VMEM((total, rows), bf16)],
        compiler_params=pltpu.CompilerParams(vmem_limit_bytes=56 * 1024 * 1024),
    )(send, *blocks)


def unpack_kernel(back_ref, first_ref, last_ref, *refs):
    count = (len(refs) - 1) // 2
    weights, outs, turned = refs[:count], refs[count : 2 * count], refs[-1]
    first = first_ref.shape[1]
    capacity = first + last_ref.shape[1]

    def place(unit, carry):
        slot = back_ref[unit]
        owner = slot // capacity
        at = slot % capacity
        rows = pl.ds(pl.multiple_of(unit * SLAB, SLAB), SLAB)

        @pl.when(at < first)
        def _():
            turned[rows, :] = first_ref[owner, at]

        @pl.when(at >= first)
        def _():
            turned[rows, :] = last_ref[owner, at - first]

        return carry

    lax.fori_loop(0, turned.shape[0] // SLAB, place, 0)
    begin = 0
    for weight, out in zip(weights, outs):
        width = out.shape[1]
        steps = turned[begin : begin + width, :].astype(f32).T
        out[...] = weight[...].astype(f32) + steps
        begin += width


def unpack_units(back, first, last, weights):
    rows = first.shape[3]
    total = sum(weight.shape[1] for weight in weights)
    vmem = pl.BlockSpec(memory_space=pltpu.VMEM)
    return pl.pallas_call(
        unpack_kernel,
        in_specs=[pl.BlockSpec(memory_space=pltpu.SMEM)] + [vmem] * (2 + len(weights)),
        out_specs=[vmem] * len(weights),
        out_shape=[jax.ShapeDtypeStruct(weight.shape, f32) for weight in weights],
        scratch_shapes=[pltpu.VMEM((total, rows), bf16)],
        compiler_params=pltpu.CompilerParams(vmem_limit_bytes=56 * 1024 * 1024),
    )(back, first, last, *weights)


def unit_rates(col_widths, rates):
    return jnp.concatenate(
        [
            jnp.full((col_width // SLAB,), step_rate, jnp.float32)
            for col_width, step_rate in zip(col_widths, rates)
        ]
    )


def rotated_step(gradient, left_ref, right_ref, moment_ref, square_ref, new_moment_ref,
                 new_square_ref, turned_ref, occupied, first_scale, second_scale):
    blocks = left_ref.shape[1] // BASIS
    right_basis = right_ref[0].astype(bf16)
    turned_ref[...] = lax.dot_general(
        right_basis, gradient, (((0,), (0,)), ((), ())), preferred_element_type=f32
    )
    for block in range(blocks):
        at = slice(block * BASIS, (block + 1) * BASIS)
        left_basis = left_ref[0, at, :].astype(bf16)
        turned = jnp.dot(turned_ref[:, at].astype(bf16), left_basis, preferred_element_type=f32)
        moment = moment_ref[0, :, at]
        square = square_ref[0, :, at]
        new_moment = beta_one * moment + (1.0 - beta_one) * turned
        new_square = beta_two * square + (1.0 - beta_two) * turned * turned
        new_moment_ref[0, :, at] = jnp.where(occupied > 0.5, new_moment, moment)
        new_square_ref[0, :, at] = jnp.where(occupied > 0.5, new_square, square)
        direction = new_moment * first_scale / (jnp.sqrt(new_square * second_scale) + adam_eps)
        turned_ref[:, at] = lax.dot_general(
            direction.astype(bf16), left_basis, (((1,), (1,)), ((), ())),
            preferred_element_type=f32,
        )
    return jnp.dot(right_basis, turned_ref[...].astype(bf16), preferred_element_type=f32)


def slot_kernel(place_ref, scale_ref, gradient_ref, left_ref, right_ref, moment_ref, square_ref,
                change_ref, new_moment_ref, new_square_ref, whole_ref, turned_ref):
    step = pl.program_id(0)
    steps = pl.num_programs(0)
    sources, rows = gradient_ref.shape[0], gradient_ref.shape[3]
    rate = scale_ref[step]
    occupied = scale_ref[steps + step]

    @pl.when(occupied > 0.5)
    def _():
        for source in range(sources):
            whole_ref[:, source * rows : (source + 1) * rows] = gradient_ref[source, 0].astype(f32)
        whole_ref[...] = rate * rotated_step(
            whole_ref[...].astype(bf16), left_ref, right_ref, moment_ref, square_ref,
            new_moment_ref, new_square_ref, turned_ref, occupied,
            scale_ref[2 * steps], scale_ref[2 * steps + 1],
        )
        for source in range(sources):
            change_ref[source, 0] = whole_ref[:, source * rows : (source + 1) * rows].astype(bf16)

    @pl.when(occupied <= 0.5)
    def _():
        change_ref[...] = jnp.zeros_like(change_ref)

    @pl.when(jnp.logical_and(occupied <= 0.5, place_ref[steps + step] > 0))
    def _():
        new_moment_ref[...] = moment_ref[...]
        new_square_ref[...] = square_ref[...]


def slot_call(places, scales, gradient, left_basis, right_basis, moment, square, written):
    sources, steps, _, rows = gradient.shape
    row_count = sources * rows
    moment = moment.transpose(0, 2, 1)
    square = square.transpose(0, 2, 1)
    state = pl.BlockSpec((1, SLAB, row_count), lambda step, place: (place[step], 0, 0))
    traded = pl.BlockSpec((sources, 1, SLAB, rows), lambda step, place: (0, step, 0, 0))
    operands = [places, scales, gradient, left_basis, right_basis, moment, square]
    in_specs = [
        pl.BlockSpec(memory_space=pltpu.SMEM),
        traded,
        pl.BlockSpec((1, row_count, BASIS), lambda step, place: (place[step], 0, 0)),
        pl.BlockSpec((1, SLAB, SLAB), lambda step, place: (place[step], 0, 0)),
        state,
        state,
    ]
    aliases = {}
    kernel = slot_kernel
    if written == "same":
        aliases = {5: 1, 6: 2}
    elif written is not None:
        operands += [value.transpose(0, 2, 1) for value in written]
        in_specs += [pl.BlockSpec(memory_space=pl.ANY)] * 2
        aliases = {7: 1, 8: 2}

        def kernel(*refs):
            slot_kernel(*refs[:7], *refs[9:])

    change, new_moment, new_square = pl.pallas_call(
        kernel,
        grid_spec=pltpu.PrefetchScalarGridSpec(
            num_scalar_prefetch=1,
            grid=(steps,),
            in_specs=in_specs,
            out_specs=[traded, state, state],
            scratch_shapes=[
                pltpu.VMEM((SLAB, row_count), f32),
                pltpu.VMEM((SLAB, row_count), f32),
            ],
        ),
        out_shape=[
            jax.ShapeDtypeStruct(gradient.shape, bf16),
            jax.ShapeDtypeStruct(moment.shape, f32),
            jax.ShapeDtypeStruct(square.shape, f32),
        ],
        input_output_aliases=aliases,
        compiler_params=pltpu.CompilerParams(vmem_limit_bytes=48 * 1024 * 1024),
    )(*operands)
    return change, new_moment.transpose(0, 2, 1), new_square.transpose(0, 2, 1)


def slot_group(scales, gradient, left_basis, right_basis, moment, square, group, written):
    capacity = moment.shape[0]
    count = group.stop - group.start
    places = jnp.concatenate(
        [
            jnp.arange(group.start, group.stop, dtype=jnp.int32),
            jnp.ones((count,), jnp.int32),
        ]
    )
    scales = jnp.concatenate(
        [
            scales[group],
            scales[capacity + group.start : capacity + group.stop],
            scales[2 * capacity :],
        ]
    )
    return slot_call(places, scales, gradient, left_basis, right_basis, moment, square, written)


def all_slots(scales, gradient, left_basis, right_basis, moment, square):
    group = slice(0, moment.shape[0])
    return slot_group(
        scales, gradient, left_basis, right_basis, moment, square, group, None
    )


def late_steps(places, scales, gradient, left_basis, right_basis, moment, square):
    return slot_call(places, scales, gradient, left_basis, right_basis, moment, square, "same")


def correction_scales(tcount):
    return jnp.stack([1.0 / (1.0 - beta_one**tcount), 1.0 / (1.0 - beta_two**tcount)])


def slot_scales(owners, rates, capacity, wide_index, tcount):
    slot_ids = wide_index * capacity + jnp.arange(capacity, dtype=jnp.int32)
    own = (owners[None, :] == slot_ids[:, None]).astype(f32)
    return jnp.concatenate(
        [
            -jnp.sum(own * rates[None, :], axis=1),
            jnp.sum(own, axis=1),
            correction_scales(tcount),
        ]
    )


def ranks_within(owners, capacity):
    device = owners // capacity
    units = owners.shape[0]
    earlier = jnp.arange(units)[None, :] < jnp.arange(units)[:, None]
    return jnp.sum(
        jnp.where(earlier & (device[None, :] == device[:, None]), 1, 0).astype(jnp.int32), axis=1
    )


def turned_lanes(value, tables, sign):
    near = pltpu.roll(value, 112, 1) * tables[1]
    far = pltpu.roll(value, 16, 1) * tables[2]
    return value * tables[0] + sign * (near + far)


def lane_ids(shape):
    return lax.broadcasted_iota(jnp.int32, shape, 1)


def head_inputs(head, query_ref, key_value_ref, rotary_ref, tables, bias_ref):
    at = slice(head * 128, (head + 1) * 128)
    query = turned_lanes(query_ref[:, at], tables, 1.0).astype(bf16)
    key_value = key_value_ref[:, at].astype(bf16)
    key = jnp.where(lane_ids(key_value.shape) < NOPE, key_value, rotary_ref[...])
    scores = against_rows(query, key) * (NOPE + ROPE) ** (-0.5) + bias_ref[...]
    exp_scores = jnp.exp(scores - jnp.max(scores, axis=1, keepdims=True))
    probs = exp_scores / jnp.sum(exp_scores, axis=1, keepdims=True)
    return query, key_value, key, probs


def attend_kernel(query_ref, key_value_ref, rotary_ref, table_ref, bias_ref, out_ref):
    tables = [table_ref[at] for at in range(3)]
    mixed = []
    for head in range(2):
        _, key_value, _, probs = head_inputs(
            head, query_ref, key_value_ref, rotary_ref, tables, bias_ref
        )
        mixed.append(product(probs.astype(bf16), key_value))
    lower = pltpu.roll(mixed[0], 64, 1)
    out_ref[...] = jnp.where(lane_ids(lower.shape) < VH, lower, mixed[1]).astype(bf16)


def attend_back_kernel(query_ref, key_value_ref, rotary_ref, table_ref, bias_ref, grad_ref,
                       query_grad_ref, key_value_grad_ref, sums_ref):
    tables = [table_ref[at] for at in range(3)]
    scale = (NOPE + ROPE) ** (-0.5)

    @pl.when(pl.program_id(0) == 0)
    def _():
        sums_ref[...] = jnp.zeros_like(sums_ref)

    for head in range(2):
        at = slice(head * 128, (head + 1) * 128)
        query, key_value, key, probs = head_inputs(
            head, query_ref, key_value_ref, rotary_ref, tables, bias_ref
        )
        grad = grad_ref[...].astype(f32)
        lanes = lane_ids(grad.shape)
        if head == 0:
            grad = pltpu.roll(grad, 64, 1)
        grad = jnp.where(lanes < NOPE, 0.0, grad).astype(bf16)
        value_grad = inner_rows(probs.astype(bf16), grad)
        prob_grad = against_rows(grad, key_value)
        delta = jnp.sum(probs * prob_grad, axis=1, keepdims=True)
        score_grad = (probs * (prob_grad - delta)).astype(bf16)
        query_grad = turned_lanes(scale * product(score_grad, key), tables, -1.0).astype(bf16)
        key_grad = scale * inner_rows(score_grad, query)
        key_value_grad = jnp.where(lanes < NOPE, key_grad, value_grad).astype(bf16)
        query_grad_ref[:, at] = query_grad
        key_value_grad_ref[:, at] = key_value_grad
        sums_ref[0] += query_grad.astype(f32) * query_ref[:, at]
        sums_ref[1] += key_value_grad.astype(f32) * key_value_ref[:, at]
        sums_ref[2] += key_grad


def attend_specs(tokens):
    pair = pl.BlockSpec((tokens, 256), lambda step: (0, step))
    single = pl.BlockSpec((tokens, 128), lambda step: (0, step))
    shared = pl.BlockSpec((tokens, 128), lambda step: (0, 0))
    tables = pl.BlockSpec((3, tokens, 128), lambda step: (0, 0, 0))
    bias = pl.BlockSpec((tokens, tokens), lambda step: (0, 0))
    return pair, single, shared, tables, bias


def attend(queries, keys_values, rotary, tables, bias):
    tokens, width = queries.shape
    pair, single, shared, table_spec, bias_spec = attend_specs(tokens)
    return pl.pallas_call(
        attend_kernel,
        grid=(width // 256,),
        in_specs=[pair, pair, shared, table_spec, bias_spec],
        out_specs=single,
        out_shape=jax.ShapeDtypeStruct((tokens, width // 2), bf16),
        compiler_params=pltpu.CompilerParams(vmem_limit_bytes=48 * 1024 * 1024),
    )(queries, keys_values, rotary, tables, bias)


def attend_back(queries, keys_values, rotary, tables, bias, grad):
    tokens, width = queries.shape
    pair, single, shared, table_spec, bias_spec = attend_specs(tokens)
    return pl.pallas_call(
        attend_back_kernel,
        grid=(width // 256,),
        in_specs=[pair, pair, shared, table_spec, bias_spec, single],
        out_specs=[pair, pair, table_spec],
        out_shape=[
            jax.ShapeDtypeStruct((tokens, width), bf16),
            jax.ShapeDtypeStruct((tokens, width), bf16),
            jax.ShapeDtypeStruct((3, tokens, 128), f32),
        ],
        compiler_params=pltpu.CompilerParams(vmem_limit_bytes=48 * 1024 * 1024),
    )(queries, keys_values, rotary, tables, bias, grad)


def routes(owners, capacity, room, wide_count):
    units = owners.shape[0]
    if room == capacity:
        places = owners
    else:
        places = owners // capacity * room + ranks_within(owners, capacity)
    slots = jnp.arange(wide_count * room, dtype=jnp.int32)
    matches = slots[:, None] == places[None, :]
    unit_of = jnp.sum(
        jnp.where(matches, jnp.arange(units, dtype=jnp.int32)[None, :], 0), axis=1
    )
    return jnp.minimum(unit_of, units - 1), places


def late_places(owners, rates, capacity, room, wide_index, tcount):
    ranks = ranks_within(owners, capacity)
    mine = owners // capacity == wide_index
    own = mine[None, :] & (ranks[None, :] == jnp.arange(room, dtype=jnp.int32)[:, None])
    slot = jnp.sum(jnp.where(own, (owners % capacity)[None, :], 0), axis=1)
    filled = jnp.sum(own.astype(jnp.int32), axis=1)
    last = jnp.maximum(jnp.sum(filled) - 1, 0)
    last_slot = jnp.sum(jnp.where(jnp.arange(room) == last, slot, 0))
    places = jnp.where(filled > 0, slot, last_slot)
    untouched = jnp.where((jnp.arange(room) == 0) & (filled == 0), 1, 0)
    scales = jnp.concatenate(
        [
            -jnp.sum(own.astype(f32) * rates[None, :], axis=1),
            filled.astype(f32),
            correction_scales(tcount),
        ]
    )
    return jnp.concatenate([places, untouched]).astype(jnp.int32), scales


def unit_rows(blocks):
    joined = jnp.concatenate([block.T for block in blocks], axis=0).astype(bf16)
    return joined.reshape(-1, SLAB, joined.shape[1])


def unit_columns(units, blocks):
    joined = units.reshape(-1, units.shape[2])
    pieces, begin = ([], 0)
    for block in blocks:
        pieces.append(joined[begin : begin + block.shape[1]].T.astype(f32))
        begin += block.shape[1]
    return pieces


def trade_joined(parts, count):
    steps = [part.shape[0] // count for part in parts]
    widths = [part.shape[2] for part in parts]
    room = max(steps)
    joined = jnp.concatenate(
        [
            jnp.pad(
                part.reshape(count, own, SLAB, width), ((0, 0), (0, room - own), (0, 0), (0, 0))
            )
            for part, own, width in zip(parts, steps, widths)
        ],
        axis=3,
    )
    traded = lax.all_to_all(joined, "wide", split_axis=0, concat_axis=0, tiled=True)
    pieces, begin = ([], 0)
    for own, width in zip(steps, widths):
        pieces.append(traded[:, :own, :, begin : begin + width])
        begin += width
    return pieces


def body(
    x_in,
    grad_out,
    w_qa,
    w_kv,
    w_kr,
    w_qb,
    w_kvb,
    w_o,
    w_gate,
    w_up,
    w_down,
    norm_gains,
    q_gain,
    kv_gain,
    deal,
    lengths,
    step_count,
    owner_a,
    owner_b,
    owner_c,
    basis_la,
    basis_ra,
    basis_lb,
    basis_rb,
    basis_lc,
    basis_rc,
    mom_a,
    sq_a,
    mom_b,
    sq_b,
    mom_c,
    sq_c,
    kr_mom,
    kr_sq,
    gain_mom,
    gain_sq,
    qgain_mom,
    qgain_sq,
    kvgain_mom,
    kvgain_sq,
):
    wide_count = lax.axis_size("wide")
    wide_index = lax.axis_index("wide")
    narrow_index = lax.axis_index("narrow")
    row_count, local_width = x_in.shape
    piece_rows = row_count // wide_count
    deal_row = lax.dynamic_index_in_dim(deal, wide_index, 0, keepdims=False)
    wide_ids = jnp.arange(wide_count, dtype=jnp.int32)
    inverse = jnp.sum(
        jnp.where(deal_row[None, :] == wide_ids[:, None], wide_ids[None, :], 0), axis=1
    )

    def to_working(features):
        outgoing = jnp.take(
            features.reshape((wide_count, piece_rows) + features.shape[1:]), inverse, axis=0,
            mode="clip",
        )
        dealt = lax.all_to_all(outgoing, "wide", split_axis=0, concat_axis=0, tiled=True)
        return dealt.reshape(row_count, -1)

    token_in = to_working(x_in)
    residual = token_in.astype(f32)
    seq_lengths = lengths[0]
    seq_ends = jnp.cumsum(seq_lengths)
    row_ids = jnp.arange(row_count, dtype=jnp.int32)
    segment = jnp.sum((row_ids[:, None] >= seq_ends[None, :-1]).astype(jnp.int32), axis=1)
    pick = jnp.arange(seq_lengths.shape[0], dtype=jnp.int32)[None, :] == segment[:, None]
    seq_start = jnp.sum(jnp.where(pick, (seq_ends - seq_lengths)[None, :], 0), axis=1)
    live_rows = (segment < seq_lengths.shape[0] - 1).astype(f32)[:, None]
    cosine_table, sine_table = rope_tables(row_ids - seq_start)
    cos_heads = cosine_table[:, None, :]
    sin_heads = sine_table[:, None, :]

    latent_own = jnp.concatenate([w_qa, w_kv, w_kr], axis=1)
    heads_here = w_o.shape[1] // VH
    padded_qb = jnp.pad(
        w_qb.reshape(w_qb.shape[0], heads_here, NOPE + ROPE),
        ((0, 0), (0, 0), (0, 128 - NOPE - ROPE)),
    ).reshape(w_qb.shape[0], -1)
    full_latent = lax.all_gather(latent_own, "wide", axis=0, tiled=True)
    full_qb = lax.all_gather(padded_qb, "wide", axis=0, tiled=True)
    full_kvb = lax.all_gather(w_kvb, "wide", axis=0, tiled=True)
    full_o = lax.all_gather(w_o, "wide", axis=0, tiled=True)
    full_gate = lax.all_gather(w_gate, "wide", axis=0, tiled=True)
    full_up = lax.all_gather(w_up, "wide", axis=0, tiled=True)
    full_down = lax.all_gather(w_down, "wide", axis=0, tiled=True)
    gains_all = gather_small(jnp.concatenate([norm_gains[0], norm_gains[1], q_gain, kv_gain]))
    first_gain = gains_all[:, :local_width].reshape(1, -1)
    second_gain = gains_all[:, local_width : 2 * local_width].reshape(1, -1)
    q_width = q_gain.shape[0]
    kv_width = kv_gain.shape[0]
    q_gain_all = gains_all[:, 2 * local_width : 2 * local_width + q_width].reshape(1, -1)
    kv_gain_all = gains_all[:, 2 * local_width + q_width :].reshape(1, -1)

    def inverse_rms(features, width):
        wide = features.astype(f32)
        return lax.rsqrt(jnp.sum(wide * wide, axis=1, keepdims=True) / width + norm_eps)

    token_all, full_latent = gather_features(token_in, full_latent)
    inv_first = inverse_rms(token_all, D)
    normed = (token_all.astype(f32) * inv_first * first_gain).astype(bf16)
    latents = product(normed, full_latent)
    q_latent = latents[:, :q_width]
    kv_latent = latents[:, q_width : q_width + kv_width]
    key_rot = latents[:, q_width + kv_width :]
    narrow_count = lax.axis_size("narrow")
    latents_all = gather_features(latents[:, : q_width + kv_width].astype(bf16))
    latents_all = latents_all.reshape(row_count, narrow_count, q_width + kv_width)
    q_latent_all = latents_all[:, :, :q_width].reshape(row_count, QR).astype(f32)
    kv_latent_all = latents_all[:, :, q_width:].reshape(row_count, KVR).astype(f32)
    inv_q = inverse_rms(q_latent_all, QR)
    inv_kv = inverse_rms(kv_latent_all, KVR)
    q_normed = (q_latent_all * inv_q * q_gain_all).astype(bf16)
    kv_normed = (kv_latent_all * inv_kv * kv_gain_all).astype(bf16)
    q_pre = product(q_normed, full_qb)
    kv_pre = product(kv_normed, full_kvb)
    key_turned = rotate(key_rot, cosine_table, sine_table, 1.0)
    rotary = jnp.pad(key_turned, ((0, 0), (NOPE, 128 - NOPE - ROPE))).astype(bf16)
    allowed = (segment[:, None] == segment[None, :]) & (row_ids[None, :] <= row_ids[:, None])
    bias = jnp.where(allowed, 0.0, masked_value).astype(f32)
    half_pads = ((NOPE, 128 - NOPE - ROPE // 2), (NOPE + ROPE // 2, 128 - NOPE - ROPE))

    def lane_table(lower, upper):
        return sum(
            jnp.pad(part, ((0, 0), pads)) for part, pads in zip((lower, upper), half_pads)
        )

    empty = jnp.zeros_like(sine_table)
    tables = jnp.stack(
        [
            lane_table(cosine_table, cosine_table)
            + jnp.where(jnp.arange(128) < NOPE, 1.0, 0.0)[None, :],
            lane_table(-sine_table, empty),
            lane_table(empty, sine_table),
        ]
    )
    latents_all, grad_out = tie(latents_all, grad_out)
    heads_out = attend(q_pre, kv_pre, rotary, tables, bias)
    grad_all, heads_out = gather_features(grad_out, heads_out)
    token_grad_all = to_working(grad_all)
    grad_top = lax.dynamic_slice_in_dim(
        token_grad_all, narrow_index * local_width, local_width, 1
    ).astype(f32)
    mlp_grad = (residual_scale * live_rows * token_grad_all.astype(f32)).astype(bf16)
    attn_out = reduce_features(against_rows(heads_out, full_o).astype(bf16))
    middle = residual + residual_scale * live_rows * attn_out
    middle_all = gather_features(middle.astype(bf16)).astype(f32)
    inv_second = inverse_rms(middle_all, D)
    normed_two = (middle_all * inv_second * second_gain).astype(bf16)
    gate_act = product(normed_two, full_gate)
    upward = product(normed_two, full_up)
    sigmoid_gate = jax.nn.sigmoid(gate_act)
    silu_gate = gate_act * sigmoid_gate
    active = (silu_gate * upward).astype(bf16)
    mlp_part = against_rows(active, full_down).astype(bf16)
    mlp_passed, mlp_inner, mlp_near = reduce_start(mlp_part)
    down_products = chunk_products(mlp_grad, active)
    active_grad = product(mlp_grad, full_down)
    gate_grad = (
        active_grad * upward * (sigmoid_gate + silu_gate * (1.0 - sigmoid_gate))
    ).astype(bf16)
    up_grad = (active_grad * silu_gate).astype(bf16)
    gate_grad, up_grad, down_products = tie(gate_grad, up_grad, down_products)
    down_sum = Scatter(down_products)
    normed_two_part = (
        against_rows(gate_grad, full_gate) + against_rows(up_grad, full_up)
    ).astype(bf16)
    passed, inner, near = reduce_start(normed_two_part)
    gate_products = chunk_products(normed_two, gate_grad)
    passed, gate_products, up_grad, down_sending = tie(
        passed, gate_products, up_grad, down_sum.outgoing()
    )
    down_sum.send(down_sending)
    gate_sum = Scatter(gate_products)
    relayed = reduce_relay(normed_two_part, passed)
    relayed, up_grad = tie(relayed, up_grad)
    second = along_line(relayed, pairs_second)
    up_sum = Scatter(chunk_products(normed_two, up_grad))
    second, up_sum.parts = tie(second, up_sum.parts)
    normed_two_grad = reduce_end(normed_two_part, (inner, near, second))
    post_gain_grad = jnp.sum(normed_two_grad * middle * inv_second, axis=0)
    direct_grad = grad_top + inv_second * norm_gains[1] * normed_two_grad
    direct_all, sendings = gather_features(
        direct_grad.astype(bf16),
        (gate_sum.outgoing(), up_sum.outgoing(), down_sum.outgoing()),
    )
    direct_all = direct_all.astype(f32)
    top_all = token_grad_all.astype(f32)
    second_dot = jnp.sum((direct_all - top_all) * middle_all, axis=1, keepdims=True)
    attn_grad = (
        residual_scale
        * live_rows
        * (direct_all - middle_all * (inv_second**2 * second_dot / D))
    ).astype(bf16)
    middle_grad = direct_grad - middle * (inv_second**2 * second_dot / D)
    for weight_sum, sending in zip((gate_sum, up_sum, down_sum), sendings):
        weight_sum.send(sending)
    o_full = weight_product(attn_grad, heads_out)
    attn_grad, o_full = tie(attn_grad, o_full)
    block_o = scatter_rows(o_full)
    mlp_passed, attn_grad = tie(mlp_passed, attn_grad)
    mlp_second = along_line(reduce_relay(mlp_part, mlp_passed), pairs_second)
    heads_grad = product(attn_grad, full_o).astype(bf16)

    q_pre_grad, kv_pre_grad, head_sums = attend_back(
        q_pre, kv_pre, rotary, tables, bias, heads_grad
    )
    mlp_arrived = (mlp_inner, mlp_near, mlp_second)
    head_sums, q_pre_grad, gate_sending, up_sending = tie(
        head_sums, q_pre_grad, gate_sum.outgoing(), up_sum.outgoing()
    )
    gate_sum.send(gate_sending)
    up_sum.send(up_sending)
    mlp_out = reduce_end(mlp_part, mlp_arrived)
    layer_out = middle + residual_scale * live_rows * mlp_out
    rot_partial = rotate(
        head_sums[2, :, NOPE : NOPE + ROPE], cosine_table, sine_table, -1.0
    )
    q_dot = jnp.sum(head_sums[0], axis=1)
    kv_dot = jnp.sum(head_sums[1], axis=1)
    dots = row_parts(jnp.concatenate([jnp.stack([q_dot, kv_dot]), rot_partial.T], axis=0))
    q_part = against_rows(q_pre_grad, full_qb).astype(bf16)
    kv_part = against_rows(kv_pre_grad, full_kvb).astype(bf16)
    both_part = jnp.concatenate(
        [
            q_part.reshape(row_count, narrow_count, q_width),
            kv_part.reshape(row_count, narrow_count, kv_width),
        ],
        axis=-1,
    ).reshape(row_count, -1)
    passed, inner, near = reduce_start(both_part)
    tcount = step_count[0].astype(f32)
    wide_rate = D ** (-0.5)
    block_down = down_sum.finish(w_down.shape[1])
    block_gate = gate_sum.finish(w_gate.shape[1])
    block_up = up_sum.finish(w_up.shape[1])
    passed, q_pre_late, kv_pre_late, block_down, block_gate, block_up = tie(
        passed, q_pre_grad, kv_pre_grad, block_down, block_gate, block_up
    )
    main_blocks = [block_o, block_gate, block_up, block_down]
    late_blocks_widths = [q_width, kv_width]
    late_units = sum(late_blocks_widths) // SLAB
    main_rates = unit_rates(
        [block.shape[1] for block in main_blocks], [1.0, wide_rate, wide_rate, 0.125]
    )
    late_rates = unit_rates(late_blocks_widths, [wide_rate, wide_rate])
    late_owners, main_owners = owner_a[0, :late_units], owner_a[0, late_units:]
    capacity_a = mom_a.shape[0]
    main_send, main_back = routes(main_owners, capacity_a, capacity_a, wide_count)
    main_scales = slot_scales(main_owners, main_rates, capacity_a, wide_index, tcount)
    first_slots = (capacity_a + 1) // 2
    groups = [slice(0, first_slots), slice(first_slots, capacity_a)]
    main_sent = pack_units(
        main_send, main_blocks, wide_count, [group.stop - group.start for group in groups]
    )
    second = along_line(reduce_relay(both_part, passed), pairs_second)
    head_columns = w_kvb.shape[1]
    qb_full = inner_rows(q_normed, q_pre_late).astype(bf16)
    kvb_full = inner_rows(kv_normed, kv_pre_late).astype(bf16)
    head_products = jnp.concatenate(
        [
            qb_full.reshape(wide_count, -1, head_columns),
            kvb_full.reshape(wide_count, -1, head_columns),
        ],
        axis=1,
    ).reshape(-1, head_columns)
    second, dots, main_sent, head_products = tie(second, dots, main_sent, head_products)
    main_owned = [
        lax.all_to_all(part, "wide", split_axis=0, concat_axis=0, tiled=True)
        for part in main_sent
    ]
    dots = sum(dots).T
    q_dot, kv_dot = dots[:, :1], dots[:, 1:2]
    rot_grad = dots[:, 2:].astype(bf16)
    head_products, block_o = tie(head_products, block_o)
    block_heads = scatter_rows(head_products)
    both_grad = reduce_end(both_part, (inner, near, second))
    q_normed_grad = both_grad[:, :q_width]
    kv_normed_grad = both_grad[:, q_width:]
    q_gain_grad = jnp.sum(q_normed_grad * q_latent * inv_q, axis=0)
    kv_gain_grad = jnp.sum(kv_normed_grad * kv_latent * inv_kv, axis=0)
    q_latent_grad = (
        inv_q * q_gain * q_normed_grad - q_latent * inv_q**2 * q_dot / QR
    ).astype(bf16)
    kv_latent_grad = (
        inv_kv * kv_gain * kv_normed_grad - kv_latent * inv_kv**2 * kv_dot / KVR
    ).astype(bf16)
    share = (narrow_index == 0).astype(f32)
    first_dot = row_parts(
        jnp.sum(q_latent_grad.astype(f32) * q_latent, axis=1)
        + jnp.sum(kv_latent_grad.astype(f32) * kv_latent, axis=1)
        + share * jnp.sum(rot_grad.astype(f32) * key_rot, axis=1)
    )
    latent_grad = jnp.concatenate([q_latent_grad, kv_latent_grad, rot_grad], axis=1)
    full_kr = full_latent[:, q_width + kv_width :]
    own_kr = lax.dynamic_slice_in_dim(full_kr, narrow_index * local_width, local_width, 0)
    normed_part = against_rows(
        latent_grad[:, : q_width + kv_width], full_latent[:, : q_width + kv_width]
    ).astype(bf16)
    normed_passed, normed_inner, normed_near = reduce_start(normed_part)
    latent_full = weight_product(normed, latent_grad)
    normed_passed, latent_full = tie(normed_passed, latent_full)
    latent_late, first_owned, first_dot = tie(latent_full, main_owned[0], first_dot)
    first_dot = sum(first_dot)[:, None]
    block_latent = scatter_rows(latent_late)
    normed_second = along_line(reduce_relay(normed_part, normed_passed), pairs_second)
    normed_second, first_owned = tie(normed_second, first_owned)
    change_one, mid_mom_a, mid_sq_a = slot_group(
        main_scales, first_owned, basis_la, basis_ra, mom_a, sq_a, groups[0], None
    )
    change_one, last_owned = tie(change_one, main_owned[1])
    back_one = lax.all_to_all(change_one, "wide", split_axis=0, concat_axis=0, tiled=True)
    normed_grad = reduce_end(normed_part, (normed_inner, normed_near, normed_second)) + (
        against_rows(rot_grad, own_kr)
    )
    in_gain_grad = jnp.sum(normed_grad * residual * inv_first, axis=0)
    input_grad = (
        middle_grad
        + inv_first * norm_gains[0] * normed_grad
        - residual * inv_first**2 * first_dot / D
    )

    change_two, mid_mom_a, mid_sq_a = slot_group(
        main_scales, last_owned, basis_la, basis_ra, mom_a, sq_a, groups[1],
        (mid_mom_a, mid_sq_a),
    )
    block_latent, block_heads, change_two = tie(block_latent, block_heads, change_two)
    back_two = lax.all_to_all(change_two, "wide", split_axis=0, concat_axis=0, tiled=True)
    block_qb = block_heads[: w_qb.shape[0]].reshape(w_qb.shape[0], heads_here, 128)
    block_qb = block_qb[:, :, : NOPE + ROPE].reshape(w_qb.shape)
    block_kvb = block_heads[w_qb.shape[0] :]
    block_qa = block_latent[:, :q_width]
    block_kv = block_latent[:, q_width : q_width + kv_width]
    block_kr = block_latent[:, q_width + kv_width :]
    late_blocks = [block_qa, block_kv]
    late_capacity = min(late_units, capacity_a)
    late_send, late_back = routes(late_owners, capacity_a, late_capacity, wide_count)
    late_slots, late_scales = late_places(
        late_owners, late_rates, capacity_a, late_capacity, wide_index, tcount
    )
    owners_b, owners_c = owner_b[0], owner_c[0]
    capacity_b, capacity_c = mom_b.shape[0], mom_c.shape[0]
    b_send, b_back = routes(owners_b, capacity_b, capacity_b, wide_count)
    c_send, c_back = routes(owners_c, capacity_c, capacity_c, wide_count)
    sent_parts = [
        jnp.take(unit_rows(blocks), send, axis=0, mode="clip")
        for blocks, send in (
            (late_blocks, late_send),
            ([block_qb], b_send),
            ([block_kvb], c_send),
        )
    ]
    sent_parts, back_two = tie(sent_parts, back_two)
    late_owned, owned_b, owned_c = trade_joined(sent_parts, wide_count)

    gain_part = jnp.concatenate([in_gain_grad, post_gain_grad, q_gain_grad, kv_gain_grad])
    gain_high = lax.optimization_barrier(gain_part.astype(bf16))
    gain_low = (gain_part - gain_high.astype(f32)).astype(bf16)
    gain_rows = jnp.concatenate([gain_high, gain_low])
    gain_height = -(-gain_rows.shape[0] // local_width)
    gain_rows = jnp.pad(gain_rows, (0, gain_height * local_width - gain_rows.shape[0]))
    gain_rows = jnp.broadcast_to(
        gain_rows.reshape(1, gain_height, local_width), (wide_count, gain_height, local_width)
    )
    leaving = jnp.concatenate(
        [
            layer_out.astype(bf16).reshape(wide_count, piece_rows, local_width),
            input_grad.astype(bf16).reshape(wide_count, piece_rows, local_width),
            gain_rows,
        ],
        axis=1,
    )
    leaving, late_owned = tie(leaving, late_owned)
    returned_rows = lax.all_to_all(leaving, "wide", split_axis=0, concat_axis=0, tiled=True)
    placed = jnp.take(returned_rows[:, : 2 * piece_rows], deal_row, axis=0, mode="clip")
    final_out = placed[:, :piece_rows].astype(f32).reshape(row_count, local_width)
    final_grad = placed[:, piece_rows:].astype(f32).reshape(row_count, local_width)
    gain_rows = returned_rows[:, 2 * piece_rows :].reshape(wide_count, -1)
    gain_size = gain_part.shape[0]
    gain_grads = jnp.sum(gain_rows[:, :gain_size].astype(f32), axis=0) + jnp.sum(
        gain_rows[:, gain_size : 2 * gain_size].astype(f32), axis=0
    )
    gains_total = gain_grads[: 2 * local_width].reshape(2, local_width)
    qgain_total = gain_grads[2 * local_width : 2 * local_width + q_width]
    kvgain_total = gain_grads[2 * local_width + q_width :]
    late_change, new_mom_a, new_sq_a = late_steps(
        late_slots, late_scales, late_owned, basis_la, basis_ra, mid_mom_a, mid_sq_a
    )
    change_b, new_mom_b, new_sq_b = all_slots(
        slot_scales(owners_b, unit_rates([block_qb.shape[1]], [QR ** (-0.5)]), capacity_b,
                    wide_index, tcount),
        owned_b, basis_lb, basis_rb, mom_b, sq_b,
    )
    change_c, new_mom_c, new_sq_c = all_slots(
        slot_scales(owners_c, unit_rates([block_kvb.shape[1]], [KVR ** (-0.5)]), capacity_c,
                    wide_index, tcount),
        owned_c, basis_lc, basis_rc, mom_c, sq_c,
    )
    late_change, final_grad = tie(late_change, final_grad)
    returned = trade_joined(
        [change.reshape((-1,) + change.shape[2:]) for change in (late_change, change_b, change_c)],
        wide_count,
    )
    late_result, result_b, result_c = [
        jnp.take(part.reshape((-1,) + part.shape[2:]), back, axis=0, mode="clip")
        for part, back in zip(returned, (late_back, b_back, c_back))
    ]
    new_o, new_gate, new_up, new_down = unpack_units(
        main_back, back_one, back_two, [w_o, w_gate, w_up, w_down]
    )
    update_qa, update_kv = unit_columns(late_result, late_blocks)
    update_qb = unit_columns(result_b, [block_qb])[0]
    update_kvb = unit_columns(result_c, [block_kvb])[0]
    block_kr = block_kr.astype(f32)
    update_kr, new_kr_mom, new_kr_sq = plain_adam(block_kr, kr_mom, kr_sq, wide_rate, tcount)
    update_gains, new_gain_mom, new_gain_sq = plain_adam(
        gains_total, gain_mom, gain_sq, gain_rate, tcount
    )
    update_qgain, new_qgain_mom, new_qgain_sq = plain_adam(
        qgain_total, qgain_mom, qgain_sq, gain_rate, tcount
    )
    update_kvgain, new_kvgain_mom, new_kvgain_sq = plain_adam(
        kvgain_total, kvgain_mom, kvgain_sq, gain_rate, tcount
    )
    return (
        final_out,
        final_grad,
        block_qa.astype(f32),
        block_kv.astype(f32),
        block_qb.astype(f32),
        block_kvb.astype(f32),
        block_o.astype(f32),
        block_gate,
        block_up,
        block_down,
        w_qa.astype(f32) + update_qa,
        w_kv.astype(f32) + update_kv,
        w_qb.astype(f32) + update_qb,
        w_kvb.astype(f32) + update_kvb,
        new_o,
        new_gate,
        new_up,
        new_down,
        block_kr,
        w_kr.astype(f32) + update_kr,
        new_kr_mom,
        new_kr_sq,
        gains_total,
        norm_gains + update_gains,
        new_gain_mom,
        new_gain_sq,
        qgain_total,
        q_gain + update_qgain,
        new_qgain_mom,
        new_qgain_sq,
        kvgain_total,
        kv_gain + update_kvgain,
        new_kvgain_mom,
        new_kvgain_sq,
        new_mom_a,
        new_sq_a,
        new_mom_b,
        new_sq_b,
        new_mom_c,
        new_sq_c,
    )


def solution(mesh):
    return jax.shard_map(
        body,
        mesh=mesh,
        in_specs=(
            P("wide", "narrow"),
            P("wide", "narrow"),
            P("wide", "narrow"),
            P("wide", "narrow"),
            P("wide", None),
            P("wide", "narrow"),
            P("wide", "narrow"),
            P("wide", "narrow"),
            P("wide", "narrow"),
            P("wide", "narrow"),
            P("wide", "narrow"),
            P(None, "narrow"),
            P("narrow"),
            P("narrow"),
            P(),
            P("wide", None),
            P(),
            P("narrow", None),
            P("narrow", None),
            P("narrow", None),
            P("wide", None, "narrow"),
            P("wide", None, "narrow"),
            P("wide", None, "narrow"),
            P("wide", None, "narrow"),
            P("wide", None, "narrow"),
            P("wide", None, "narrow"),
            P("wide", None, "narrow"),
            P("wide", None, "narrow"),
            P("wide", None, "narrow"),
            P("wide", None, "narrow"),
            P("wide", None, "narrow"),
            P("wide", None, "narrow"),
            P("wide", None),
            P("wide", None),
            P(None, "narrow"),
            P(None, "narrow"),
            P("narrow"),
            P("narrow"),
            P("narrow"),
            P("narrow"),
        ),
        out_specs=(
            P("wide", "narrow"),
            P("wide", "narrow"),
            P("wide", "narrow"),
            P("wide", "narrow"),
            P("wide", "narrow"),
            P("wide", "narrow"),
            P("wide", "narrow"),
            P("wide", "narrow"),
            P("wide", "narrow"),
            P("wide", "narrow"),
            P("wide", "narrow"),
            P("wide", "narrow"),
            P("wide", "narrow"),
            P("wide", "narrow"),
            P("wide", "narrow"),
            P("wide", "narrow"),
            P("wide", "narrow"),
            P("wide", "narrow"),
            P("wide", None),
            P("wide", None),
            P("wide", None),
            P("wide", None),
            P(None, "narrow"),
            P(None, "narrow"),
            P(None, "narrow"),
            P(None, "narrow"),
            P("narrow"),
            P("narrow"),
            P("narrow"),
            P("narrow"),
            P("narrow"),
            P("narrow"),
            P("narrow"),
            P("narrow"),
            P("wide", None, "narrow"),
            P("wide", None, "narrow"),
            P("wide", None, "narrow"),
            P("wide", None, "narrow"),
            P("wide", None, "narrow"),
            P("wide", None, "narrow"),
        ),
        check_vma=False,
    )
```

```python
import functools

import jax
import jax.numpy as jnp
from jax import lax
from jax.experimental import pallas as pl
from jax.experimental.pallas import tpu as pltpu
from jax.sharding import PartitionSpec as P

D = 2560
NOPE = 64
ROPE = 32
VH = 64
QR = 768
KVR = 256
SLAB = 64
BASIS = 128


norm_eps = 1e-05
residual_scale = 1.4 / 62**0.5
beta_one = 0.9
beta_two = 0.95
adam_eps = 1e-08
gain_rate = 0.5
masked_value = -1e30
bf16 = jnp.bfloat16
f32 = jnp.float32


def product(left_side, right_side):
    return jnp.dot(left_side, right_side, preferred_element_type=jnp.float32)


def inner_rows(left_side, right_side):
    return lax.dot_general(
        left_side, right_side, (((0,), (0,)), ((), ())), preferred_element_type=jnp.float32
    )


def against_rows(left_side, right_side):
    return lax.dot_general(
        left_side, right_side, (((1,), (1,)), ((), ())), preferred_element_type=jnp.float32
    )


def rope_tables(positions):
    half_width = ROPE // 2
    frequency = 10000.0 ** (-2.0 * jnp.arange(half_width, dtype=jnp.float32) / ROPE)
    angles = positions.astype(jnp.float32)[:, None] * frequency[None, :]
    return (jnp.cos(angles), jnp.sin(angles))


def rotate(block_in, cosine_table, sine_table, direction_sign):
    half_width = block_in.shape[-1] // 2
    lower_half = block_in[..., :half_width]
    upper_half = block_in[..., half_width:]
    signed_sine = direction_sign * sine_table
    return jnp.concatenate(
        [
            lower_half * cosine_table - upper_half * signed_sine,
            upper_half * cosine_table + lower_half * signed_sine,
        ],
        axis=-1,
    )


def plain_adam(gradient, moment, square, step_rate, tcount):
    new_moment = beta_one * moment + (1.0 - beta_one) * gradient
    new_square = beta_two * square + (1.0 - beta_two) * gradient * gradient
    direction = (
        new_moment
        / (1.0 - beta_one**tcount)
        / (jnp.sqrt(new_square / (1.0 - beta_two**tcount)) + adam_eps)
    )
    return (-step_rate * direction, new_moment, new_square)


def shifted(value, step):
    count = lax.axis_size("narrow")
    return lax.ppermute(value, "narrow", [(i, (i + step) % count) for i in range(count)])


def flipped(value, bit):
    count = lax.axis_size("wide")
    return lax.ppermute(value, "wide", [(i, i ^ bit) for i in range(count)])


def along_line(value, pairs):
    return lax.ppermute(value, "narrow", pairs)


pairs_next = [(0, 1), (1, 0), (2, 3), (3, 2)]
pairs_second = [(0, 2), (2, 0), (1, 3), (3, 1)]
pairs_inner = [(1, 2), (2, 1)]
pairs_outward = [(1, 0), (2, 3)]
pairs_inward = [(0, 1), (3, 2)]


def gather_features(features, hold=None):
    count = lax.axis_size("narrow")
    index = lax.axis_index("narrow")
    width = features.shape[1]
    second = along_line(features, pairs_second)
    near = along_line(features, pairs_next)
    inner = along_line(features, pairs_inner)
    if hold is not None:
        second, hold = tie(second, hold)
    outer = along_line(second, pairs_outward)
    third = jnp.where((index == 1) | (index == 2), inner, outer)
    parts = [features, near, second, third]
    places = [index ^ step for step in range(count)]
    joined = jnp.zeros((features.shape[0], count * width), features.dtype)
    for place, part in zip(places, parts):
        joined = lax.dynamic_update_slice(joined, part, (0, place * width))
    return joined if hold is None else (joined, hold)


def line_piece(features, place):
    width = features.shape[1] // lax.axis_size("narrow")
    return lax.dynamic_slice_in_dim(features, place * width, width, 1)


def reduce_start(features):
    index = lax.axis_index("narrow")
    far = line_piece(features, index ^ 3)
    passed = along_line(far, pairs_inward)
    inner = along_line(far, pairs_inner)
    near = along_line(line_piece(features, index ^ 1), pairs_next)
    return passed, inner, near


def reduce_relay(features, passed):
    index = lax.axis_index("narrow")
    return (line_piece(features, index ^ 2).astype(f32) + passed.astype(f32)).astype(bf16)


def reduce_end(features, arrived):
    index = lax.axis_index("narrow")
    total = line_piece(features, index).astype(f32)
    for part in arrived:
        total = total + part.astype(f32)
    return total


def reduce_features(features):
    passed, inner, near = reduce_start(features)
    second = along_line(reduce_relay(features, passed), pairs_second)
    return reduce_end(features, (inner, near, second))


def gather_small(values):
    count = lax.axis_size("narrow")
    index = lax.axis_index("narrow")
    joined = jnp.zeros((count, values.shape[0]), values.dtype)
    for step in range(count):
        part = shifted(values, step) if step else values
        joined = lax.dynamic_update_slice(joined, part[None], ((index - step) % count, 0))
    return joined


def tie(*values):
    return lax.optimization_barrier(values)


def wide_totals(values):
    bit = 1
    while bit < lax.axis_size("wide"):
        values = values + flipped(values, bit)
        bit *= 2
    return values


def row_parts(values):
    return [values] + [shifted(values, step) for step in range(1, lax.axis_size("narrow"))]


def row_totals(values):
    count = lax.axis_size("narrow")
    return values + sum(shifted(values, step) for step in range(1, count))


def halving_orders(count):
    bits = list(range(1, count.bit_length() - 1))
    middle = len(bits) // 2
    return [bits, bits[middle:] + bits[:middle]]


def chunk_rows(features):
    count = lax.axis_size("wide")
    tokens, width = features.shape
    places = []
    for core in (1, 0):
        for half, order in enumerate(halving_orders(count)):
            chunks = [core]
            for bit in reversed(order):
                chunks = chunks + [chunk | (1 << bit) for chunk in chunks]
            places.append([(chunk, half) for chunk in chunks])
    chunks = jnp.array([chunk for group in places for chunk, _ in group], jnp.int32)
    halves = jnp.array([half for group in places for _, half in group], jnp.int32)
    pieces = features.T.reshape(2 * count, width // (2 * count), tokens)
    order = 2 * (lax.axis_index("wide") ^ chunks) + halves
    rows = jnp.take(pieces, order, axis=0, mode="clip").reshape(width, tokens)
    return rows[: width // 2], rows[width // 2 :]


def halves_of(rows):
    half = rows.shape[0] // 2
    return rows[:half], rows[half:]


def summed(values):
    total = values[0].astype(f32)
    for value in values[1:]:
        total = total + value.astype(f32)
    return total


def add_kernel(sizes, rows, *refs):
    outs = refs[sum(sizes) :]
    begin = 0
    for group, size in enumerate(sizes):
        columns = outs[0].shape[1]
        total = summed([ref[:, :columns] for ref in refs[begin : begin + size]])
        begin += size
        if len(outs) == 1:
            outs[0][group * rows : (group + 1) * rows, :] = total.astype(outs[0].dtype)
        else:
            outs[group][...] = total.astype(outs[group].dtype)


def add_rows(groups, place, rows, joined, kept):
    columns = groups[0][0].shape[1]
    start = place * rows
    if rows % 16:
        totals = [summed([part[start : start + rows] for part in parts]) for parts in groups]
        if joined:
            return jnp.concatenate(totals, axis=0)[:, :kept]
        return [total.astype(bf16) for total in totals]
    steps = 1 if joined or rows % 32 else 2
    block = rows // steps
    source = pl.BlockSpec((block, columns), lambda step: (place * steps + step, 0))
    if joined:
        out_specs = [pl.BlockSpec((len(groups) * rows, kept), lambda step: (0, 0))]
        out_shape = [jax.ShapeDtypeStruct((len(groups) * rows, kept), f32)]
    else:
        out_specs = [pl.BlockSpec((block, columns), lambda step: (step, 0))] * len(groups)
        out_shape = [jax.ShapeDtypeStruct((rows, columns), bf16)] * len(groups)
    outs = pl.pallas_call(
        functools.partial(add_kernel, [len(parts) for parts in groups], block),
        grid=(steps,),
        in_specs=[source] * sum(len(parts) for parts in groups),
        out_specs=out_specs,
        out_shape=out_shape,
        compiler_params=pltpu.CompilerParams(vmem_limit_bytes=48 * 1024 * 1024),
    )(*[part for parts in groups for part in parts])
    return outs[0] if joined else list(outs)


class Scatter:
    def __init__(self, products):
        near, away = products[:2], products[2:]
        self.orders = halving_orders(lax.axis_size("wide"))
        self.parts = [[own, flipped(sent, 1)] for own, sent in zip(near, away)]
        self.rows = near[0].shape[0]
        self.stage = 0

    def outgoing(self):
        return add_rows(self.parts, 1, self.rows // 2, False, None)

    def send(self, sending):
        for at, value in enumerate(sending):
            bit = 1 << self.orders[at][self.stage]
            self.parts[at] = self.parts[at] + [flipped(value, bit)]
        self.rows //= 2
        self.stage += 1

    def step(self):
        self.send(self.outgoing())

    def finish(self, kept):
        while self.stage < len(self.orders[0]):
            self.step()
        return add_rows(self.parts, 0, self.rows, True, kept)


def chunk_kernel(order_ref, left_ref, right_ref, near_a, near_b, away_a, away_b, whole_ref):
    core = order_ref[2 * pl.num_programs(0)]
    rows = near_a.shape[0]
    whole_ref[...] = inner_rows(left_ref[...], right_ref[...])
    near = pl.multiple_of(core * 2 * rows, 2 * rows)
    away = pl.multiple_of((1 - core) * 2 * rows, 2 * rows)
    columns = whole_ref.shape[1]
    for out, start in ((near_a, near), (near_b, near + rows), (away_a, away), (away_b, away + rows)):
        out[:, :columns] = whole_ref[pl.ds(start, rows), :].astype(bf16)
        if out.shape[1] > columns:
            out[:, columns:] = jnp.zeros((rows, out.shape[1] - columns), bf16)


def chunk_places(count):
    table = []
    for order in halving_orders(count):
        chips = [0]
        for bit in reversed(order):
            chips = chips + [chip | (1 << (bit - 1)) for chip in chips]
        table.append([chips.index(chip) for chip in range(count // 2)])
    return table


def chunk_products(left, right):
    count = lax.axis_size("wide")
    tokens, width = left.shape
    columns = right.shape[1]
    chips = count // 2
    group = width // chips
    rows = group // 4
    if group % 128 or rows % 16:
        away, near = [product(part, right).astype(bf16) for part in chunk_rows(left)]
        return [*halves_of(near), *halves_of(away)]
    index = lax.axis_index("wide")
    relative = (index // 2) ^ jnp.arange(chips, dtype=jnp.int32)
    order = jnp.concatenate(
        [jnp.array(table, jnp.int32)[relative] for table in chunk_places(count)]
        + [(index % 2)[None]]
    ).astype(jnp.int32)
    padded = -(-columns // 128) * 128
    first = pl.BlockSpec((rows, padded), lambda step, at: (at[step], 0))
    last = pl.BlockSpec((rows, padded), lambda step, at: (at[pl.num_programs(0) + step], 0))
    return list(
        pl.pallas_call(
            chunk_kernel,
            grid_spec=pltpu.PrefetchScalarGridSpec(
                num_scalar_prefetch=1,
                grid=(chips,),
                in_specs=[
                    pl.BlockSpec((tokens, group), lambda step, at: (0, step)),
                    pl.BlockSpec((tokens, columns), lambda step, at: (0, 0)),
                ],
                out_specs=[first, last, first, last],
                scratch_shapes=[pltpu.VMEM((group, columns), f32)],
            ),
            out_shape=[jax.ShapeDtypeStruct((chips * rows, padded), bf16)] * 4,
            compiler_params=pltpu.CompilerParams(vmem_limit_bytes=48 * 1024 * 1024),
        )(order, left, right)
    )


def weight_kernel(left_ref, right_ref, out_ref):
    out_ref[...] = inner_rows(left_ref[...], right_ref[...]).astype(bf16)


def weight_product(left, right):
    tokens, width = left.shape
    columns = right.shape[1]
    group = width // 4
    if group % 128:
        return inner_rows(left, right).astype(bf16)
    return pl.pallas_call(
        weight_kernel,
        grid=(4,),
        in_specs=[
            pl.BlockSpec((tokens, group), lambda step: (0, step)),
            pl.BlockSpec((tokens, columns), lambda step: (0, 0)),
        ],
        out_specs=pl.BlockSpec((group, columns), lambda step: (step, 0)),
        out_shape=jax.ShapeDtypeStruct((width, columns), bf16),
        compiler_params=pltpu.CompilerParams(vmem_limit_bytes=48 * 1024 * 1024),
    )(left, right)


def scatter_rows(partial):
    return lax.psum_scatter(partial, "wide", scatter_dimension=0, tiled=True)


def pack_kernel(send_ref, *refs):
    count = len(refs) - 3
    blocks, outs, turned = refs[:count], refs[count : count + 2], refs[-1]
    begin = 0
    for block in blocks:
        width = block.shape[1]
        turned[begin : begin + width, :] = block[...].astype(f32).T.astype(bf16)
        begin += width
    capacity = outs[0].shape[1] + outs[1].shape[1]
    for out, offset in zip(outs, (0, outs[0].shape[1])):
        slots = out.shape[1]

        def place(step, carry, out=out, offset=offset, slots=slots):
            owner = step // slots
            slot = step % slots
            unit = send_ref[owner * capacity + offset + slot]
            out[owner, slot] = turned[pl.ds(pl.multiple_of(unit * SLAB, SLAB), SLAB), :]
            return carry

        lax.fori_loop(0, out.shape[0] * slots, place, 0)


def pack_units(send, blocks, count, sizes):
    rows = blocks[0].shape[0]
    total = sum(block.shape[1] for block in blocks)
    vmem = pl.BlockSpec(memory_space=pltpu.VMEM)
    return pl.pallas_call(
        pack_kernel,
        in_specs=[pl.BlockSpec(memory_space=pltpu.SMEM)] + [vmem] * len(blocks),
        out_specs=[vmem] * 2,
        out_shape=[jax.ShapeDtypeStruct((count, size, SLAB, rows), bf16) for size in sizes],
        scratch_shapes=[pltpu.VMEM((total, rows), bf16)],
        compiler_params=pltpu.CompilerParams(vmem_limit_bytes=56 * 1024 * 1024),
    )(send, *blocks)


def unpack_kernel(back_ref, first_ref, last_ref, *refs):
    count = (len(refs) - 1) // 2
    weights, outs, turned = refs[:count], refs[count : 2 * count], refs[-1]
    first = first_ref.shape[1]
    capacity = first + last_ref.shape[1]

    def place(unit, carry):
        slot = back_ref[unit]
        owner = slot // capacity
        at = slot % capacity
        rows = pl.ds(pl.multiple_of(unit * SLAB, SLAB), SLAB)

        @pl.when(at < first)
        def _():
            turned[rows, :] = first_ref[owner, at]

        @pl.when(at >= first)
        def _():
            turned[rows, :] = last_ref[owner, at - first]

        return carry

    lax.fori_loop(0, turned.shape[0] // SLAB, place, 0)
    begin = 0
    for weight, out in zip(weights, outs):
        width = out.shape[1]
        steps = turned[begin : begin + width, :].astype(f32).T
        out[...] = weight[...].astype(f32) + steps
        begin += width


def unpack_units(back, first, last, weights):
    rows = first.shape[3]
    total = sum(weight.shape[1] for weight in weights)
    vmem = pl.BlockSpec(memory_space=pltpu.VMEM)
    return pl.pallas_call(
        unpack_kernel,
        in_specs=[pl.BlockSpec(memory_space=pltpu.SMEM)] + [vmem] * (2 + len(weights)),
        out_specs=[vmem] * len(weights),
        out_shape=[jax.ShapeDtypeStruct(weight.shape, f32) for weight in weights],
        scratch_shapes=[pltpu.VMEM((total, rows), bf16)],
        compiler_params=pltpu.CompilerParams(vmem_limit_bytes=56 * 1024 * 1024),
    )(back, first, last, *weights)


def unit_rates(col_widths, rates):
    return jnp.concatenate(
        [
            jnp.full((col_width // SLAB,), step_rate, jnp.float32)
            for col_width, step_rate in zip(col_widths, rates)
        ]
    )


def rotated_step(gradient, left_ref, right_ref, moment_ref, square_ref, new_moment_ref,
                 new_square_ref, turned_ref, occupied, first_scale, second_scale):
    blocks = left_ref.shape[1] // BASIS
    right_basis = right_ref[0].astype(bf16)
    turned_ref[...] = lax.dot_general(
        right_basis, gradient, (((0,), (0,)), ((), ())), preferred_element_type=f32
    )
    for block in range(blocks):
        at = slice(block * BASIS, (block + 1) * BASIS)
        left_basis = left_ref[0, at, :].astype(bf16)
        turned = jnp.dot(turned_ref[:, at].astype(bf16), left_basis, preferred_element_type=f32)
        moment = moment_ref[0, :, at]
        square = square_ref[0, :, at]
        new_moment = beta_one * moment + (1.0 - beta_one) * turned
        new_square = beta_two * square + (1.0 - beta_two) * turned * turned
        new_moment_ref[0, :, at] = jnp.where(occupied > 0.5, new_moment, moment)
        new_square_ref[0, :, at] = jnp.where(occupied > 0.5, new_square, square)
        direction = new_moment * first_scale / (jnp.sqrt(new_square * second_scale) + adam_eps)
        turned_ref[:, at] = lax.dot_general(
            direction.astype(bf16), left_basis, (((1,), (1,)), ((), ())),
            preferred_element_type=f32,
        )
    return jnp.dot(right_basis, turned_ref[...].astype(bf16), preferred_element_type=f32)


def slot_kernel(place_ref, scale_ref, gradient_ref, left_ref, right_ref, moment_ref, square_ref,
                change_ref, new_moment_ref, new_square_ref, whole_ref, turned_ref):
    step = pl.program_id(0)
    steps = pl.num_programs(0)
    sources, rows = gradient_ref.shape[0], gradient_ref.shape[3]
    rate = scale_ref[step]
    occupied = scale_ref[steps + step]

    @pl.when(occupied > 0.5)
    def _():
        for source in range(sources):
            whole_ref[:, source * rows : (source + 1) * rows] = gradient_ref[source, 0].astype(f32)
        whole_ref[...] = rate * rotated_step(
            whole_ref[...].astype(bf16), left_ref, right_ref, moment_ref, square_ref,
            new_moment_ref, new_square_ref, turned_ref, occupied,
            scale_ref[2 * steps], scale_ref[2 * steps + 1],
        )
        for source in range(sources):
            change_ref[source, 0] = whole_ref[:, source * rows : (source + 1) * rows].astype(bf16)

    @pl.when(occupied <= 0.5)
    def _():
        change_ref[...] = jnp.zeros_like(change_ref)

    @pl.when(jnp.logical_and(occupied <= 0.5, place_ref[steps + step] > 0))
    def _():
        new_moment_ref[...] = moment_ref[...]
        new_square_ref[...] = square_ref[...]


def slot_call(places, scales, gradient, left_basis, right_basis, moment, square, written):
    sources, steps, _, rows = gradient.shape
    row_count = sources * rows
    moment = moment.transpose(0, 2, 1)
    square = square.transpose(0, 2, 1)
    state = pl.BlockSpec((1, SLAB, row_count), lambda step, place: (place[step], 0, 0))
    traded = pl.BlockSpec((sources, 1, SLAB, rows), lambda step, place: (0, step, 0, 0))
    operands = [places, scales, gradient, left_basis, right_basis, moment, square]
    in_specs = [
        pl.BlockSpec(memory_space=pltpu.SMEM),
        traded,
        pl.BlockSpec((1, row_count, BASIS), lambda step, place: (place[step], 0, 0)),
        pl.BlockSpec((1, SLAB, SLAB), lambda step, place: (place[step], 0, 0)),
        state,
        state,
    ]
    aliases = {}
    kernel = slot_kernel
    if written == "same":
        aliases = {5: 1, 6: 2}
    elif written is not None:
        operands += [value.transpose(0, 2, 1) for value in written]
        in_specs += [pl.BlockSpec(memory_space=pl.ANY)] * 2
        aliases = {7: 1, 8: 2}

        def kernel(*refs):
            slot_kernel(*refs[:7], *refs[9:])

    change, new_moment, new_square = pl.pallas_call(
        kernel,
        grid_spec=pltpu.PrefetchScalarGridSpec(
            num_scalar_prefetch=1,
            grid=(steps,),
            in_specs=in_specs,
            out_specs=[traded, state, state],
            scratch_shapes=[
                pltpu.VMEM((SLAB, row_count), f32),
                pltpu.VMEM((SLAB, row_count), f32),
            ],
        ),
        out_shape=[
            jax.ShapeDtypeStruct(gradient.shape, bf16),
            jax.ShapeDtypeStruct(moment.shape, f32),
            jax.ShapeDtypeStruct(square.shape, f32),
        ],
        input_output_aliases=aliases,
        compiler_params=pltpu.CompilerParams(vmem_limit_bytes=48 * 1024 * 1024),
    )(*operands)
    return change, new_moment.transpose(0, 2, 1), new_square.transpose(0, 2, 1)


def slot_group(scales, gradient, left_basis, right_basis, moment, square, group, written):
    capacity = moment.shape[0]
    count = group.stop - group.start
    places = jnp.concatenate(
        [
            jnp.arange(group.start, group.stop, dtype=jnp.int32),
            jnp.ones((count,), jnp.int32),
        ]
    )
    scales = jnp.concatenate(
        [
            scales[group],
            scales[capacity + group.start : capacity + group.stop],
            scales[2 * capacity :],
        ]
    )
    return slot_call(places, scales, gradient, left_basis, right_basis, moment, square, written)


def all_slots(scales, gradient, left_basis, right_basis, moment, square):
    group = slice(0, moment.shape[0])
    return slot_group(
        scales, gradient, left_basis, right_basis, moment, square, group, None
    )


def late_steps(places, scales, gradient, left_basis, right_basis, moment, square):
    return slot_call(places, scales, gradient, left_basis, right_basis, moment, square, "same")


def correction_scales(tcount):
    return jnp.stack([1.0 / (1.0 - beta_one**tcount), 1.0 / (1.0 - beta_two**tcount)])


def slot_scales(owners, rates, capacity, wide_index, tcount):
    slot_ids = wide_index * capacity + jnp.arange(capacity, dtype=jnp.int32)
    own = (owners[None, :] == slot_ids[:, None]).astype(f32)
    return jnp.concatenate(
        [
            -jnp.sum(own * rates[None, :], axis=1),
            jnp.sum(own, axis=1),
            correction_scales(tcount),
        ]
    )


def ranks_within(owners, capacity):
    device = owners // capacity
    units = owners.shape[0]
    earlier = jnp.arange(units)[None, :] < jnp.arange(units)[:, None]
    return jnp.sum(
        jnp.where(earlier & (device[None, :] == device[:, None]), 1, 0).astype(jnp.int32), axis=1
    )


def turned_lanes(value, tables, sign):
    near = pltpu.roll(value, 112, 1) * tables[1]
    far = pltpu.roll(value, 16, 1) * tables[2]
    return value * tables[0] + sign * (near + far)


def lane_ids(shape):
    return lax.broadcasted_iota(jnp.int32, shape, 1)


def head_inputs(head, query_ref, key_value_ref, rotary_ref, tables, bias_ref):
    at = slice(head * 128, (head + 1) * 128)
    query = turned_lanes(query_ref[:, at], tables, 1.0).astype(bf16)
    key_value = key_value_ref[:, at].astype(bf16)
    key = jnp.where(lane_ids(key_value.shape) < NOPE, key_value, rotary_ref[...])
    scores = against_rows(query, key) * (NOPE + ROPE) ** (-0.5) + bias_ref[...]
    exp_scores = jnp.exp(scores - jnp.max(scores, axis=1, keepdims=True))
    probs = exp_scores / jnp.sum(exp_scores, axis=1, keepdims=True)
    return query, key_value, key, probs


def attend_kernel(query_ref, key_value_ref, rotary_ref, table_ref, bias_ref, out_ref):
    tables = [table_ref[at] for at in range(3)]
    mixed = []
    for head in range(2):
        _, key_value, _, probs = head_inputs(
            head, query_ref, key_value_ref, rotary_ref, tables, bias_ref
        )
        mixed.append(product(probs.astype(bf16), key_value))
    lower = pltpu.roll(mixed[0], 64, 1)
    out_ref[...] = jnp.where(lane_ids(lower.shape) < VH, lower, mixed[1]).astype(bf16)


def attend_back_kernel(query_ref, key_value_ref, rotary_ref, table_ref, bias_ref, grad_ref,
                       query_grad_ref, key_value_grad_ref, sums_ref):
    tables = [table_ref[at] for at in range(3)]
    scale = (NOPE + ROPE) ** (-0.5)

    @pl.when(pl.program_id(0) == 0)
    def _():
        sums_ref[...] = jnp.zeros_like(sums_ref)

    for head in range(2):
        at = slice(head * 128, (head + 1) * 128)
        query, key_value, key, probs = head_inputs(
            head, query_ref, key_value_ref, rotary_ref, tables, bias_ref
        )
        grad = grad_ref[...].astype(f32)
        lanes = lane_ids(grad.shape)
        if head == 0:
            grad = pltpu.roll(grad, 64, 1)
        grad = jnp.where(lanes < NOPE, 0.0, grad).astype(bf16)
        value_grad = inner_rows(probs.astype(bf16), grad)
        prob_grad = against_rows(grad, key_value)
        delta = jnp.sum(probs * prob_grad, axis=1, keepdims=True)
        score_grad = (probs * (prob_grad - delta)).astype(bf16)
        query_grad = turned_lanes(scale * product(score_grad, key), tables, -1.0).astype(bf16)
        key_grad = scale * inner_rows(score_grad, query)
        key_value_grad = jnp.where(lanes < NOPE, key_grad, value_grad).astype(bf16)
        query_grad_ref[:, at] = query_grad
        key_value_grad_ref[:, at] = key_value_grad
        sums_ref[0] += query_grad.astype(f32) * query_ref[:, at]
        sums_ref[1] += key_value_grad.astype(f32) * key_value_ref[:, at]
        sums_ref[2] += key_grad


def attend_specs(tokens):
    pair = pl.BlockSpec((tokens, 256), lambda step: (0, step))
    single = pl.BlockSpec((tokens, 128), lambda step: (0, step))
    shared = pl.BlockSpec((tokens, 128), lambda step: (0, 0))
    tables = pl.BlockSpec((3, tokens, 128), lambda step: (0, 0, 0))
    bias = pl.BlockSpec((tokens, tokens), lambda step: (0, 0))
    return pair, single, shared, tables, bias


def attend(queries, keys_values, rotary, tables, bias):
    tokens, width = queries.shape
    pair, single, shared, table_spec, bias_spec = attend_specs(tokens)
    return pl.pallas_call(
        attend_kernel,
        grid=(width // 256,),
        in_specs=[pair, pair, shared, table_spec, bias_spec],
        out_specs=single,
        out_shape=jax.ShapeDtypeStruct((tokens, width // 2), bf16),
        compiler_params=pltpu.CompilerParams(vmem_limit_bytes=48 * 1024 * 1024),
    )(queries, keys_values, rotary, tables, bias)


def attend_back(queries, keys_values, rotary, tables, bias, grad):
    tokens, width = queries.shape
    pair, single, shared, table_spec, bias_spec = attend_specs(tokens)
    return pl.pallas_call(
        attend_back_kernel,
        grid=(width // 256,),
        in_specs=[pair, pair, shared, table_spec, bias_spec, single],
        out_specs=[pair, pair, table_spec],
        out_shape=[
            jax.ShapeDtypeStruct((tokens, width), bf16),
            jax.ShapeDtypeStruct((tokens, width), bf16),
            jax.ShapeDtypeStruct((3, tokens, 128), f32),
        ],
        compiler_params=pltpu.CompilerParams(vmem_limit_bytes=48 * 1024 * 1024),
    )(queries, keys_values, rotary, tables, bias, grad)


def routes(owners, capacity, room, wide_count):
    units = owners.shape[0]
    if room == capacity:
        places = owners
    else:
        places = owners // capacity * room + ranks_within(owners, capacity)
    slots = jnp.arange(wide_count * room, dtype=jnp.int32)
    matches = slots[:, None] == places[None, :]
    unit_of = jnp.sum(
        jnp.where(matches, jnp.arange(units, dtype=jnp.int32)[None, :], 0), axis=1
    )
    return jnp.minimum(unit_of, units - 1), places


def late_places(owners, rates, capacity, room, wide_index, tcount):
    ranks = ranks_within(owners, capacity)
    mine = owners // capacity == wide_index
    own = mine[None, :] & (ranks[None, :] == jnp.arange(room, dtype=jnp.int32)[:, None])
    slot = jnp.sum(jnp.where(own, (owners % capacity)[None, :], 0), axis=1)
    filled = jnp.sum(own.astype(jnp.int32), axis=1)
    last = jnp.maximum(jnp.sum(filled) - 1, 0)
    last_slot = jnp.sum(jnp.where(jnp.arange(room) == last, slot, 0))
    places = jnp.where(filled > 0, slot, last_slot)
    untouched = jnp.where((jnp.arange(room) == 0) & (filled == 0), 1, 0)
    scales = jnp.concatenate(
        [
            -jnp.sum(own.astype(f32) * rates[None, :], axis=1),
            filled.astype(f32),
            correction_scales(tcount),
        ]
    )
    return jnp.concatenate([places, untouched]).astype(jnp.int32), scales


def unit_rows(blocks):
    joined = jnp.concatenate([block.T for block in blocks], axis=0).astype(bf16)
    return joined.reshape(-1, SLAB, joined.shape[1])


def unit_columns(units, blocks):
    joined = units.reshape(-1, units.shape[2])
    pieces, begin = ([], 0)
    for block in blocks:
        pieces.append(joined[begin : begin + block.shape[1]].T.astype(f32))
        begin += block.shape[1]
    return pieces


def trade_joined(parts, count):
    steps = [part.shape[0] // count for part in parts]
    widths = [part.shape[2] for part in parts]
    room = max(steps)
    joined = jnp.concatenate(
        [
            jnp.pad(
                part.reshape(count, own, SLAB, width), ((0, 0), (0, room - own), (0, 0), (0, 0))
            )
            for part, own, width in zip(parts, steps, widths)
        ],
        axis=3,
    )
    traded = lax.all_to_all(joined, "wide", split_axis=0, concat_axis=0, tiled=True)
    pieces, begin = ([], 0)
    for own, width in zip(steps, widths):
        pieces.append(traded[:, :own, :, begin : begin + width])
        begin += width
    return pieces


def body(
    x_in,
    grad_out,
    w_qa,
    w_kv,
    w_kr,
    w_qb,
    w_kvb,
    w_o,
    w_gate,
    w_up,
    w_down,
    norm_gains,
    q_gain,
    kv_gain,
    deal,
    lengths,
    step_count,
    owner_a,
    owner_b,
    owner_c,
    basis_la,
    basis_ra,
    basis_lb,
    basis_rb,
    basis_lc,
    basis_rc,
    mom_a,
    sq_a,
    mom_b,
    sq_b,
    mom_c,
    sq_c,
    kr_mom,
    kr_sq,
    gain_mom,
    gain_sq,
    qgain_mom,
    qgain_sq,
    kvgain_mom,
    kvgain_sq,
):
    wide_count = lax.axis_size("wide")
    wide_index = lax.axis_index("wide")
    narrow_index = lax.axis_index("narrow")
    row_count, local_width = x_in.shape
    piece_rows = row_count // wide_count
    deal_row = lax.dynamic_index_in_dim(deal, wide_index, 0, keepdims=False)
    wide_ids = jnp.arange(wide_count, dtype=jnp.int32)
    inverse = jnp.sum(
        jnp.where(deal_row[None, :] == wide_ids[:, None], wide_ids[None, :], 0), axis=1
    )

    def to_working(features):
        outgoing = jnp.take(
            features.reshape((wide_count, piece_rows) + features.shape[1:]), inverse, axis=0,
            mode="clip",
        )
        dealt = lax.all_to_all(outgoing, "wide", split_axis=0, concat_axis=0, tiled=True)
        return dealt.reshape(row_count, -1)

    token_in = to_working(x_in)
    residual = token_in.astype(f32)
    seq_lengths = lengths[0]
    seq_ends = jnp.cumsum(seq_lengths)
    row_ids = jnp.arange(row_count, dtype=jnp.int32)
    segment = jnp.sum((row_ids[:, None] >= seq_ends[None, :-1]).astype(jnp.int32), axis=1)
    pick = jnp.arange(seq_lengths.shape[0], dtype=jnp.int32)[None, :] == segment[:, None]
    seq_start = jnp.sum(jnp.where(pick, (seq_ends - seq_lengths)[None, :], 0), axis=1)
    live_rows = (segment < seq_lengths.shape[0] - 1).astype(f32)[:, None]
    cosine_table, sine_table = rope_tables(row_ids - seq_start)
    cos_heads = cosine_table[:, None, :]
    sin_heads = sine_table[:, None, :]

    latent_own = jnp.concatenate([w_qa, w_kv, w_kr], axis=1)
    heads_here = w_o.shape[1] // VH
    padded_qb = jnp.pad(
        w_qb.reshape(w_qb.shape[0], heads_here, NOPE + ROPE),
        ((0, 0), (0, 0), (0, 128 - NOPE - ROPE)),
    ).reshape(w_qb.shape[0], -1)
    full_latent = lax.all_gather(latent_own, "wide", axis=0, tiled=True)
    full_qb = lax.all_gather(padded_qb, "wide", axis=0, tiled=True)
    full_kvb = lax.all_gather(w_kvb, "wide", axis=0, tiled=True)
    full_o = lax.all_gather(w_o, "wide", axis=0, tiled=True)
    full_gate = lax.all_gather(w_gate, "wide", axis=0, tiled=True)
    full_up = lax.all_gather(w_up, "wide", axis=0, tiled=True)
    full_down = lax.all_gather(w_down, "wide", axis=0, tiled=True)
    gains_all = gather_small(jnp.concatenate([norm_gains[0], norm_gains[1], q_gain, kv_gain]))
    first_gain = gains_all[:, :local_width].reshape(1, -1)
    second_gain = gains_all[:, local_width : 2 * local_width].reshape(1, -1)
    q_width = q_gain.shape[0]
    kv_width = kv_gain.shape[0]
    q_gain_all = gains_all[:, 2 * local_width : 2 * local_width + q_width].reshape(1, -1)
    kv_gain_all = gains_all[:, 2 * local_width + q_width :].reshape(1, -1)

    def inverse_rms(features, width):
        wide = features.astype(f32)
        return lax.rsqrt(jnp.sum(wide * wide, axis=1, keepdims=True) / width + norm_eps)

    token_all, full_latent = gather_features(token_in, full_latent)
    inv_first = inverse_rms(token_all, D)
    normed = (token_all.astype(f32) * inv_first * first_gain).astype(bf16)
    latents = product(normed, full_latent)
    q_latent = latents[:, :q_width]
    kv_latent = latents[:, q_width : q_width + kv_width]
    key_rot = latents[:, q_width + kv_width :]
    narrow_count = lax.axis_size("narrow")
    latents_all = gather_features(latents[:, : q_width + kv_width].astype(bf16))
    latents_all = latents_all.reshape(row_count, narrow_count, q_width + kv_width)
    q_latent_all = latents_all[:, :, :q_width].reshape(row_count, QR).astype(f32)
    kv_latent_all = latents_all[:, :, q_width:].reshape(row_count, KVR).astype(f32)
    inv_q = inverse_rms(q_latent_all, QR)
    inv_kv = inverse_rms(kv_latent_all, KVR)
    q_normed = (q_latent_all * inv_q * q_gain_all).astype(bf16)
    kv_normed = (kv_latent_all * inv_kv * kv_gain_all).astype(bf16)
    q_pre = product(q_normed, full_qb)
    kv_pre = product(kv_normed, full_kvb)
    key_turned = rotate(key_rot, cosine_table, sine_table, 1.0)
    rotary = jnp.pad(key_turned, ((0, 0), (NOPE, 128 - NOPE - ROPE))).astype(bf16)
    allowed = (segment[:, None] == segment[None, :]) & (row_ids[None, :] <= row_ids[:, None])
    bias = jnp.where(allowed, 0.0, masked_value).astype(f32)
    half_pads = ((NOPE, 128 - NOPE - ROPE // 2), (NOPE + ROPE // 2, 128 - NOPE - ROPE))

    def lane_table(lower, upper):
        return sum(
            jnp.pad(part, ((0, 0), pads)) for part, pads in zip((lower, upper), half_pads)
        )

    empty = jnp.zeros_like(sine_table)
    tables = jnp.stack(
        [
            lane_table(cosine_table, cosine_table)
            + jnp.where(jnp.arange(128) < NOPE, 1.0, 0.0)[None, :],
            lane_table(-sine_table, empty),
            lane_table(empty, sine_table),
        ]
    )
    latents_all, grad_out = tie(latents_all, grad_out)
    heads_out = attend(q_pre, kv_pre, rotary, tables, bias)
    grad_all, heads_out = gather_features(grad_out, heads_out)
    token_grad_all = to_working(grad_all)
    grad_top = lax.dynamic_slice_in_dim(
        token_grad_all, narrow_index * local_width, local_width, 1
    ).astype(f32)
    mlp_grad = (residual_scale * live_rows * token_grad_all.astype(f32)).astype(bf16)
    attn_out = reduce_features(against_rows(heads_out, full_o).astype(bf16))
    middle = residual + residual_scale * live_rows * attn_out
    middle_all = gather_features(middle.astype(bf16)).astype(f32)
    inv_second = inverse_rms(middle_all, D)
    normed_two = (middle_all * inv_second * second_gain).astype(bf16)
    gate_act = product(normed_two, full_gate)
    upward = product(normed_two, full_up)
    sigmoid_gate = jax.nn.sigmoid(gate_act)
    silu_gate = gate_act * sigmoid_gate
    active = (silu_gate * upward).astype(bf16)
    mlp_part = against_rows(active, full_down).astype(bf16)
    mlp_passed, mlp_inner, mlp_near = reduce_start(mlp_part)
    down_products = chunk_products(mlp_grad, active)
    active_grad = product(mlp_grad, full_down)
    gate_grad = (
        active_grad * upward * (sigmoid_gate + silu_gate * (1.0 - sigmoid_gate))
    ).astype(bf16)
    up_grad = (active_grad * silu_gate).astype(bf16)
    gate_grad, up_grad, down_products = tie(gate_grad, up_grad, down_products)
    down_sum = Scatter(down_products)
    normed_two_part = (
        against_rows(gate_grad, full_gate) + against_rows(up_grad, full_up)
    ).astype(bf16)
    passed, inner, near = reduce_start(normed_two_part)
    gate_products = chunk_products(normed_two, gate_grad)
    passed, gate_products, up_grad, down_sending = tie(
        passed, gate_products, up_grad, down_sum.outgoing()
    )
    down_sum.send(down_sending)
    gate_sum = Scatter(gate_products)
    relayed = reduce_relay(normed_two_part, passed)
    relayed, up_grad = tie(relayed, up_grad)
    second = along_line(relayed, pairs_second)
    up_sum = Scatter(chunk_products(normed_two, up_grad))
    second, up_sum.parts, gate_sending = tie(second, up_sum.parts, gate_sum.outgoing())
    gate_sum.send(gate_sending)
    normed_two_grad = reduce_end(normed_two_part, (inner, near, second))
    post_gain_grad = jnp.sum(normed_two_grad * middle * inv_second, axis=0)
    direct_grad = grad_top + inv_second * norm_gains[1] * normed_two_grad
    direct_all, sendings = gather_features(
        direct_grad.astype(bf16),
        (up_sum.outgoing(), down_sum.outgoing()),
    )
    direct_all = direct_all.astype(f32)
    top_all = token_grad_all.astype(f32)
    second_dot = jnp.sum((direct_all - top_all) * middle_all, axis=1, keepdims=True)
    attn_grad = (
        residual_scale
        * live_rows
        * (direct_all - middle_all * (inv_second**2 * second_dot / D))
    ).astype(bf16)
    middle_grad = direct_grad - middle * (inv_second**2 * second_dot / D)
    for weight_sum, sending in zip((up_sum, down_sum), sendings):
        weight_sum.send(sending)
    o_full = weight_product(attn_grad, heads_out)
    attn_grad, o_full, gate_sending = tie(attn_grad, o_full, gate_sum.outgoing())
    gate_sum.send(gate_sending)
    block_o = scatter_rows(o_full)
    mlp_passed, attn_grad = tie(mlp_passed, attn_grad)
    mlp_second = along_line(reduce_relay(mlp_part, mlp_passed), pairs_second)
    heads_grad = product(attn_grad, full_o).astype(bf16)

    q_pre_grad, kv_pre_grad, head_sums = attend_back(
        q_pre, kv_pre, rotary, tables, bias, heads_grad
    )
    mlp_arrived = (mlp_inner, mlp_near, mlp_second)
    head_sums, q_pre_grad, up_sending = tie(head_sums, q_pre_grad, up_sum.outgoing())
    up_sum.send(up_sending)
    rot_partial = rotate(
        head_sums[2, :, NOPE : NOPE + ROPE], cosine_table, sine_table, -1.0
    )
    q_dot = jnp.sum(head_sums[0], axis=1)
    kv_dot = jnp.sum(head_sums[1], axis=1)
    dots = row_parts(jnp.concatenate([jnp.stack([q_dot, kv_dot]), rot_partial.T], axis=0))
    q_part = against_rows(q_pre_grad, full_qb).astype(bf16)
    kv_part = against_rows(kv_pre_grad, full_kvb).astype(bf16)
    both_part = jnp.concatenate(
        [
            q_part.reshape(row_count, narrow_count, q_width),
            kv_part.reshape(row_count, narrow_count, kv_width),
        ],
        axis=-1,
    ).reshape(row_count, -1)
    passed, inner, near = reduce_start(both_part)
    tcount = step_count[0].astype(f32)
    wide_rate = D ** (-0.5)
    block_down = down_sum.finish(w_down.shape[1])
    block_gate = gate_sum.finish(w_gate.shape[1])
    block_up = up_sum.finish(w_up.shape[1])
    passed, q_pre_late, kv_pre_late, block_down, block_gate, block_up = tie(
        passed, q_pre_grad, kv_pre_grad, block_down, block_gate, block_up
    )
    main_blocks = [block_o, block_gate, block_up, block_down]
    late_blocks_widths = [q_width, kv_width]
    late_units = sum(late_blocks_widths) // SLAB
    main_rates = unit_rates(
        [block.shape[1] for block in main_blocks], [1.0, wide_rate, wide_rate, 0.125]
    )
    late_rates = unit_rates(late_blocks_widths, [wide_rate, wide_rate])
    late_owners, main_owners = owner_a[0, :late_units], owner_a[0, late_units:]
    capacity_a = mom_a.shape[0]
    main_send, main_back = routes(main_owners, capacity_a, capacity_a, wide_count)
    main_scales = slot_scales(main_owners, main_rates, capacity_a, wide_index, tcount)
    first_slots = (capacity_a + 1) // 2
    groups = [slice(0, first_slots), slice(first_slots, capacity_a)]
    main_sent = pack_units(
        main_send, main_blocks, wide_count, [group.stop - group.start for group in groups]
    )
    second = along_line(reduce_relay(both_part, passed), pairs_second)
    head_columns = w_kvb.shape[1]
    qb_full = inner_rows(q_normed, q_pre_late).astype(bf16)
    kvb_full = inner_rows(kv_normed, kv_pre_late).astype(bf16)
    head_products = jnp.concatenate(
        [
            qb_full.reshape(wide_count, -1, head_columns),
            kvb_full.reshape(wide_count, -1, head_columns),
        ],
        axis=1,
    ).reshape(-1, head_columns)
    second, dots, main_sent, head_products = tie(second, dots, main_sent, head_products)
    main_owned = [
        lax.all_to_all(part, "wide", split_axis=0, concat_axis=0, tiled=True)
        for part in main_sent
    ]
    dots = sum(dots).T
    q_dot, kv_dot = dots[:, :1], dots[:, 1:2]
    rot_grad = dots[:, 2:].astype(bf16)
    head_products, block_o = tie(head_products, block_o)
    block_heads = scatter_rows(head_products)
    both_grad = reduce_end(both_part, (inner, near, second))
    q_normed_grad = both_grad[:, :q_width]
    kv_normed_grad = both_grad[:, q_width:]
    q_gain_grad = jnp.sum(q_normed_grad * q_latent * inv_q, axis=0)
    kv_gain_grad = jnp.sum(kv_normed_grad * kv_latent * inv_kv, axis=0)
    q_latent_grad = (
        inv_q * q_gain * q_normed_grad - q_latent * inv_q**2 * q_dot / QR
    ).astype(bf16)
    kv_latent_grad = (
        inv_kv * kv_gain * kv_normed_grad - kv_latent * inv_kv**2 * kv_dot / KVR
    ).astype(bf16)
    first_dot = (
        norm_eps * (inv_q**2 * q_dot + inv_kv**2 * kv_dot)
        + jnp.sum(rot_grad.astype(f32) * key_rot, axis=1, keepdims=True)
    )
    latent_grad = jnp.concatenate([q_latent_grad, kv_latent_grad, rot_grad], axis=1)
    full_kr = full_latent[:, q_width + kv_width :]
    own_kr = lax.dynamic_slice_in_dim(full_kr, narrow_index * local_width, local_width, 0)
    normed_part = against_rows(
        latent_grad[:, : q_width + kv_width], full_latent[:, : q_width + kv_width]
    ).astype(bf16)
    normed_passed, normed_inner, normed_near = reduce_start(normed_part)
    latent_full = weight_product(normed, latent_grad)
    normed_passed, latent_full = tie(normed_passed, latent_full)
    latent_late, first_owned = tie(latent_full, main_owned[0])
    block_latent = scatter_rows(latent_late)
    normed_second = along_line(reduce_relay(normed_part, normed_passed), pairs_second)
    normed_second, first_owned, mlp_arrived = tie(normed_second, first_owned, mlp_arrived)
    mlp_out = reduce_end(mlp_part, mlp_arrived)
    layer_out = middle + residual_scale * live_rows * mlp_out
    normed_grad = reduce_end(normed_part, (normed_inner, normed_near, normed_second)) + (
        against_rows(rot_grad, own_kr)
    )
    in_gain_grad = jnp.sum(normed_grad * residual * inv_first, axis=0)
    input_grad = (
        middle_grad
        + inv_first * norm_gains[0] * normed_grad
        - residual * inv_first**2 * first_dot / D
    )
    gain_part = jnp.concatenate([in_gain_grad, post_gain_grad, q_gain_grad, kv_gain_grad])
    gain_high = lax.optimization_barrier(gain_part.astype(bf16))
    gain_low = (gain_part - gain_high.astype(f32)).astype(bf16)
    gain_rows = jnp.concatenate([gain_high, gain_low])
    gain_height = -(-gain_rows.shape[0] // local_width)
    gain_rows = jnp.pad(gain_rows, (0, gain_height * local_width - gain_rows.shape[0]))
    gain_rows = jnp.broadcast_to(
        gain_rows.reshape(1, gain_height, local_width), (wide_count, gain_height, local_width)
    )
    leaving = jnp.concatenate(
        [
            layer_out.astype(bf16).reshape(wide_count, piece_rows, local_width),
            input_grad.astype(bf16).reshape(wide_count, piece_rows, local_width),
            gain_rows,
        ],
        axis=1,
    )
    leaving, first_owned, last_owned = tie(leaving, first_owned, main_owned[1])
    returned_rows = lax.all_to_all(leaving, "wide", split_axis=0, concat_axis=0, tiled=True)
    change_one, mid_mom_a, mid_sq_a = slot_group(
        main_scales, first_owned, basis_la, basis_ra, mom_a, sq_a, groups[0], None
    )
    change_one, last_owned, returned_rows = tie(change_one, last_owned, returned_rows)
    back_one = lax.all_to_all(change_one, "wide", split_axis=0, concat_axis=0, tiled=True)

    change_two, mid_mom_a, mid_sq_a = slot_group(
        main_scales, last_owned, basis_la, basis_ra, mom_a, sq_a, groups[1],
        (mid_mom_a, mid_sq_a),
    )
    block_latent, block_heads, change_two = tie(block_latent, block_heads, change_two)
    block_qb = block_heads[: w_qb.shape[0]].reshape(w_qb.shape[0], heads_here, 128)
    block_qb = block_qb[:, :, : NOPE + ROPE].reshape(w_qb.shape)
    block_kvb = block_heads[w_qb.shape[0] :]
    block_qa = block_latent[:, :q_width]
    block_kv = block_latent[:, q_width : q_width + kv_width]
    block_kr = block_latent[:, q_width + kv_width :]
    late_blocks = [block_qa, block_kv]
    late_capacity = min(late_units, capacity_a)
    late_send, late_back = routes(late_owners, capacity_a, late_capacity, wide_count)
    late_slots, late_scales = late_places(
        late_owners, late_rates, capacity_a, late_capacity, wide_index, tcount
    )
    owners_b, owners_c = owner_b[0], owner_c[0]
    capacity_b, capacity_c = mom_b.shape[0], mom_c.shape[0]
    b_send, b_back = routes(owners_b, capacity_b, capacity_b, wide_count)
    c_send, c_back = routes(owners_c, capacity_c, capacity_c, wide_count)
    sent_parts = [
        jnp.take(unit_rows(blocks), send, axis=0, mode="clip")
        for blocks, send in (
            (late_blocks, late_send),
            ([block_qb], b_send),
            ([block_kvb], c_send),
        )
    ]
    sent_parts, back_one = tie(sent_parts, back_one)
    late_owned, owned_b, owned_c = trade_joined(sent_parts, wide_count)
    change_two, late_owned, owned_b, owned_c = tie(change_two, late_owned, owned_b, owned_c)
    back_two = lax.all_to_all(change_two, "wide", split_axis=0, concat_axis=0, tiled=True)

    placed = jnp.take(returned_rows[:, : 2 * piece_rows], deal_row, axis=0, mode="clip")
    final_out = placed[:, :piece_rows].astype(f32).reshape(row_count, local_width)
    final_grad = placed[:, piece_rows:].astype(f32).reshape(row_count, local_width)
    gain_rows = returned_rows[:, 2 * piece_rows :].reshape(wide_count, -1)
    gain_size = gain_part.shape[0]
    gain_grads = jnp.sum(gain_rows[:, :gain_size].astype(f32), axis=0) + jnp.sum(
        gain_rows[:, gain_size : 2 * gain_size].astype(f32), axis=0
    )
    gains_total = gain_grads[: 2 * local_width].reshape(2, local_width)
    qgain_total = gain_grads[2 * local_width : 2 * local_width + q_width]
    kvgain_total = gain_grads[2 * local_width + q_width :]
    late_change, new_mom_a, new_sq_a = late_steps(
        late_slots, late_scales, late_owned, basis_la, basis_ra, mid_mom_a, mid_sq_a
    )
    change_b, new_mom_b, new_sq_b = all_slots(
        slot_scales(owners_b, unit_rates([block_qb.shape[1]], [QR ** (-0.5)]), capacity_b,
                    wide_index, tcount),
        owned_b, basis_lb, basis_rb, mom_b, sq_b,
    )
    change_c, new_mom_c, new_sq_c = all_slots(
        slot_scales(owners_c, unit_rates([block_kvb.shape[1]], [KVR ** (-0.5)]), capacity_c,
                    wide_index, tcount),
        owned_c, basis_lc, basis_rc, mom_c, sq_c,
    )
    late_change, back_two = tie(late_change, back_two)
    returned = trade_joined(
        [change.reshape((-1,) + change.shape[2:]) for change in (late_change, change_b, change_c)],
        wide_count,
    )
    late_result, result_b, result_c = [
        jnp.take(part.reshape((-1,) + part.shape[2:]), back, axis=0, mode="clip")
        for part, back in zip(returned, (late_back, b_back, c_back))
    ]
    new_o, new_gate, new_up, new_down = unpack_units(
        main_back, back_one, back_two, [w_o, w_gate, w_up, w_down]
    )
    update_qa, update_kv = unit_columns(late_result, late_blocks)
    update_qb = unit_columns(result_b, [block_qb])[0]
    update_kvb = unit_columns(result_c, [block_kvb])[0]
    block_kr = block_kr.astype(f32)
    update_kr, new_kr_mom, new_kr_sq = plain_adam(block_kr, kr_mom, kr_sq, wide_rate, tcount)
    update_gains, new_gain_mom, new_gain_sq = plain_adam(
        gains_total, gain_mom, gain_sq, gain_rate, tcount
    )
    update_qgain, new_qgain_mom, new_qgain_sq = plain_adam(
        qgain_total, qgain_mom, qgain_sq, gain_rate, tcount
    )
    update_kvgain, new_kvgain_mom, new_kvgain_sq = plain_adam(
        kvgain_total, kvgain_mom, kvgain_sq, gain_rate, tcount
    )
    return (
        final_out,
        final_grad,
        block_qa.astype(f32),
        block_kv.astype(f32),
        block_qb.astype(f32),
        block_kvb.astype(f32),
        block_o.astype(f32),
        block_gate,
        block_up,
        block_down,
        w_qa.astype(f32) + update_qa,
        w_kv.astype(f32) + update_kv,
        w_qb.astype(f32) + update_qb,
        w_kvb.astype(f32) + update_kvb,
        new_o,
        new_gate,
        new_up,
        new_down,
        block_kr,
        w_kr.astype(f32) + update_kr,
        new_kr_mom,
        new_kr_sq,
        gains_total,
        norm_gains + update_gains,
        new_gain_mom,
        new_gain_sq,
        qgain_total,
        q_gain + update_qgain,
        new_qgain_mom,
        new_qgain_sq,
        kvgain_total,
        kv_gain + update_kvgain,
        new_kvgain_mom,
        new_kvgain_sq,
        new_mom_a,
        new_sq_a,
        new_mom_b,
        new_sq_b,
        new_mom_c,
        new_sq_c,
    )


def solution(mesh):
    return jax.shard_map(
        body,
        mesh=mesh,
        in_specs=(
            P("wide", "narrow"),
            P("wide", "narrow"),
            P("wide", "narrow"),
            P("wide", "narrow"),
            P("wide", None),
            P("wide", "narrow"),
            P("wide", "narrow"),
            P("wide", "narrow"),
            P("wide", "narrow"),
            P("wide", "narrow"),
            P("wide", "narrow"),
            P(None, "narrow"),
            P("narrow"),
            P("narrow"),
            P(),
            P("wide", None),
            P(),
            P("narrow", None),
            P("narrow", None),
            P("narrow", None),
            P("wide", None, "narrow"),
            P("wide", None, "narrow"),
            P("wide", None, "narrow"),
            P("wide", None, "narrow"),
            P("wide", None, "narrow"),
            P("wide", None, "narrow"),
            P("wide", None, "narrow"),
            P("wide", None, "narrow"),
            P("wide", None, "narrow"),
            P("wide", None, "narrow"),
            P("wide", None, "narrow"),
            P("wide", None, "narrow"),
            P("wide", None),
            P("wide", None),
            P(None, "narrow"),
            P(None, "narrow"),
            P("narrow"),
            P("narrow"),
            P("narrow"),
            P("narrow"),
        ),
        out_specs=(
            P("wide", "narrow"),
            P("wide", "narrow"),
            P("wide", "narrow"),
            P("wide", "narrow"),
            P("wide", "narrow"),
            P("wide", "narrow"),
            P("wide", "narrow"),
            P("wide", "narrow"),
            P("wide", "narrow"),
            P("wide", "narrow"),
            P("wide", "narrow"),
            P("wide", "narrow"),
            P("wide", "narrow"),
            P("wide", "narrow"),
            P("wide", "narrow"),
            P("wide", "narrow"),
            P("wide", "narrow"),
            P("wide", "narrow"),
            P("wide", None),
            P("wide", None),
            P("wide", None),
            P("wide", None),
            P(None, "narrow"),
            P(None, "narrow"),
            P(None, "narrow"),
            P(None, "narrow"),
            P("narrow"),
            P("narrow"),
            P("narrow"),
            P("narrow"),
            P("narrow"),
            P("narrow"),
            P("narrow"),
            P("narrow"),
            P("wide", None, "narrow"),
            P("wide", None, "narrow"),
            P("wide", None, "narrow"),
            P("wide", None, "narrow"),
            P("wide", None, "narrow"),
            P("wide", None, "narrow"),
        ),
        check_vma=False,
    )
```

```python
import functools

import jax
import jax.numpy as jnp
from jax import lax
from jax.experimental import pallas as pl
from jax.experimental.pallas import tpu as pltpu
from jax.sharding import PartitionSpec as P

D = 2560
NOPE = 64
ROPE = 32
VH = 64
QR = 768
KVR = 256
SLAB = 64
BASIS = 128


norm_eps = 1e-05
residual_scale = 1.4 / 62**0.5
beta_one = 0.9
beta_two = 0.95
adam_eps = 1e-08
gain_rate = 0.5
masked_value = -1e30
bf16 = jnp.bfloat16
f32 = jnp.float32


def product(left_side, right_side):
    return jnp.dot(left_side, right_side, preferred_element_type=jnp.float32)


def inner_rows(left_side, right_side):
    return lax.dot_general(
        left_side, right_side, (((0,), (0,)), ((), ())), preferred_element_type=jnp.float32
    )


def against_rows(left_side, right_side):
    return lax.dot_general(
        left_side, right_side, (((1,), (1,)), ((), ())), preferred_element_type=jnp.float32
    )


def rope_tables(positions):
    half_width = ROPE // 2
    frequency = 10000.0 ** (-2.0 * jnp.arange(half_width, dtype=jnp.float32) / ROPE)
    angles = positions.astype(jnp.float32)[:, None] * frequency[None, :]
    return (jnp.cos(angles), jnp.sin(angles))


def rotate(block_in, cosine_table, sine_table, direction_sign):
    half_width = block_in.shape[-1] // 2
    lower_half = block_in[..., :half_width]
    upper_half = block_in[..., half_width:]
    signed_sine = direction_sign * sine_table
    return jnp.concatenate(
        [
            lower_half * cosine_table - upper_half * signed_sine,
            upper_half * cosine_table + lower_half * signed_sine,
        ],
        axis=-1,
    )


def plain_adam(gradient, moment, square, step_rate, tcount):
    new_moment = beta_one * moment + (1.0 - beta_one) * gradient
    new_square = beta_two * square + (1.0 - beta_two) * gradient * gradient
    direction = (
        new_moment
        / (1.0 - beta_one**tcount)
        / (jnp.sqrt(new_square / (1.0 - beta_two**tcount)) + adam_eps)
    )
    return (-step_rate * direction, new_moment, new_square)


def shifted(value, step):
    count = lax.axis_size("narrow")
    return lax.ppermute(value, "narrow", [(i, (i + step) % count) for i in range(count)])


def flipped(value, bit):
    count = lax.axis_size("wide")
    return lax.ppermute(value, "wide", [(i, i ^ bit) for i in range(count)])


def along_line(value, pairs):
    return lax.ppermute(value, "narrow", pairs)


pairs_next = [(0, 1), (1, 0), (2, 3), (3, 2)]
pairs_second = [(0, 2), (2, 0), (1, 3), (3, 1)]
pairs_inner = [(1, 2), (2, 1)]
pairs_outward = [(1, 0), (2, 3)]
pairs_inward = [(0, 1), (3, 2)]


def gather_features(features, hold=None):
    count = lax.axis_size("narrow")
    index = lax.axis_index("narrow")
    width = features.shape[1]
    second = along_line(features, pairs_second)
    near = along_line(features, pairs_next)
    inner = along_line(features, pairs_inner)
    if hold is not None:
        second, hold = tie(second, hold)
    outer = along_line(second, pairs_outward)
    third = jnp.where((index == 1) | (index == 2), inner, outer)
    parts = [features, near, second, third]
    places = [index ^ step for step in range(count)]
    joined = jnp.zeros((features.shape[0], count * width), features.dtype)
    for place, part in zip(places, parts):
        joined = lax.dynamic_update_slice(joined, part, (0, place * width))
    return joined if hold is None else (joined, hold)


def line_piece(features, place):
    width = features.shape[1] // lax.axis_size("narrow")
    return lax.dynamic_slice_in_dim(features, place * width, width, 1)


def reduce_start(features):
    index = lax.axis_index("narrow")
    far = line_piece(features, index ^ 3)
    passed = along_line(far, pairs_inward)
    inner = along_line(far, pairs_inner)
    near = along_line(line_piece(features, index ^ 1), pairs_next)
    return passed, inner, near


def reduce_relay(features, passed):
    index = lax.axis_index("narrow")
    return (line_piece(features, index ^ 2).astype(f32) + passed.astype(f32)).astype(bf16)


def reduce_end(features, arrived):
    index = lax.axis_index("narrow")
    total = line_piece(features, index).astype(f32)
    for part in arrived:
        total = total + part.astype(f32)
    return total


def reduce_features(features):
    passed, inner, near = reduce_start(features)
    second = along_line(reduce_relay(features, passed), pairs_second)
    return reduce_end(features, (inner, near, second))


def gather_small(values):
    count = lax.axis_size("narrow")
    index = lax.axis_index("narrow")
    joined = jnp.zeros((count, values.shape[0]), values.dtype)
    for step in range(count):
        part = shifted(values, step) if step else values
        joined = lax.dynamic_update_slice(joined, part[None], ((index - step) % count, 0))
    return joined


def tie(*values):
    return lax.optimization_barrier(values)


def wide_totals(values):
    bit = 1
    while bit < lax.axis_size("wide"):
        values = values + flipped(values, bit)
        bit *= 2
    return values


def row_parts(values):
    return [values] + [shifted(values, step) for step in range(1, lax.axis_size("narrow"))]


def row_totals(values):
    count = lax.axis_size("narrow")
    return values + sum(shifted(values, step) for step in range(1, count))


def halving_orders(count):
    bits = list(range(1, count.bit_length() - 1))
    middle = len(bits) // 2
    return [bits, bits[middle:] + bits[:middle]]


def chunk_rows(features):
    count = lax.axis_size("wide")
    tokens, width = features.shape
    places = []
    for core in (1, 0):
        for half, order in enumerate(halving_orders(count)):
            chunks = [core]
            for bit in reversed(order):
                chunks = chunks + [chunk | (1 << bit) for chunk in chunks]
            places.append([(chunk, half) for chunk in chunks])
    chunks = jnp.array([chunk for group in places for chunk, _ in group], jnp.int32)
    halves = jnp.array([half for group in places for _, half in group], jnp.int32)
    pieces = features.T.reshape(2 * count, width // (2 * count), tokens)
    order = 2 * (lax.axis_index("wide") ^ chunks) + halves
    rows = jnp.take(pieces, order, axis=0, mode="clip").reshape(width, tokens)
    return rows[: width // 2], rows[width // 2 :]


def halves_of(rows):
    half = rows.shape[0] // 2
    return rows[:half], rows[half:]


def summed(values):
    total = values[0].astype(f32)
    for value in values[1:]:
        total = total + value.astype(f32)
    return total


def add_kernel(sizes, rows, *refs):
    outs = refs[sum(sizes) :]
    begin = 0
    for group, size in enumerate(sizes):
        columns = outs[0].shape[1]
        total = summed([ref[:, :columns] for ref in refs[begin : begin + size]])
        begin += size
        if len(outs) == 1:
            outs[0][group * rows : (group + 1) * rows, :] = total.astype(outs[0].dtype)
        else:
            outs[group][...] = total.astype(outs[group].dtype)


def add_rows(groups, place, rows, joined, kept):
    columns = groups[0][0].shape[1]
    start = place * rows
    if rows % 16:
        totals = [summed([part[start : start + rows] for part in parts]) for parts in groups]
        if joined:
            return jnp.concatenate(totals, axis=0)[:, :kept]
        return [total.astype(bf16) for total in totals]
    steps = 1 if joined or rows % 32 else 2
    block = rows // steps
    source = pl.BlockSpec((block, columns), lambda step: (place * steps + step, 0))
    if joined:
        out_specs = [pl.BlockSpec((len(groups) * rows, kept), lambda step: (0, 0))]
        out_shape = [jax.ShapeDtypeStruct((len(groups) * rows, kept), f32)]
    else:
        out_specs = [pl.BlockSpec((block, columns), lambda step: (step, 0))] * len(groups)
        out_shape = [jax.ShapeDtypeStruct((rows, columns), bf16)] * len(groups)
    outs = pl.pallas_call(
        functools.partial(add_kernel, [len(parts) for parts in groups], block),
        grid=(steps,),
        in_specs=[source] * sum(len(parts) for parts in groups),
        out_specs=out_specs,
        out_shape=out_shape,
        compiler_params=pltpu.CompilerParams(vmem_limit_bytes=48 * 1024 * 1024),
    )(*[part for parts in groups for part in parts])
    return outs[0] if joined else list(outs)


class Scatter:
    def __init__(self, products):
        near, away = products[:2], products[2:]
        self.orders = halving_orders(lax.axis_size("wide"))
        self.parts = [[own, flipped(sent, 1)] for own, sent in zip(near, away)]
        self.rows = near[0].shape[0]
        self.stage = 0

    def outgoing(self):
        return add_rows(self.parts, 1, self.rows // 2, False, None)

    def send(self, sending):
        for at, value in enumerate(sending):
            bit = 1 << self.orders[at][self.stage]
            self.parts[at] = self.parts[at] + [flipped(value, bit)]
        self.rows //= 2
        self.stage += 1

    def step(self):
        self.send(self.outgoing())

    def finish(self, kept):
        while self.stage < len(self.orders[0]):
            self.step()
        return add_rows(self.parts, 0, self.rows, True, kept)


def chunk_kernel(order_ref, left_ref, right_ref, near_a, near_b, away_a, away_b, whole_ref):
    core = order_ref[2 * pl.num_programs(0)]
    rows = near_a.shape[0]
    whole_ref[...] = inner_rows(left_ref[...], right_ref[...])
    near = pl.multiple_of(core * 2 * rows, 2 * rows)
    away = pl.multiple_of((1 - core) * 2 * rows, 2 * rows)
    columns = whole_ref.shape[1]
    for out, start in ((near_a, near), (near_b, near + rows), (away_a, away), (away_b, away + rows)):
        out[:, :columns] = whole_ref[pl.ds(start, rows), :].astype(bf16)
        if out.shape[1] > columns:
            out[:, columns:] = jnp.zeros((rows, out.shape[1] - columns), bf16)


def chunk_places(count):
    table = []
    for order in halving_orders(count):
        chips = [0]
        for bit in reversed(order):
            chips = chips + [chip | (1 << (bit - 1)) for chip in chips]
        table.append([chips.index(chip) for chip in range(count // 2)])
    return table


def chunk_products(left, right):
    count = lax.axis_size("wide")
    tokens, width = left.shape
    columns = right.shape[1]
    chips = count // 2
    group = width // chips
    rows = group // 4
    if group % 128 or rows % 16:
        away, near = [product(part, right).astype(bf16) for part in chunk_rows(left)]
        return [*halves_of(near), *halves_of(away)]
    index = lax.axis_index("wide")
    relative = (index // 2) ^ jnp.arange(chips, dtype=jnp.int32)
    order = jnp.concatenate(
        [jnp.array(table, jnp.int32)[relative] for table in chunk_places(count)]
        + [(index % 2)[None]]
    ).astype(jnp.int32)
    padded = -(-columns // 128) * 128
    first = pl.BlockSpec((rows, padded), lambda step, at: (at[step], 0))
    last = pl.BlockSpec((rows, padded), lambda step, at: (at[pl.num_programs(0) + step], 0))
    return list(
        pl.pallas_call(
            chunk_kernel,
            grid_spec=pltpu.PrefetchScalarGridSpec(
                num_scalar_prefetch=1,
                grid=(chips,),
                in_specs=[
                    pl.BlockSpec((tokens, group), lambda step, at: (0, step)),
                    pl.BlockSpec((tokens, columns), lambda step, at: (0, 0)),
                ],
                out_specs=[first, last, first, last],
                scratch_shapes=[pltpu.VMEM((group, columns), f32)],
            ),
            out_shape=[jax.ShapeDtypeStruct((chips * rows, padded), bf16)] * 4,
            compiler_params=pltpu.CompilerParams(vmem_limit_bytes=48 * 1024 * 1024),
        )(order, left, right)
    )


def weight_kernel(left_ref, right_ref, out_ref):
    out_ref[...] = inner_rows(left_ref[...], right_ref[...]).astype(bf16)


def weight_product(left, right):
    tokens, width = left.shape
    columns = right.shape[1]
    group = width // 4
    if group % 128:
        return inner_rows(left, right).astype(bf16)
    return pl.pallas_call(
        weight_kernel,
        grid=(4,),
        in_specs=[
            pl.BlockSpec((tokens, group), lambda step: (0, step)),
            pl.BlockSpec((tokens, columns), lambda step: (0, 0)),
        ],
        out_specs=pl.BlockSpec((group, columns), lambda step: (step, 0)),
        out_shape=jax.ShapeDtypeStruct((width, columns), bf16),
        compiler_params=pltpu.CompilerParams(vmem_limit_bytes=48 * 1024 * 1024),
    )(left, right)


def scatter_rows(partial):
    return lax.psum_scatter(partial, "wide", scatter_dimension=0, tiled=True)


def pack_kernel(send_ref, *refs):
    count = len(refs) - 3
    blocks, outs, turned = refs[:count], refs[count : count + 2], refs[-1]
    begin = 0
    for block in blocks:
        width = block.shape[1]
        turned[begin : begin + width, :] = block[...].astype(f32).T.astype(bf16)
        begin += width
    capacity = outs[0].shape[1] + outs[1].shape[1]
    for out, offset in zip(outs, (0, outs[0].shape[1])):
        slots = out.shape[1]

        def place(step, carry, out=out, offset=offset, slots=slots):
            owner = step // slots
            slot = step % slots
            unit = send_ref[owner * capacity + offset + slot]
            out[owner, slot] = turned[pl.ds(pl.multiple_of(unit * SLAB, SLAB), SLAB), :]
            return carry

        lax.fori_loop(0, out.shape[0] * slots, place, 0)


def pack_units(send, blocks, count, sizes):
    rows = blocks[0].shape[0]
    total = sum(block.shape[1] for block in blocks)
    vmem = pl.BlockSpec(memory_space=pltpu.VMEM)
    return pl.pallas_call(
        pack_kernel,
        in_specs=[pl.BlockSpec(memory_space=pltpu.SMEM)] + [vmem] * len(blocks),
        out_specs=[vmem] * 2,
        out_shape=[jax.ShapeDtypeStruct((count, size, SLAB, rows), bf16) for size in sizes],
        scratch_shapes=[pltpu.VMEM((total, rows), bf16)],
        compiler_params=pltpu.CompilerParams(vmem_limit_bytes=56 * 1024 * 1024),
    )(send, *blocks)


def unpack_kernel(back_ref, first_ref, last_ref, *refs):
    count = (len(refs) - 1) // 2
    weights, outs, turned = refs[:count], refs[count : 2 * count], refs[-1]
    first = first_ref.shape[1]
    capacity = first + last_ref.shape[1]

    def place(unit, carry):
        slot = back_ref[unit]
        owner = slot // capacity
        at = slot % capacity
        rows = pl.ds(pl.multiple_of(unit * SLAB, SLAB), SLAB)

        @pl.when(at < first)
        def _():
            turned[rows, :] = first_ref[owner, at]

        @pl.when(at >= first)
        def _():
            turned[rows, :] = last_ref[owner, at - first]

        return carry

    lax.fori_loop(0, turned.shape[0] // SLAB, place, 0)
    begin = 0
    for weight, out in zip(weights, outs):
        width = out.shape[1]
        steps = turned[begin : begin + width, :].astype(f32).T
        out[...] = weight[...].astype(f32) + steps
        begin += width


def unpack_units(back, first, last, weights):
    rows = first.shape[3]
    total = sum(weight.shape[1] for weight in weights)
    vmem = pl.BlockSpec(memory_space=pltpu.VMEM)
    return pl.pallas_call(
        unpack_kernel,
        in_specs=[pl.BlockSpec(memory_space=pltpu.SMEM)] + [vmem] * (2 + len(weights)),
        out_specs=[vmem] * len(weights),
        out_shape=[jax.ShapeDtypeStruct(weight.shape, f32) for weight in weights],
        scratch_shapes=[pltpu.VMEM((total, rows), bf16)],
        compiler_params=pltpu.CompilerParams(vmem_limit_bytes=56 * 1024 * 1024),
    )(back, first, last, *weights)


def unit_rates(col_widths, rates):
    return jnp.concatenate(
        [
            jnp.full((col_width // SLAB,), step_rate, jnp.float32)
            for col_width, step_rate in zip(col_widths, rates)
        ]
    )


def rotated_step(gradient, left_ref, right_ref, moment_ref, square_ref, new_moment_ref,
                 new_square_ref, turned_ref, occupied, first_scale, second_scale):
    blocks = left_ref.shape[1] // BASIS
    right_basis = right_ref[0].astype(bf16)
    turned_ref[...] = lax.dot_general(
        right_basis, gradient, (((0,), (0,)), ((), ())), preferred_element_type=f32
    )
    for block in range(blocks):
        at = slice(block * BASIS, (block + 1) * BASIS)
        left_basis = left_ref[0, at, :].astype(bf16)
        turned = jnp.dot(turned_ref[:, at].astype(bf16), left_basis, preferred_element_type=f32)
        moment = moment_ref[0, :, at]
        square = square_ref[0, :, at]
        new_moment = beta_one * moment + (1.0 - beta_one) * turned
        new_square = beta_two * square + (1.0 - beta_two) * turned * turned
        new_moment_ref[0, :, at] = jnp.where(occupied > 0.5, new_moment, moment)
        new_square_ref[0, :, at] = jnp.where(occupied > 0.5, new_square, square)
        direction = new_moment * first_scale / (jnp.sqrt(new_square * second_scale) + adam_eps)
        turned_ref[:, at] = lax.dot_general(
            direction.astype(bf16), left_basis, (((1,), (1,)), ((), ())),
            preferred_element_type=f32,
        )
    return jnp.dot(right_basis, turned_ref[...].astype(bf16), preferred_element_type=f32)


def slot_kernel(place_ref, scale_ref, gradient_ref, left_ref, right_ref, moment_ref, square_ref,
                change_ref, new_moment_ref, new_square_ref, whole_ref, turned_ref):
    step = pl.program_id(0)
    steps = pl.num_programs(0)
    sources, rows = gradient_ref.shape[0], gradient_ref.shape[3]
    rate = scale_ref[step]
    occupied = scale_ref[steps + step]

    @pl.when(occupied > 0.5)
    def _():
        for source in range(sources):
            whole_ref[:, source * rows : (source + 1) * rows] = gradient_ref[source, 0].astype(f32)
        whole_ref[...] = rate * rotated_step(
            whole_ref[...].astype(bf16), left_ref, right_ref, moment_ref, square_ref,
            new_moment_ref, new_square_ref, turned_ref, occupied,
            scale_ref[2 * steps], scale_ref[2 * steps + 1],
        )
        for source in range(sources):
            change_ref[source, 0] = whole_ref[:, source * rows : (source + 1) * rows].astype(bf16)

    @pl.when(occupied <= 0.5)
    def _():
        change_ref[...] = jnp.zeros_like(change_ref)

    @pl.when(jnp.logical_and(occupied <= 0.5, place_ref[steps + step] > 0))
    def _():
        new_moment_ref[...] = moment_ref[...]
        new_square_ref[...] = square_ref[...]


def slot_call(places, scales, gradient, left_basis, right_basis, moment, square, written):
    sources, steps, _, rows = gradient.shape
    row_count = sources * rows
    moment = moment.transpose(0, 2, 1)
    square = square.transpose(0, 2, 1)
    state = pl.BlockSpec((1, SLAB, row_count), lambda step, place: (place[step], 0, 0))
    traded = pl.BlockSpec((sources, 1, SLAB, rows), lambda step, place: (0, step, 0, 0))
    operands = [places, scales, gradient, left_basis, right_basis, moment, square]
    in_specs = [
        pl.BlockSpec(memory_space=pltpu.SMEM),
        traded,
        pl.BlockSpec((1, row_count, BASIS), lambda step, place: (place[step], 0, 0)),
        pl.BlockSpec((1, SLAB, SLAB), lambda step, place: (place[step], 0, 0)),
        state,
        state,
    ]
    aliases = {}
    kernel = slot_kernel
    if written == "same":
        aliases = {5: 1, 6: 2}
    elif written is not None:
        operands += [value.transpose(0, 2, 1) for value in written]
        in_specs += [pl.BlockSpec(memory_space=pl.ANY)] * 2
        aliases = {7: 1, 8: 2}

        def kernel(*refs):
            slot_kernel(*refs[:7], *refs[9:])

    change, new_moment, new_square = pl.pallas_call(
        kernel,
        grid_spec=pltpu.PrefetchScalarGridSpec(
            num_scalar_prefetch=1,
            grid=(steps,),
            in_specs=in_specs,
            out_specs=[traded, state, state],
            scratch_shapes=[
                pltpu.VMEM((SLAB, row_count), f32),
                pltpu.VMEM((SLAB, row_count), f32),
            ],
        ),
        out_shape=[
            jax.ShapeDtypeStruct(gradient.shape, bf16),
            jax.ShapeDtypeStruct(moment.shape, f32),
            jax.ShapeDtypeStruct(square.shape, f32),
        ],
        input_output_aliases=aliases,
        compiler_params=pltpu.CompilerParams(vmem_limit_bytes=48 * 1024 * 1024),
    )(*operands)
    return change, new_moment.transpose(0, 2, 1), new_square.transpose(0, 2, 1)


def slot_group(scales, gradient, left_basis, right_basis, moment, square, group, written):
    capacity = moment.shape[0]
    count = group.stop - group.start
    places = jnp.concatenate(
        [
            jnp.arange(group.start, group.stop, dtype=jnp.int32),
            jnp.ones((count,), jnp.int32),
        ]
    )
    scales = jnp.concatenate(
        [
            scales[group],
            scales[capacity + group.start : capacity + group.stop],
            scales[2 * capacity :],
        ]
    )
    return slot_call(places, scales, gradient, left_basis, right_basis, moment, square, written)


def all_slots(scales, gradient, left_basis, right_basis, moment, square):
    group = slice(0, moment.shape[0])
    return slot_group(
        scales, gradient, left_basis, right_basis, moment, square, group, None
    )


def late_steps(places, scales, gradient, left_basis, right_basis, moment, square):
    return slot_call(places, scales, gradient, left_basis, right_basis, moment, square, "same")


def correction_scales(tcount):
    return jnp.stack([1.0 / (1.0 - beta_one**tcount), 1.0 / (1.0 - beta_two**tcount)])


def slot_scales(owners, rates, capacity, wide_index, tcount):
    slot_ids = wide_index * capacity + jnp.arange(capacity, dtype=jnp.int32)
    own = (owners[None, :] == slot_ids[:, None]).astype(f32)
    return jnp.concatenate(
        [
            -jnp.sum(own * rates[None, :], axis=1),
            jnp.sum(own, axis=1),
            correction_scales(tcount),
        ]
    )


def ranks_within(owners, capacity):
    device = owners // capacity
    units = owners.shape[0]
    earlier = jnp.arange(units)[None, :] < jnp.arange(units)[:, None]
    return jnp.sum(
        jnp.where(earlier & (device[None, :] == device[:, None]), 1, 0).astype(jnp.int32), axis=1
    )


def turned_lanes(value, tables, sign):
    near = pltpu.roll(value, 112, 1) * tables[1]
    far = pltpu.roll(value, 16, 1) * tables[2]
    return value * tables[0] + sign * (near + far)


def lane_ids(shape):
    return lax.broadcasted_iota(jnp.int32, shape, 1)


def head_inputs(head, query_ref, key_value_ref, rotary_ref, tables, bias_ref):
    at = slice(head * 128, (head + 1) * 128)
    query = turned_lanes(query_ref[:, at], tables, 1.0).astype(bf16)
    key_value = key_value_ref[:, at].astype(bf16)
    key = jnp.where(lane_ids(key_value.shape) < NOPE, key_value, rotary_ref[...])
    scores = against_rows(query, key) * (NOPE + ROPE) ** (-0.5) + bias_ref[...]
    exp_scores = jnp.exp(scores - jnp.max(scores, axis=1, keepdims=True))
    probs = exp_scores / jnp.sum(exp_scores, axis=1, keepdims=True)
    return query, key_value, key, probs


def attend_kernel(query_ref, key_value_ref, rotary_ref, table_ref, bias_ref, out_ref):
    tables = [table_ref[at] for at in range(3)]
    mixed = []
    for head in range(2):
        _, key_value, _, probs = head_inputs(
            head, query_ref, key_value_ref, rotary_ref, tables, bias_ref
        )
        mixed.append(product(probs.astype(bf16), key_value))
    lower = pltpu.roll(mixed[0], 64, 1)
    out_ref[...] = jnp.where(lane_ids(lower.shape) < VH, lower, mixed[1]).astype(bf16)


def attend_back_kernel(query_ref, key_value_ref, rotary_ref, table_ref, bias_ref, grad_ref,
                       query_grad_ref, key_value_grad_ref, sums_ref):
    tables = [table_ref[at] for at in range(3)]
    scale = (NOPE + ROPE) ** (-0.5)

    @pl.when(pl.program_id(0) == 0)
    def _():
        sums_ref[...] = jnp.zeros_like(sums_ref)

    for head in range(2):
        at = slice(head * 128, (head + 1) * 128)
        query, key_value, key, probs = head_inputs(
            head, query_ref, key_value_ref, rotary_ref, tables, bias_ref
        )
        grad = grad_ref[...].astype(f32)
        lanes = lane_ids(grad.shape)
        if head == 0:
            grad = pltpu.roll(grad, 64, 1)
        grad = jnp.where(lanes < NOPE, 0.0, grad).astype(bf16)
        value_grad = inner_rows(probs.astype(bf16), grad)
        prob_grad = against_rows(grad, key_value)
        delta = jnp.sum(probs * prob_grad, axis=1, keepdims=True)
        score_grad = (probs * (prob_grad - delta)).astype(bf16)
        query_grad = turned_lanes(scale * product(score_grad, key), tables, -1.0).astype(bf16)
        key_grad = scale * inner_rows(score_grad, query)
        key_value_grad = jnp.where(lanes < NOPE, key_grad, value_grad).astype(bf16)
        query_grad_ref[:, at] = query_grad
        key_value_grad_ref[:, at] = key_value_grad
        sums_ref[0] += query_grad.astype(f32) * query_ref[:, at]
        sums_ref[1] += key_value_grad.astype(f32) * key_value_ref[:, at]
        sums_ref[2] += key_grad


def attend_specs(tokens):
    pair = pl.BlockSpec((tokens, 256), lambda step: (0, step))
    single = pl.BlockSpec((tokens, 128), lambda step: (0, step))
    shared = pl.BlockSpec((tokens, 128), lambda step: (0, 0))
    tables = pl.BlockSpec((3, tokens, 128), lambda step: (0, 0, 0))
    bias = pl.BlockSpec((tokens, tokens), lambda step: (0, 0))
    return pair, single, shared, tables, bias


def attend(queries, keys_values, rotary, tables, bias):
    tokens, width = queries.shape
    pair, single, shared, table_spec, bias_spec = attend_specs(tokens)
    return pl.pallas_call(
        attend_kernel,
        grid=(width // 256,),
        in_specs=[pair, pair, shared, table_spec, bias_spec],
        out_specs=single,
        out_shape=jax.ShapeDtypeStruct((tokens, width // 2), bf16),
        compiler_params=pltpu.CompilerParams(vmem_limit_bytes=48 * 1024 * 1024),
    )(queries, keys_values, rotary, tables, bias)


def attend_back(queries, keys_values, rotary, tables, bias, grad):
    tokens, width = queries.shape
    pair, single, shared, table_spec, bias_spec = attend_specs(tokens)
    return pl.pallas_call(
        attend_back_kernel,
        grid=(width // 256,),
        in_specs=[pair, pair, shared, table_spec, bias_spec, single],
        out_specs=[pair, pair, table_spec],
        out_shape=[
            jax.ShapeDtypeStruct((tokens, width), bf16),
            jax.ShapeDtypeStruct((tokens, width), bf16),
            jax.ShapeDtypeStruct((3, tokens, 128), f32),
        ],
        compiler_params=pltpu.CompilerParams(vmem_limit_bytes=48 * 1024 * 1024),
    )(queries, keys_values, rotary, tables, bias, grad)


def routes(owners, capacity, room, wide_count):
    units = owners.shape[0]
    if room == capacity:
        places = owners
    else:
        places = owners // capacity * room + ranks_within(owners, capacity)
    slots = jnp.arange(wide_count * room, dtype=jnp.int32)
    matches = slots[:, None] == places[None, :]
    unit_of = jnp.sum(
        jnp.where(matches, jnp.arange(units, dtype=jnp.int32)[None, :], 0), axis=1
    )
    return jnp.minimum(unit_of, units - 1), places


def late_places(owners, rates, capacity, room, wide_index, tcount):
    ranks = ranks_within(owners, capacity)
    mine = owners // capacity == wide_index
    own = mine[None, :] & (ranks[None, :] == jnp.arange(room, dtype=jnp.int32)[:, None])
    slot = jnp.sum(jnp.where(own, (owners % capacity)[None, :], 0), axis=1)
    filled = jnp.sum(own.astype(jnp.int32), axis=1)
    last = jnp.maximum(jnp.sum(filled) - 1, 0)
    last_slot = jnp.sum(jnp.where(jnp.arange(room) == last, slot, 0))
    places = jnp.where(filled > 0, slot, last_slot)
    untouched = jnp.where((jnp.arange(room) == 0) & (filled == 0), 1, 0)
    scales = jnp.concatenate(
        [
            -jnp.sum(own.astype(f32) * rates[None, :], axis=1),
            filled.astype(f32),
            correction_scales(tcount),
        ]
    )
    return jnp.concatenate([places, untouched]).astype(jnp.int32), scales


def unit_rows(blocks):
    joined = jnp.concatenate([block.T for block in blocks], axis=0).astype(bf16)
    return joined.reshape(-1, SLAB, joined.shape[1])


def unit_columns(units, blocks):
    joined = units.reshape(-1, units.shape[2])
    pieces, begin = ([], 0)
    for block in blocks:
        pieces.append(joined[begin : begin + block.shape[1]].T.astype(f32))
        begin += block.shape[1]
    return pieces


def trade_joined(parts, count):
    steps = [part.shape[0] // count for part in parts]
    widths = [part.shape[2] for part in parts]
    room = max(steps)
    joined = jnp.concatenate(
        [
            jnp.pad(
                part.reshape(count, own, SLAB, width), ((0, 0), (0, room - own), (0, 0), (0, 0))
            )
            for part, own, width in zip(parts, steps, widths)
        ],
        axis=3,
    )
    traded = lax.all_to_all(joined, "wide", split_axis=0, concat_axis=0, tiled=True)
    pieces, begin = ([], 0)
    for own, width in zip(steps, widths):
        pieces.append(traded[:, :own, :, begin : begin + width])
        begin += width
    return pieces


def body(
    x_in,
    grad_out,
    w_qa,
    w_kv,
    w_kr,
    w_qb,
    w_kvb,
    w_o,
    w_gate,
    w_up,
    w_down,
    norm_gains,
    q_gain,
    kv_gain,
    deal,
    lengths,
    step_count,
    owner_a,
    owner_b,
    owner_c,
    basis_la,
    basis_ra,
    basis_lb,
    basis_rb,
    basis_lc,
    basis_rc,
    mom_a,
    sq_a,
    mom_b,
    sq_b,
    mom_c,
    sq_c,
    kr_mom,
    kr_sq,
    gain_mom,
    gain_sq,
    qgain_mom,
    qgain_sq,
    kvgain_mom,
    kvgain_sq,
):
    wide_count = lax.axis_size("wide")
    wide_index = lax.axis_index("wide")
    narrow_index = lax.axis_index("narrow")
    row_count, local_width = x_in.shape
    piece_rows = row_count // wide_count
    deal_row = lax.dynamic_index_in_dim(deal, wide_index, 0, keepdims=False)
    wide_ids = jnp.arange(wide_count, dtype=jnp.int32)
    inverse = jnp.sum(
        jnp.where(deal_row[None, :] == wide_ids[:, None], wide_ids[None, :], 0), axis=1
    )

    def to_working(features):
        outgoing = jnp.take(
            features.reshape((wide_count, piece_rows) + features.shape[1:]), inverse, axis=0,
            mode="clip",
        )
        dealt = lax.all_to_all(outgoing, "wide", split_axis=0, concat_axis=0, tiled=True)
        return dealt.reshape(row_count, -1)

    token_in = to_working(x_in)
    residual = token_in.astype(f32)
    seq_lengths = lengths[0]
    seq_ends = jnp.cumsum(seq_lengths)
    row_ids = jnp.arange(row_count, dtype=jnp.int32)
    segment = jnp.sum((row_ids[:, None] >= seq_ends[None, :-1]).astype(jnp.int32), axis=1)
    pick = jnp.arange(seq_lengths.shape[0], dtype=jnp.int32)[None, :] == segment[:, None]
    seq_start = jnp.sum(jnp.where(pick, (seq_ends - seq_lengths)[None, :], 0), axis=1)
    live_rows = (segment < seq_lengths.shape[0] - 1).astype(f32)[:, None]
    cosine_table, sine_table = rope_tables(row_ids - seq_start)
    cos_heads = cosine_table[:, None, :]
    sin_heads = sine_table[:, None, :]

    latent_own = jnp.concatenate([w_qa, w_kv, w_kr], axis=1)
    heads_here = w_o.shape[1] // VH
    padded_qb = jnp.pad(
        w_qb.reshape(w_qb.shape[0], heads_here, NOPE + ROPE),
        ((0, 0), (0, 0), (0, 128 - NOPE - ROPE)),
    ).reshape(w_qb.shape[0], -1)
    full_latent = lax.all_gather(latent_own, "wide", axis=0, tiled=True)
    full_qb = lax.all_gather(padded_qb, "wide", axis=0, tiled=True)
    full_kvb = lax.all_gather(w_kvb, "wide", axis=0, tiled=True)
    full_o = lax.all_gather(w_o, "wide", axis=0, tiled=True)
    full_gate = lax.all_gather(w_gate, "wide", axis=0, tiled=True)
    full_up = lax.all_gather(w_up, "wide", axis=0, tiled=True)
    full_down = lax.all_gather(w_down, "wide", axis=0, tiled=True)
    gains_all = gather_small(jnp.concatenate([norm_gains[0], norm_gains[1], q_gain, kv_gain]))
    first_gain = gains_all[:, :local_width].reshape(1, -1)
    second_gain = gains_all[:, local_width : 2 * local_width].reshape(1, -1)
    q_width = q_gain.shape[0]
    kv_width = kv_gain.shape[0]
    q_gain_all = gains_all[:, 2 * local_width : 2 * local_width + q_width].reshape(1, -1)
    kv_gain_all = gains_all[:, 2 * local_width + q_width :].reshape(1, -1)

    def inverse_rms(features, width):
        wide = features.astype(f32)
        return lax.rsqrt(jnp.sum(wide * wide, axis=1, keepdims=True) / width + norm_eps)

    token_all, full_latent = gather_features(token_in, full_latent)
    inv_first = inverse_rms(token_all, D)
    normed = (token_all.astype(f32) * inv_first * first_gain).astype(bf16)
    latents = product(normed, full_latent)
    q_latent = latents[:, :q_width]
    kv_latent = latents[:, q_width : q_width + kv_width]
    key_rot = latents[:, q_width + kv_width :]
    narrow_count = lax.axis_size("narrow")
    latents_all = gather_features(latents[:, : q_width + kv_width].astype(bf16))
    latents_all = latents_all.reshape(row_count, narrow_count, q_width + kv_width)
    q_latent_all = latents_all[:, :, :q_width].reshape(row_count, QR).astype(f32)
    kv_latent_all = latents_all[:, :, q_width:].reshape(row_count, KVR).astype(f32)
    inv_q = inverse_rms(q_latent_all, QR)
    inv_kv = inverse_rms(kv_latent_all, KVR)
    q_normed = (q_latent_all * inv_q * q_gain_all).astype(bf16)
    kv_normed = (kv_latent_all * inv_kv * kv_gain_all).astype(bf16)
    q_pre = product(q_normed, full_qb)
    kv_pre = product(kv_normed, full_kvb)
    key_turned = rotate(key_rot, cosine_table, sine_table, 1.0)
    rotary = jnp.pad(key_turned, ((0, 0), (NOPE, 128 - NOPE - ROPE))).astype(bf16)
    allowed = (segment[:, None] == segment[None, :]) & (row_ids[None, :] <= row_ids[:, None])
    bias = jnp.where(allowed, 0.0, masked_value).astype(f32)
    half_pads = ((NOPE, 128 - NOPE - ROPE // 2), (NOPE + ROPE // 2, 128 - NOPE - ROPE))

    def lane_table(lower, upper):
        return sum(
            jnp.pad(part, ((0, 0), pads)) for part, pads in zip((lower, upper), half_pads)
        )

    empty = jnp.zeros_like(sine_table)
    tables = jnp.stack(
        [
            lane_table(cosine_table, cosine_table)
            + jnp.where(jnp.arange(128) < NOPE, 1.0, 0.0)[None, :],
            lane_table(-sine_table, empty),
            lane_table(empty, sine_table),
        ]
    )
    latents_all, grad_out = tie(latents_all, grad_out)
    heads_out = attend(q_pre, kv_pre, rotary, tables, bias)
    grad_all, heads_out = gather_features(grad_out, heads_out)
    token_grad_all = to_working(grad_all)
    grad_top = lax.dynamic_slice_in_dim(
        token_grad_all, narrow_index * local_width, local_width, 1
    ).astype(f32)
    mlp_grad = (residual_scale * live_rows * token_grad_all.astype(f32)).astype(bf16)
    attn_out = reduce_features(against_rows(heads_out, full_o).astype(bf16))
    middle = residual + residual_scale * live_rows * attn_out
    middle_all = gather_features(middle.astype(bf16)).astype(f32)
    inv_second = inverse_rms(middle_all, D)
    normed_two = (middle_all * inv_second * second_gain).astype(bf16)
    gate_act = product(normed_two, full_gate)
    upward = product(normed_two, full_up)
    sigmoid_gate = jax.nn.sigmoid(gate_act)
    silu_gate = gate_act * sigmoid_gate
    active = (silu_gate * upward).astype(bf16)
    mlp_part = against_rows(active, full_down).astype(bf16)
    mlp_passed, mlp_inner, mlp_near = reduce_start(mlp_part)
    down_products = chunk_products(mlp_grad, active)
    active_grad = product(mlp_grad, full_down)
    gate_grad = (
        active_grad * upward * (sigmoid_gate + silu_gate * (1.0 - sigmoid_gate))
    ).astype(bf16)
    up_grad = (active_grad * silu_gate).astype(bf16)
    gate_grad, up_grad, down_products = tie(gate_grad, up_grad, down_products)
    down_sum = Scatter(down_products)
    normed_two_part = (
        against_rows(gate_grad, full_gate) + against_rows(up_grad, full_up)
    ).astype(bf16)
    passed, inner, near = reduce_start(normed_two_part)
    gate_products = chunk_products(normed_two, gate_grad)
    passed, gate_products, up_grad, down_sending = tie(
        passed, gate_products, up_grad, down_sum.outgoing()
    )
    down_sum.send(down_sending)
    gate_sum = Scatter(gate_products)
    relayed = reduce_relay(normed_two_part, passed)
    relayed, up_grad = tie(relayed, up_grad)
    second = along_line(relayed, pairs_second)
    up_sum = Scatter(chunk_products(normed_two, up_grad))
    second, up_sum.parts, gate_sending = tie(second, up_sum.parts, gate_sum.outgoing())
    gate_sum.send(gate_sending)
    normed_two_grad = reduce_end(normed_two_part, (inner, near, second))
    post_gain_grad = jnp.sum(normed_two_grad * middle * inv_second, axis=0)
    direct_grad = grad_top + inv_second * norm_gains[1] * normed_two_grad
    direct_all, sendings = gather_features(
        direct_grad.astype(bf16),
        (up_sum.outgoing(), down_sum.outgoing()),
    )
    direct_all = direct_all.astype(f32)
    top_all = token_grad_all.astype(f32)
    second_dot = jnp.sum((direct_all - top_all) * middle_all, axis=1, keepdims=True)
    attn_grad = (
        residual_scale
        * live_rows
        * (direct_all - middle_all * (inv_second**2 * second_dot / D))
    ).astype(bf16)
    middle_grad = direct_grad - middle * (inv_second**2 * second_dot / D)
    for weight_sum, sending in zip((up_sum, down_sum), sendings):
        weight_sum.send(sending)
    o_full = weight_product(attn_grad, heads_out)
    attn_grad, o_full, gate_sending = tie(attn_grad, o_full, gate_sum.outgoing())
    gate_sum.send(gate_sending)
    block_o = scatter_rows(o_full)
    mlp_passed, attn_grad = tie(mlp_passed, attn_grad)
    mlp_second = along_line(reduce_relay(mlp_part, mlp_passed), pairs_second)
    heads_grad = product(attn_grad, full_o).astype(bf16)

    q_pre_grad, kv_pre_grad, head_sums = attend_back(
        q_pre, kv_pre, rotary, tables, bias, heads_grad
    )
    mlp_arrived = (mlp_inner, mlp_near, mlp_second)
    head_sums, q_pre_grad, up_sending = tie(head_sums, q_pre_grad, up_sum.outgoing())
    up_sum.send(up_sending)
    rot_partial = rotate(
        head_sums[2, :, NOPE : NOPE + ROPE], cosine_table, sine_table, -1.0
    )
    q_dot = jnp.sum(head_sums[0], axis=1)
    kv_dot = jnp.sum(head_sums[1], axis=1)
    dots = row_parts(jnp.concatenate([jnp.stack([q_dot, kv_dot]), rot_partial.T], axis=0))
    q_part = against_rows(q_pre_grad, full_qb).astype(bf16)
    kv_part = against_rows(kv_pre_grad, full_kvb).astype(bf16)
    both_part = jnp.concatenate(
        [
            q_part.reshape(row_count, narrow_count, q_width),
            kv_part.reshape(row_count, narrow_count, kv_width),
        ],
        axis=-1,
    ).reshape(row_count, -1)
    passed, inner, near = reduce_start(both_part)
    tcount = step_count[0].astype(f32)
    wide_rate = D ** (-0.5)
    block_down = down_sum.finish(w_down.shape[1])
    block_gate = gate_sum.finish(w_gate.shape[1])
    block_up = up_sum.finish(w_up.shape[1])
    passed, q_pre_late, kv_pre_late, block_down, block_gate, block_up = tie(
        passed, q_pre_grad, kv_pre_grad, block_down, block_gate, block_up
    )
    main_blocks = [block_o, block_gate, block_up, block_down]
    late_blocks_widths = [q_width, kv_width]
    late_units = sum(late_blocks_widths) // SLAB
    main_rates = unit_rates(
        [block.shape[1] for block in main_blocks], [1.0, wide_rate, wide_rate, 0.125]
    )
    late_rates = unit_rates(late_blocks_widths, [wide_rate, wide_rate])
    late_owners, main_owners = owner_a[0, :late_units], owner_a[0, late_units:]
    capacity_a = mom_a.shape[0]
    main_send, main_back = routes(main_owners, capacity_a, capacity_a, wide_count)
    main_scales = slot_scales(main_owners, main_rates, capacity_a, wide_index, tcount)
    first_slots = (capacity_a + 1) // 2
    groups = [slice(0, first_slots), slice(first_slots, capacity_a)]
    main_sent = pack_units(
        main_send, main_blocks, wide_count, [group.stop - group.start for group in groups]
    )
    second = along_line(reduce_relay(both_part, passed), pairs_second)
    head_columns = w_kvb.shape[1]
    qb_full = inner_rows(q_normed, q_pre_late).astype(bf16)
    kvb_full = inner_rows(kv_normed, kv_pre_late).astype(bf16)
    head_products = jnp.concatenate(
        [
            qb_full.reshape(wide_count, -1, head_columns),
            kvb_full.reshape(wide_count, -1, head_columns),
        ],
        axis=1,
    ).reshape(-1, head_columns)
    second, dots, main_sent, head_products = tie(second, dots, main_sent, head_products)
    main_owned = [
        lax.all_to_all(part, "wide", split_axis=0, concat_axis=0, tiled=True)
        for part in main_sent
    ]
    dots = sum(dots).T
    q_dot, kv_dot = dots[:, :1], dots[:, 1:2]
    rot_grad = dots[:, 2:].astype(bf16)
    head_products, block_o = tie(head_products, block_o)
    block_heads = scatter_rows(head_products)
    both_grad = reduce_end(both_part, (inner, near, second))
    q_normed_grad = both_grad[:, :q_width]
    kv_normed_grad = both_grad[:, q_width:]
    q_gain_grad = jnp.sum(q_normed_grad * q_latent * inv_q, axis=0)
    kv_gain_grad = jnp.sum(kv_normed_grad * kv_latent * inv_kv, axis=0)
    q_latent_grad = (
        inv_q * q_gain * q_normed_grad - q_latent * inv_q**2 * q_dot / QR
    ).astype(bf16)
    kv_latent_grad = (
        inv_kv * kv_gain * kv_normed_grad - kv_latent * inv_kv**2 * kv_dot / KVR
    ).astype(bf16)
    first_dot = (
        norm_eps * (inv_q**2 * q_dot + inv_kv**2 * kv_dot)
        + jnp.sum(rot_grad.astype(f32) * key_rot, axis=1, keepdims=True)
    )
    latent_grad = jnp.concatenate([q_latent_grad, kv_latent_grad, rot_grad], axis=1)
    full_kr = full_latent[:, q_width + kv_width :]
    own_kr = lax.dynamic_slice_in_dim(full_kr, narrow_index * local_width, local_width, 0)
    normed_part = against_rows(
        latent_grad[:, : q_width + kv_width], full_latent[:, : q_width + kv_width]
    ).astype(bf16)
    normed_passed, normed_inner, normed_near = reduce_start(normed_part)
    latent_full = weight_product(normed, latent_grad)
    normed_passed, latent_full = tie(normed_passed, latent_full)
    latent_late, first_owned = tie(latent_full, main_owned[0])
    block_latent = scatter_rows(latent_late)
    normed_second = along_line(reduce_relay(normed_part, normed_passed), pairs_second)
    normed_second, first_owned, mlp_arrived = tie(normed_second, first_owned, mlp_arrived)
    mlp_out = reduce_end(mlp_part, mlp_arrived)
    layer_out = middle + residual_scale * live_rows * mlp_out
    normed_grad = reduce_end(normed_part, (normed_inner, normed_near, normed_second)) + (
        against_rows(rot_grad, own_kr)
    )
    in_gain_grad = jnp.sum(normed_grad * residual * inv_first, axis=0)
    input_grad = (
        middle_grad
        + inv_first * norm_gains[0] * normed_grad
        - residual * inv_first**2 * first_dot / D
    )
    gain_part = jnp.concatenate([in_gain_grad, post_gain_grad, q_gain_grad, kv_gain_grad])
    gain_high = lax.optimization_barrier(gain_part.astype(bf16))
    gain_low = (gain_part - gain_high.astype(f32)).astype(bf16)
    gain_rows = jnp.concatenate([gain_high, gain_low])
    gain_height = -(-gain_rows.shape[0] // local_width)
    gain_rows = jnp.pad(gain_rows, (0, gain_height * local_width - gain_rows.shape[0]))
    gain_rows = jnp.broadcast_to(
        gain_rows.reshape(1, gain_height, local_width), (wide_count, gain_height, local_width)
    )
    leaving = jnp.concatenate(
        [
            layer_out.astype(bf16).reshape(wide_count, piece_rows, local_width),
            input_grad.astype(bf16).reshape(wide_count, piece_rows, local_width),
            gain_rows,
        ],
        axis=1,
    )
    leaving, first_owned, last_owned = tie(leaving, first_owned, main_owned[1])
    returned_rows = lax.all_to_all(leaving, "wide", split_axis=0, concat_axis=0, tiled=True)
    change_one, mid_mom_a, mid_sq_a = slot_group(
        main_scales, first_owned, basis_la, basis_ra, mom_a, sq_a, groups[0], None
    )
    change_one, last_owned, returned_rows = tie(change_one, last_owned, returned_rows)
    back_one = lax.all_to_all(change_one, "wide", split_axis=0, concat_axis=0, tiled=True)

    change_two, mid_mom_a, mid_sq_a = slot_group(
        main_scales, last_owned, basis_la, basis_ra, mom_a, sq_a, groups[1],
        (mid_mom_a, mid_sq_a),
    )
    leaving_two, back_one = tie(change_two, back_one)
    back_two = lax.all_to_all(leaving_two, "wide", split_axis=0, concat_axis=0, tiled=True)
    block_latent, block_heads, change_two = tie(block_latent, block_heads, change_two)
    block_qb = block_heads[: w_qb.shape[0]].reshape(w_qb.shape[0], heads_here, 128)
    block_qb = block_qb[:, :, : NOPE + ROPE].reshape(w_qb.shape)
    block_kvb = block_heads[w_qb.shape[0] :]
    block_qa = block_latent[:, :q_width]
    block_kv = block_latent[:, q_width : q_width + kv_width]
    block_kr = block_latent[:, q_width + kv_width :]
    late_blocks = [block_qa, block_kv]
    late_capacity = min(late_units, capacity_a)
    late_send, late_back = routes(late_owners, capacity_a, late_capacity, wide_count)
    late_slots, late_scales = late_places(
        late_owners, late_rates, capacity_a, late_capacity, wide_index, tcount
    )
    owners_b, owners_c = owner_b[0], owner_c[0]
    capacity_b, capacity_c = mom_b.shape[0], mom_c.shape[0]
    b_send, b_back = routes(owners_b, capacity_b, capacity_b, wide_count)
    c_send, c_back = routes(owners_c, capacity_c, capacity_c, wide_count)
    sent_parts = [
        jnp.take(unit_rows(blocks), send, axis=0, mode="clip")
        for blocks, send in (
            (late_blocks, late_send),
            ([block_qb], b_send),
            ([block_kvb], c_send),
        )
    ]
    sent_parts, back_two = tie(sent_parts, back_two)
    late_owned, owned_b, owned_c = trade_joined(sent_parts, wide_count)

    placed = jnp.take(returned_rows[:, : 2 * piece_rows], deal_row, axis=0, mode="clip")
    final_out = placed[:, :piece_rows].astype(f32).reshape(row_count, local_width)
    final_grad = placed[:, piece_rows:].astype(f32).reshape(row_count, local_width)
    gain_rows = returned_rows[:, 2 * piece_rows :].reshape(wide_count, -1)
    gain_size = gain_part.shape[0]
    gain_grads = jnp.sum(gain_rows[:, :gain_size].astype(f32), axis=0) + jnp.sum(
        gain_rows[:, gain_size : 2 * gain_size].astype(f32), axis=0
    )
    gains_total = gain_grads[: 2 * local_width].reshape(2, local_width)
    qgain_total = gain_grads[2 * local_width : 2 * local_width + q_width]
    kvgain_total = gain_grads[2 * local_width + q_width :]
    late_change, new_mom_a, new_sq_a = late_steps(
        late_slots, late_scales, late_owned, basis_la, basis_ra, mid_mom_a, mid_sq_a
    )
    change_b, new_mom_b, new_sq_b = all_slots(
        slot_scales(owners_b, unit_rates([block_qb.shape[1]], [QR ** (-0.5)]), capacity_b,
                    wide_index, tcount),
        owned_b, basis_lb, basis_rb, mom_b, sq_b,
    )
    change_c, new_mom_c, new_sq_c = all_slots(
        slot_scales(owners_c, unit_rates([block_kvb.shape[1]], [KVR ** (-0.5)]), capacity_c,
                    wide_index, tcount),
        owned_c, basis_lc, basis_rc, mom_c, sq_c,
    )
    late_change, back_two = tie(late_change, back_two)
    returned = trade_joined(
        [change.reshape((-1,) + change.shape[2:]) for change in (late_change, change_b, change_c)],
        wide_count,
    )
    late_result, result_b, result_c = [
        jnp.take(part.reshape((-1,) + part.shape[2:]), back, axis=0, mode="clip")
        for part, back in zip(returned, (late_back, b_back, c_back))
    ]
    new_o, new_gate, new_up, new_down = unpack_units(
        main_back, back_one, back_two, [w_o, w_gate, w_up, w_down]
    )
    update_qa, update_kv = unit_columns(late_result, late_blocks)
    update_qb = unit_columns(result_b, [block_qb])[0]
    update_kvb = unit_columns(result_c, [block_kvb])[0]
    block_kr = block_kr.astype(f32)
    update_kr, new_kr_mom, new_kr_sq = plain_adam(block_kr, kr_mom, kr_sq, wide_rate, tcount)
    update_gains, new_gain_mom, new_gain_sq = plain_adam(
        gains_total, gain_mom, gain_sq, gain_rate, tcount
    )
    update_qgain, new_qgain_mom, new_qgain_sq = plain_adam(
        qgain_total, qgain_mom, qgain_sq, gain_rate, tcount
    )
    update_kvgain, new_kvgain_mom, new_kvgain_sq = plain_adam(
        kvgain_total, kvgain_mom, kvgain_sq, gain_rate, tcount
    )
    return (
        final_out,
        final_grad,
        block_qa.astype(f32),
        block_kv.astype(f32),
        block_qb.astype(f32),
        block_kvb.astype(f32),
        block_o.astype(f32),
        block_gate,
        block_up,
        block_down,
        w_qa.astype(f32) + update_qa,
        w_kv.astype(f32) + update_kv,
        w_qb.astype(f32) + update_qb,
        w_kvb.astype(f32) + update_kvb,
        new_o,
        new_gate,
        new_up,
        new_down,
        block_kr,
        w_kr.astype(f32) + update_kr,
        new_kr_mom,
        new_kr_sq,
        gains_total,
        norm_gains + update_gains,
        new_gain_mom,
        new_gain_sq,
        qgain_total,
        q_gain + update_qgain,
        new_qgain_mom,
        new_qgain_sq,
        kvgain_total,
        kv_gain + update_kvgain,
        new_kvgain_mom,
        new_kvgain_sq,
        new_mom_a,
        new_sq_a,
        new_mom_b,
        new_sq_b,
        new_mom_c,
        new_sq_c,
    )


def solution(mesh):
    return jax.shard_map(
        body,
        mesh=mesh,
        in_specs=(
            P("wide", "narrow"),
            P("wide", "narrow"),
            P("wide", "narrow"),
            P("wide", "narrow"),
            P("wide", None),
            P("wide", "narrow"),
            P("wide", "narrow"),
            P("wide", "narrow"),
            P("wide", "narrow"),
            P("wide", "narrow"),
            P("wide", "narrow"),
            P(None, "narrow"),
            P("narrow"),
            P("narrow"),
            P(),
            P("wide", None),
            P(),
            P("narrow", None),
            P("narrow", None),
            P("narrow", None),
            P("wide", None, "narrow"),
            P("wide", None, "narrow"),
            P("wide", None, "narrow"),
            P("wide", None, "narrow"),
            P("wide", None, "narrow"),
            P("wide", None, "narrow"),
            P("wide", None, "narrow"),
            P("wide", None, "narrow"),
            P("wide", None, "narrow"),
            P("wide", None, "narrow"),
            P("wide", None, "narrow"),
            P("wide", None, "narrow"),
            P("wide", None),
            P("wide", None),
            P(None, "narrow"),
            P(None, "narrow"),
            P("narrow"),
            P("narrow"),
            P("narrow"),
            P("narrow"),
        ),
        out_specs=(
            P("wide", "narrow"),
            P("wide", "narrow"),
            P("wide", "narrow"),
            P("wide", "narrow"),
            P("wide", "narrow"),
            P("wide", "narrow"),
            P("wide", "narrow"),
            P("wide", "narrow"),
            P("wide", "narrow"),
            P("wide", "narrow"),
            P("wide", "narrow"),
            P("wide", "narrow"),
            P("wide", "narrow"),
            P("wide", "narrow"),
            P("wide", "narrow"),
            P("wide", "narrow"),
            P("wide", "narrow"),
            P("wide", "narrow"),
            P("wide", None),
            P("wide", None),
            P("wide", None),
            P("wide", None),
            P(None, "narrow"),
            P(None, "narrow"),
            P(None, "narrow"),
            P(None, "narrow"),
            P("narrow"),
            P("narrow"),
            P("narrow"),
            P("narrow"),
            P("narrow"),
            P("narrow"),
            P("narrow"),
            P("narrow"),
            P("wide", None, "narrow"),
            P("wide", None, "narrow"),
            P("wide", None, "narrow"),
            P("wide", None, "narrow"),
            P("wide", None, "narrow"),
            P("wide", None, "narrow"),
        ),
        check_vma=False,
    )
```
